256 devices in a mesh: sub: 128 (over y, z, x), mode: 2 (over core).
Axes of the slice: x: 4, y: 4, z: 8, core: 2. Of those that a mesh axis runs over, the one named last changes fastest.
Arguments:
- coupling: bfloat16 [8192, 64, 128], P('sub'), may hold values from -0.5 to 0.5
- coupling_pairs: int32 [8192, 2], P('sub'), may hold values from 0 to 3, as said below
- modes: bfloat16 [8192, 256, 256], P('sub', None, 'mode'), may hold values from -6 to 6
- mode_weights: bfloat16 [8192, 256], P('sub', 'mode'), may hold values from 0 to 1, as said below
- parent_of: int32 [8192, 1], P('sub'), may hold values from 0 to 127; in each aligned block of 64 rows (0 to 63, 64 to 127, ...) at most 2 rows name the same one
- row_block: int32 [8192], P('sub'), may hold values from 0 to 7
- parent_modes: bfloat16 [128, 512, 256], P('sub'), may hold values from -1 to 1
- parent_eigs: float32 [128, 256], P('sub'), may hold values from 0.02 to 0.5
Outputs:
- strengths: float32 [8192, 256], P('sub', 'mode')
The draws below stay inside these ranges and needn't reach their ends.
Inputs may be any that keep to these rules, and one draw needn't show every extreme that they name: `coupling_pairs`: within each child the 2 block indices are distinct. `parent_of`: the 64 children of one index of sub name any one parent at most 2 times; some parent is named exactly 2 times by some index's children. `mode_weights`: Positive.
All inputs are finite; a program needn't handle non-finite values.
Results may differ from the reference program's by a relative error of at most 0.0015.
Values may be sent and summed in bfloat16 or wider, within the bound.
No kernel may reach another device: no remote copies, remote signals or barrier semaphores. Data moves between devices by JAX's collectives and lax.ppermute only.
A program may use at most 128 MiB of HBM per device.

```python
import math
import jax
import jax.numpy as jnp
import numpy as np
from jax import lax

M = 256
MP = 256
BLK = 64
NBC = 4
KB = 2
SB = 8
CH_DEV = 64
CHILDREN = 8192
PARENTS = 128
CAPD = 2
N_SUB = 128


def draw_coupling_pairs(key, part):
    scores = jax.random.randint(jax.random.fold_in(key, 11), (CHILDREN, NBC), 0, 1 << 20)
    scores = scores * NBC + jnp.arange(NBC, dtype=jnp.int32)[None, :]
    order = jnp.argsort(scores, axis=1, stable=True)
    return order[:, :KB].astype(jnp.int32)


def draw_mode_weights(key, part):
    level = jax.random.uniform(jax.random.fold_in(key, 23), (CHILDREN, M), jnp.float32, math.log(0.5), 0.0)
    falloff = jnp.arange(M, dtype=jnp.float32) / (M - 1)
    values = jnp.exp(level) * jnp.exp(-math.log(3.0) * falloff)[None, :]
    return values.astype(jnp.bfloat16)


def draw_parent_modes(key, part):
    base = jax.random.normal(jax.random.fold_in(key, 31), (PARENTS, SB * BLK, MP), jnp.float32)
    left = jax.random.normal(jax.random.fold_in(key, 37), (PARENTS, SB * BLK, 1), jnp.float32)
    right = jax.random.normal(jax.random.fold_in(key, 41), (PARENTS, 1, MP), jnp.float32)
    base = jnp.clip(base, -4.0, 4.0)
    left = jnp.clip(left, -3.0, 3.0)
    right = jnp.clip(right, -3.0, 3.0)
    return ((base + 0.6 * left * right) / 10.0).astype(jnp.bfloat16)


def place_ends(result, own_key, least, largest):
    spot = [jax.random.randint(jax.random.fold_in(own_key, axis), (), 0, length) for axis, length in enumerate(result.shape)]
    widest = result.shape.index(max(result.shape))
    beside = spot[:widest] + [(spot[widest] + 1) % result.shape[widest]] + spot[widest + 1:]
    return result.at[tuple(spot)].set(least).at[tuple(beside)].set(largest)


def block_levels(rng, extent, shards, least, top_value):
    factor_of = 1.0
    for dim, shards_of in shards:
        draws = jax.random.uniform(jax.random.fold_in(jax.random.fold_in(rng, 6), dim), (shards_of,), jnp.float32, least / len(shards), top_value / len(shards))
        factor_of = factor_of * jnp.repeat(jnp.exp(draws), extent[dim] // shards_of).reshape((-1,) + (1,) * (len(extent) - 1 - dim))
    return factor_of


def deal_out(rng, own, number, rows, count, top, bound, skew):
    order = jax.random.permutation(rng, count)
    heavy_load, ordinary = portions_of(count, rows * top, bound, skew, True), portions_of(count, rows * top, bound, skew, False)
    places = jnp.arange(count)

    def named(lengths, rotation):
        used = int((lengths > 0).sum())
        fixed = max(1, used // 4)
        passed = fixed + (places - fixed + rotation * (used - fixed)) % max(1, count - fixed)
        return jnp.zeros((count,), jnp.int32).at[order[jnp.where(places < fixed, places, passed)]].set(jnp.asarray(lengths, jnp.int32))

    lengths = jnp.where(number % 4 == 0, named(heavy_load, number // 4), named(ordinary, number - number // 4 - 1))
    mixed = jax.random.permutation(jax.random.fold_in(own, 3), count)
    donor, taker = mixed[0:count // 2 * 2:2], mixed[1:count // 2 * 2:2]
    margin = jnp.minimum(lengths[donor] - 1, bound - lengths[taker]) // 2
    margin = jnp.where((donor == order[0]) | (taker == order[0]) | (lengths[taker] == 0), 0, jnp.maximum(margin, 0))
    passed = jax.random.randint(jax.random.fold_in(own, 4), (count // 2,), 0, 1 << 20) % (margin + 1)
    lengths = lengths.at[donor].add(-passed).at[taker].add(passed)
    members = jnp.searchsorted(jnp.cumsum(lengths), jnp.arange(rows * top), side="right").astype(jnp.int32)
    listing = members.reshape(top, rows).T
    listing = listing[jax.random.permutation(jax.random.fold_in(own, 1), rows)]
    rotation = jax.random.randint(jax.random.fold_in(own, 2), (rows, 1), 0, top)
    return jnp.take_along_axis(listing, (jnp.arange(top)[None, :] + rotation) % top, axis=1)


def portions_of(amount, total, reach, skew, full):
    portions = [(1 << 20) // math.isqrt(rank ** skew) + 1 for rank in range(1, amount + 1)]
    largest = reach if full else min(reach, max(-(-total // amount), total * portions[0] // sum(portions)))
    least = 1 if total - largest >= amount - 1 else 0
    holding, spare = [largest] + [least] * (amount - 1), total - largest - least * (amount - 1)
    while spare > 0:
        movable = [i for i in range(1, amount) if holding[i] < largest] or [i for i in range(1, amount) if holding[i] < reach]
        pool, remaining = sum([portions[i] for i in movable]), spare
        for i in movable:
            more = min(reach - holding[i], max(1, remaining * portions[i] // pool), spare)
            holding[i] = holding[i] + more
            spare = spare - more
    return np.array(holding)


def normal_values(own_key, extent, scale, most, shards=(), kind=jnp.bfloat16):
    result = scale * jax.random.normal(own_key, extent, jnp.float32)
    if shards:
        result = result * block_levels(own_key, extent, shards, -0.22, 0.18)
    return jnp.clip(result, -most, most).astype(kind)


def setup_inputs(seed: int = 0) -> dict:
    keys = jax.random.split(jax.random.key(seed), 9)
    coupling = normal_values(keys[0], (CHILDREN, BLK, KB * BLK), (KB * BLK) ** -0.5, 0.5, ((0, 128),))
    coupling_pairs = draw_coupling_pairs(jax.random.fold_in(keys[8], 71), 0)
    modes = normal_values(keys[2], (CHILDREN, NBC * BLK, M), 1.0, 6.0, ((0, 128), (2, 2)))
    mode_weights = draw_mode_weights(jax.random.fold_in(keys[8], 71), 0)
    parent_of_keys = jax.random.split(jax.random.fold_in(keys[4], 1), CHILDREN // CH_DEV)
    parent_of_turns = jax.random.permutation(jax.random.fold_in(keys[4], 3), CHILDREN // CH_DEV)
    parent_of = jax.vmap(lambda own, number: deal_out(jax.random.fold_in(keys[4], 2), own, number, CH_DEV, N_SUB, 1, CAPD, 2))(parent_of_keys, parent_of_turns).reshape((CHILDREN, 1))
    row_block = place_ends(jax.random.randint(keys[5], (CHILDREN,), 0, SB), jax.random.fold_in(keys[5], 1), 0, SB - 1).astype(jnp.int32)
    parent_modes = draw_parent_modes(jax.random.fold_in(keys[8], 71), 0)
    parent_eigs = jnp.clip(jnp.exp(math.log(0.5) - 3.218876 * jax.random.uniform(keys[7], (PARENTS, MP), jnp.float32) ** block_levels(keys[7], (PARENTS, MP), ((0, 128),), -0.2, 0.2)), 0.02, 0.5)
    return {"coupling": coupling, "coupling_pairs": coupling_pairs, "modes": modes, "mode_weights": mode_weights, "parent_of": parent_of, "row_block": row_block, "parent_modes": parent_modes, "parent_eigs": parent_eigs}


def reference(coupling, coupling_pairs, modes, mode_weights, parent_of, row_block, parent_modes, parent_eigs):
    parent_blocks = parent_modes.reshape(PARENTS, SB, BLK, MP)

    def projected_of(child):
        picked = modes[child].reshape(NBC, BLK, M)[coupling_pairs[child]].reshape(KB * BLK, M)
        record = jnp.dot(coupling[child].astype(jnp.float32), picked.astype(jnp.float32), preferred_element_type=jnp.float32)
        record = (record * mode_weights[child][None, :].astype(jnp.float32)).astype(jnp.bfloat16)
        parent_rows = parent_blocks[parent_of[child, 0], row_block[child]]
        return jnp.dot(parent_rows.T.astype(jnp.float32), record.astype(jnp.float32), preferred_element_type=jnp.float32).astype(jnp.bfloat16)

    def accumulate(gram_sum, child):
        projected = projected_of(child)
        term = jnp.dot(projected.astype(jnp.float32), projected.T.astype(jnp.float32), preferred_element_type=jnp.float32)
        return (gram_sum.at[parent_of[child, 0]].add(term), None)
    children = jnp.arange(CHILDREN).astype(jnp.int32)
    gram_sum, _ = lax.scan(accumulate, jnp.zeros((PARENTS, MP, MP), jnp.float32), children)
    pencil = gram_sum / (CH_DEV * M) + jax.vmap(jnp.diag)(parent_eigs)
    factor = jnp.linalg.cholesky(pencil)
    identity = jnp.eye(MP, dtype=pencil.dtype)
    inverse = jax.vmap(lambda lower: lax.linalg.triangular_solve(lower, identity, left_side=True, lower=True))(factor).astype(jnp.bfloat16)

    def strength(child):
        projected = projected_of(child)
        rotated = jnp.dot(inverse[parent_of[child, 0]].astype(jnp.float32), projected.astype(jnp.float32), preferred_element_type=jnp.float32)
        return jnp.sum(rotated * rotated, axis=0) / MP
    return lax.map(strength, children)
```

```python
import jax
import jax.numpy as jnp
from jax import lax
from jax.experimental import pallas as pl
from jax.experimental.pallas import tpu as pltpu
from jax.sharding import Mesh, PartitionSpec as P

MP = 256
BLK = 64
HALF = 32
SB = 8
CHILDREN_DEV = 64
CB = 16
STEPS = CHILDREN_DEV // CB
NY, NZ, NX = 4, 8, 4
NG = NY * NX
SLOTS = 2 * NZ
ROWS = 9 * SLOTS
ZROWS = 80
PB = 32
BF = jnp.bfloat16
F32 = jnp.float32
VMEM = pl.BlockSpec(memory_space=pltpu.VMEM)
SMEM = pl.BlockSpec(memory_space=pltpu.SMEM)


def params(mib, **more):
    return pltpu.CompilerParams(vmem_limit_bytes=mib * 1024 * 1024, **more)


def dot(a, b):
    return jnp.dot(a, b, preferred_element_type=F32)


def dot_nt(a, b):
    return lax.dot_general(a, b, (((1,), (1,)), ((), ())), preferred_element_type=F32)


def dot_tn(a, b):
    return lax.dot_general(a, b, (((0,), (0,)), ((), ())), preferred_element_type=F32)


def four(x):
    return jnp.concatenate([x, x, x, x], axis=0)


def tile_index():
    row = lax.broadcasted_iota(jnp.int32, (HALF, 128), 0)
    lane = lax.broadcasted_iota(jnp.int32, (HALF, 128), 1)
    return row, lane % HALF, (lane // HALF) == (row // 8)


def pack(x):
    lane = lax.broadcasted_iota(jnp.int32, (8, 128), 1)
    low = jnp.where(lane < 32, x[0:8], x[8:16])
    high = jnp.where(lane < 96, x[16:24], x[24:32])
    return jnp.where(lane < 64, low, high)


def moments_kernel(core_ref, pairs_ref, coupling_ref, modes_ref, weights_ref, record_ref, own_ref, other_ref):
    step = pl.program_id(0)
    row, col, _ = tile_index()
    lower = row >= col
    diagonal = row == col
    first = core_ref[0] == 0
    for j in range(CB):
        c = step * CB + j
        top = modes_ref[j, pl.ds(pl.multiple_of(pairs_ref[c, 0] * BLK, BLK), BLK), :]
        bottom = modes_ref[j, pl.ds(pl.multiple_of(pairs_ref[c, 1] * BLK, BLK), BLK), :]
        picked = jnp.concatenate([top, bottom], axis=0)
        record = dot(coupling_ref[j], picked)
        record = (record * weights_ref[j : j + 1, :].astype(F32)).astype(BF)
        record_ref[j] = record
        u = dot_nt(record, four(record[:HALF]))
        v = dot_nt(record[HALF:], four(record[HALF:]))
        cross = pack(u[HALF:])
        triangle = pack(jnp.where(lower, u[:HALF], v))
        diag = jnp.sum(jnp.where(diagonal, v, 0.0), axis=0, keepdims=True)
        own_ref[0, j * 8 : j * 8 + 8, :] = jnp.where(first, cross, triangle)
        other_ref[0, j * 8 : j * 8 + 8, :] = jnp.where(first, triangle, cross)
        own_ref[0, CB * 8 + j : CB * 8 + j + 1, :] = diag
        other_ref[0, CB * 8 + j : CB * 8 + j + 1, :] = diag


def moments(core, pairs, coupling, modes, weights):
    block = CB * 8 + CB
    return pl.pallas_call(
        moments_kernel,
        grid=(STEPS,),
        in_specs=[
            SMEM,
            SMEM,
            pl.BlockSpec((CB, BLK, 128), lambda i: (i, 0, 0)),
            pl.BlockSpec((CB, 256, 128), lambda i: (i, 0, 0)),
            pl.BlockSpec((CB, 128), lambda i: (i, 0)),
        ],
        out_specs=[
            pl.BlockSpec((CB, BLK, 128), lambda i: (i, 0, 0)),
            pl.BlockSpec((1, block, 128), lambda i: (i, 0, 0)),
            pl.BlockSpec((1, block, 128), lambda i: (i, 0, 0)),
        ],
        out_shape=[
            jax.ShapeDtypeStruct((CHILDREN_DEV, BLK, 128), BF),
            jax.ShapeDtypeStruct((STEPS, block, 128), F32),
            jax.ShapeDtypeStruct((STEPS, block, 128), F32),
        ],
        compiler_params=params(32),
        name="child_moments",
    )(core, pairs, coupling, modes, weights)


def slot_of(parent_ref, count_ref, c):
    p = parent_ref[c]
    k = count_ref[p]
    count_ref[p] = k + 1
    group = (p // (NZ * NX)) * NX + p % NX
    slot = ((p // NX) % NZ) * 2 + k
    return group, slot


def clear_counts(count_ref):
    for p in range(NG * NZ):
        count_ref[p] = 0


def dispatch_kernel(parent_ref, block_ref, own_ref, recv_ref, out_ref, buf_ref, count_ref):
    clear_counts(count_ref)
    lane = lax.broadcasted_iota(jnp.int32, (1, 128), 1)
    lane16 = lax.broadcasted_iota(jnp.int32, (SLOTS, 128), 1)
    empty = jnp.where(lane16 < 64, -1000.0, 0.0)
    for g in range(NG):
        buf_ref[g, 0 : 8 * SLOTS, :] = jnp.zeros((8 * SLOTS, 128), F32)
        buf_ref[g, 8 * SLOTS : ROWS, :] = empty
    for c in range(CHILDREN_DEV):
        group, slot = slot_of(parent_ref, count_ref, c)
        s, j = c // CB, c % CB
        buf_ref[group, pl.ds(slot, 8, stride=SLOTS), :] = (
            own_ref[s, j * 8 : j * 8 + 8, :] + recv_ref[s, j * 8 : j * 8 + 8, :]
        )
        r = CB * 8 + j
        diag = own_ref[s, r : r + 1, :] + recv_ref[s, r : r + 1, :]
        block = block_ref[c].astype(F32)
        buf_ref[group, pl.ds(8 * SLOTS + slot, 1), :] = jnp.where(lane < 64, block, diag)
    for g in range(NG):
        out_ref[g] = buf_ref[g].astype(BF)


def dispatch(parent, block, own, recv):
    return pl.pallas_call(
        dispatch_kernel,
        in_specs=[SMEM, SMEM, VMEM, VMEM],
        out_specs=VMEM,
        out_shape=jax.ShapeDtypeStruct((NG, ROWS, 128), BF),
        scratch_shapes=[pltpu.VMEM((NG, ROWS, 128), F32), pltpu.SMEM((NG * NZ,), jnp.int32)],
        compiler_params=params(32),
        name="dispatch",
    )(parent, block, own, recv)


def bin_kernel(recv_ref, out_ref, onehot_ref):
    count = NG * SLOTS
    meta = recv_ref[:, 8 * SLOTS : ROWS, :].astype(F32).reshape(count, 128)
    slot = lax.broadcasted_iota(jnp.int32, (count, 128), 0) % SLOTS
    lane = lax.broadcasted_iota(jnp.int32, (count, 128), 1)
    target = meta + (SB * (slot // 2)).astype(F32)
    onehot = jnp.where((lane < 64) & (target == lane.astype(F32)), 1.0, 0.0).astype(BF)
    onehot_ref[...] = onehot
    values = jnp.concatenate(
        [recv_ref[:, i * SLOTS : (i + 1) * SLOTS, :].reshape(count, 128) for i in range(9)], axis=1
    )
    bins = dot_tn(onehot, values)
    zero = jnp.zeros((8, 128), F32)
    for z in range(NZ):
        rows = [bins[8 * z : 8 * z + 8, 128 * i : 128 * (i + 1)] for i in range(9)] + [zero]
        out_ref[z] = jnp.concatenate(rows, axis=0).astype(BF)


def bin_slots(recv):
    return pl.pallas_call(
        bin_kernel,
        in_specs=[VMEM],
        out_specs=[VMEM, VMEM],
        out_shape=[
            jax.ShapeDtypeStruct((NZ, ZROWS, 128), BF),
            jax.ShapeDtypeStruct((NG * SLOTS, 128), BF),
        ],
        compiler_params=params(32),
        name="bin_slots",
    )(recv)


def sum_kernel(recv_ref, out_ref):
    total = recv_ref[0].astype(F32)
    for z in range(1, NZ):
        total = total + recv_ref[z].astype(F32)
    out_ref[...] = total


def sum_bins(recv):
    return pl.pallas_call(
        sum_kernel,
        in_specs=[VMEM],
        out_specs=VMEM,
        out_shape=jax.ShapeDtypeStruct((ZROWS, 128), F32),
        name="sum_bins",
    )(recv)


def invert(a_ref):
    lane = lax.broadcasted_iota(jnp.int32, (PB, MP), 1)
    row = lax.broadcasted_iota(jnp.int32, (PB, MP), 0)
    lane_all = lax.broadcasted_iota(jnp.int32, (MP, MP), 1)
    for b in range(MP // PB):
        r = b * PB
        panel = a_ref[r : r + PB, :]
        for j in range(PB):
            k = r + j
            col = panel[:, k : k + 1]
            inv = 1.0 / panel[j : j + 1, k : k + 1]
            pivot = jnp.where(lane[:1] == k, 1.0, panel[j : j + 1, :])
            scaled = pivot * inv
            panel = jnp.where(row == j, scaled, jnp.where(lane == k, 0.0, panel) - col * scaled)
        cols = a_ref[:, r : r + PB]
        update = jnp.dot(cols, panel, preferred_element_type=F32, precision=lax.Precision.HIGHEST)
        a_ref[...] = jnp.where((lane_all // PB) == b, 0.0, a_ref[...]) - update
        a_ref[r : r + PB, :] = panel


def split(x):
    high = x.astype(BF)
    return high, (x - high.astype(F32)).astype(BF)


def pencil_kernel(core_ref, own_ref, other_ref, q_ref, eigs_ref, out_ref, a_ref, y_ref, pack_ref):
    row, col, same = tile_index()
    first = core_ref[0] == 0
    lane8 = lax.broadcasted_iota(jnp.int32, (8, 128), 1)
    diags = jnp.where(first, other_ref[64:72, :], own_ref[64:72, :])
    diags = jnp.where(lane8 < 64, pltpu.roll(diags, 64, 1), diags)
    zero = jnp.zeros((HALF, 128), F32)
    for b in range(SB):
        own = own_ref[pl.ds(b, 8, stride=8), :]
        other = other_ref[pl.ds(b, 8, stride=8), :]
        cross = jnp.where(same, four(jnp.where(first, own, other)), 0.0)
        triangle = jnp.where(same, four(jnp.where(first, other, own)), 0.0)
        n11 = jnp.where(row > col, triangle, jnp.where(row == col, 0.5 * triangle, 0.0))
        half = jnp.where(same & (row == col), 0.5 * diags[b : b + 1, :], 0.0)
        n22 = jnp.where(row < col, triangle, half)
        lhs = jnp.concatenate(
            [jnp.concatenate([n11, zero], axis=1), jnp.concatenate([cross, n22], axis=1)], axis=0
        ).astype(BF)
        q1 = q_ref[b * BLK : b * BLK + HALF, :]
        q2 = q_ref[b * BLK + HALF : (b + 1) * BLK, :]
        y_ref[b * BLK : (b + 1) * BLK, :] = dot(lhs, jnp.concatenate([four(q1), four(q2)], axis=0)).astype(BF)
    x = dot_tn(q_ref[...], y_ref[...])
    r = lax.broadcasted_iota(jnp.int32, (MP, MP), 0)
    c = lax.broadcasted_iota(jnp.int32, (MP, MP), 1)
    a_ref[...] = (x + x.T) * (1.0 / 16384.0) + jnp.where(r == c, eigs_ref[...], 0.0)
    invert(a_ref)
    high, low = split(a_ref[...] * (1.0 / MP))
    q = q_ref[...]
    y_high, y_low = split(dot(q, high) + dot(q, low))
    for b in range(SB):
        s = b * BLK
        qb = q_ref[s : s + BLK, :]
        u = dot_nt(qb, four(y_high[s : s + HALF])) + dot_nt(qb, four(y_low[s : s + HALF]))
        v = dot_nt(qb[HALF:], four(y_high[s + HALF : s + BLK])) + dot_nt(
            qb[HALF:], four(y_low[s + HALF : s + BLK])
        )
        cross = pack(2.0 * u[HALF:])
        triangle = pack(
            jnp.where(row > col, 2.0 * u[:HALF], jnp.where(row == col, u[:HALF], 2.0 * v))
        )
        pack_ref[pl.ds(b, 8, stride=8), :] = jnp.where(first, cross, triangle)
        pack_ref[64 + b : 65 + b, :] = jnp.sum(jnp.where(row == col, v, 0.0), axis=0, keepdims=True)
    pack_ref[72:80, :] = jnp.zeros((8, 128), F32)
    result = pack_ref[...].astype(BF)
    for z in range(NZ):
        out_ref[z] = result


def pencil_blocks(core, own, other, q, eigs):
    return pl.pallas_call(
        pencil_kernel,
        in_specs=[SMEM, VMEM, VMEM, VMEM, VMEM],
        out_specs=VMEM,
        out_shape=jax.ShapeDtypeStruct((NZ, ZROWS, 128), BF),
        scratch_shapes=[
            pltpu.VMEM((MP, MP), F32),
            pltpu.VMEM((SB * BLK, MP), BF),
            pltpu.VMEM((ZROWS, 128), F32),
        ],
        compiler_params=params(32),
        name="pencil_blocks",
    )(core, own, other, q, eigs)


def select_kernel(bins_ref, onehot_ref, out_ref):
    onehot = onehot_ref[:, 0:64]
    bins = [bins_ref[z].astype(F32) for z in range(NZ)]
    for i in range(9):
        values = jnp.concatenate([x[8 * i : 8 * i + 8] for x in bins], axis=0).astype(BF)
        picked = dot(onehot, values).astype(BF)
        out_ref[:, i * SLOTS : (i + 1) * SLOTS, :] = picked.reshape(NG, SLOTS, 128)


def select_bins(bins, onehot):
    return pl.pallas_call(
        select_kernel,
        in_specs=[VMEM, VMEM],
        out_specs=VMEM,
        out_shape=jax.ShapeDtypeStruct((NG, ROWS, 128), BF),
        compiler_params=params(32),
        name="select_bins",
    )(bins, onehot)


def collect_kernel(parent_ref, recv_ref, out_ref, buf_ref, count_ref):
    clear_counts(count_ref)
    for g in range(NG):
        buf_ref[g] = recv_ref[g].astype(F32)
    for c in range(CHILDREN_DEV):
        group, slot = slot_of(parent_ref, count_ref, c)
        s, j = c // CB, c % CB
        out_ref[s, j * 8 : j * 8 + 8, :] = buf_ref[group, pl.ds(slot, 8, stride=SLOTS), :]
        r = CB * 8 + j
        out_ref[s, r : r + 1, :] = buf_ref[group, pl.ds(8 * SLOTS + slot, 1), :]


def collect(parent, recv):
    return pl.pallas_call(
        collect_kernel,
        in_specs=[SMEM, VMEM],
        out_specs=VMEM,
        out_shape=jax.ShapeDtypeStruct((STEPS, CB * 9, 128), F32),
        scratch_shapes=[pltpu.VMEM((NG, ROWS, 128), F32), pltpu.SMEM((NG * NZ,), jnp.int32)],
        compiler_params=params(32),
        name="collect",
    )(parent, recv)


def strength_kernel(core_ref, own_ref, other_ref, record_ref, out_ref):
    row, col, same = tile_index()
    first = core_ref[0] == 0
    lower = same & (row >= col)
    upper = same & (row < col)
    diagonal = same & (row == col)
    zero = jnp.zeros((HALF, 128), F32)
    for j in range(CB):
        own = own_ref[0, j * 8 : j * 8 + 8, :]
        other = other_ref[0, j * 8 : j * 8 + 8, :]
        r = CB * 8 + j
        diag = jnp.where(first, other_ref[0, r : r + 1, :], own_ref[0, r : r + 1, :])
        cross = jnp.where(same, four(jnp.where(first, own, other)), 0.0)
        triangle = four(jnp.where(first, other, own))
        m11 = jnp.where(lower, triangle, 0.0)
        m22 = jnp.where(upper, triangle, jnp.where(diagonal, diag, 0.0))
        lhs = jnp.concatenate(
            [jnp.concatenate([m11, zero], axis=1), jnp.concatenate([cross, m22], axis=1)], axis=0
        ).astype(BF)
        record = record_ref[j]
        rhs = jnp.concatenate([four(record[:HALF]), four(record[HALF:])], axis=0)
        rotated = dot(lhs, rhs)
        out_ref[j : j + 1, :] = jnp.sum(rotated * record.astype(F32), axis=0, keepdims=True)


def strengths(core, own, other, record):
    block = CB * 9
    return pl.pallas_call(
        strength_kernel,
        grid=(STEPS,),
        in_specs=[
            SMEM,
            pl.BlockSpec((1, block, 128), lambda i: (i, 0, 0)),
            pl.BlockSpec((1, block, 128), lambda i: (i, 0, 0)),
            pl.BlockSpec((CB, BLK, 128), lambda i: (i, 0, 0)),
        ],
        out_specs=pl.BlockSpec((CB, 128), lambda i: (i, 0)),
        out_shape=jax.ShapeDtypeStruct((CHILDREN_DEV, 128), F32),
        compiler_params=params(32),
        name="strengths",
    )(core, own, other, record)


def swap(x):
    return lax.ppermute(x, "mode", [(0, 1), (1, 0)])


def exchange(x, axes):
    return lax.all_to_all(x, axes, split_axis=0, concat_axis=0, tiled=True)


def per_device(coupling, pairs, modes, weights, parent_of, row_block, parent_modes, parent_eigs):
    core = lax.axis_index("mode").astype(jnp.int32).reshape(1)
    parent = parent_of.reshape(CHILDREN_DEV)
    record, own, other = moments(core, pairs, coupling, modes, weights)
    sent = dispatch(parent, row_block, own, swap(other))
    binned, onehot = bin_slots(exchange(sent, ("y", "x")))
    total = sum_bins(exchange(binned, "z"))
    blocks = pencil_blocks(core, total, swap(total), parent_modes[0], parent_eigs)
    picked = select_bins(exchange(blocks, "z"), onehot)
    mine = collect(parent, exchange(picked, ("y", "x")))
    return strengths(core, mine, swap(mine), record)


def solution(mesh):
    grid = Mesh(mesh.devices.reshape(NY, NZ, NX, 2), ("y", "z", "x", "mode"))
    sub = ("y", "z", "x")
    in_specs = (
        P(sub, None, None),
        P(sub, None),
        P(sub, None, "mode"),
        P(sub, "mode"),
        P(sub, None),
        P(sub),
        P(sub, None, None),
        P(sub, None),
    )
    return jax.shard_map(
        per_device, mesh=grid, in_specs=in_specs, out_specs=P(sub, "mode"), check_vma=False
    )
```

```python
import jax
import jax.numpy as jnp
from jax import lax
from jax.experimental import pallas as pl
from jax.experimental.pallas import tpu as pltpu
from jax.sharding import Mesh, PartitionSpec as P

MP = 256
BLK = 64
HALF = 32
SB = 8
CHILDREN_DEV = 64
CB = 16
STEPS = CHILDREN_DEV // CB
NY, NZ, NX = 4, 8, 4
NG = NY * NX
SLOTS = 2 * NZ
ROWS = 9 * SLOTS
ZROWS = 80
PB = 32
BF = jnp.bfloat16
F32 = jnp.float32
VMEM = pl.BlockSpec(memory_space=pltpu.VMEM)
SMEM = pl.BlockSpec(memory_space=pltpu.SMEM)


def params(mib, **more):
    return pltpu.CompilerParams(vmem_limit_bytes=mib * 1024 * 1024, **more)


def dot(a, b):
    return jnp.dot(a, b, preferred_element_type=F32)


def dot_nt(a, b):
    return lax.dot_general(a, b, (((1,), (1,)), ((), ())), preferred_element_type=F32)


def dot_tn(a, b):
    return lax.dot_general(a, b, (((0,), (0,)), ((), ())), preferred_element_type=F32)


def four(x):
    return jnp.concatenate([x, x, x, x], axis=0)


def tile_index():
    row = lax.broadcasted_iota(jnp.int32, (HALF, 128), 0)
    lane = lax.broadcasted_iota(jnp.int32, (HALF, 128), 1)
    return row, lane % HALF, (lane // HALF) == (row // 8)


def pack(x):
    lane = lax.broadcasted_iota(jnp.int32, (8, 128), 1)
    low = jnp.where(lane < 32, x[0:8], x[8:16])
    high = jnp.where(lane < 96, x[16:24], x[24:32])
    return jnp.where(lane < 64, low, high)


def side_by_side(x):
    return jnp.concatenate([x[0:8], x[8:16], x[16:24], x[24:32]], axis=1)


def moments_kernel(
    core_ref, pairs_ref, parent_ref, block_ref, coupling_ref, modes_ref, weights_ref,
    record_ref, own_ref, other_ref, onehot_ref, count_ref,
):
    step = pl.program_id(0)
    row = lax.broadcasted_iota(jnp.int32, (HALF, HALF), 0)
    col = lax.broadcasted_iota(jnp.int32, (HALF, HALF), 1)
    lower = row >= col
    diagonal = lax.broadcasted_iota(jnp.int32, (HALF, BLK), 1) == (
        lax.broadcasted_iota(jnp.int32, (HALF, BLK), 0) + HALF
    )
    slots = lax.broadcasted_iota(jnp.int32, (1, NG * SLOTS), 1)
    first = core_ref[0] == 0

    @pl.when(step == 0)
    def _():
        for p in range(NG * NZ):
            count_ref[p] = 0

    for pair in range(CB // 2):
        records = []
        for j in (2 * pair, 2 * pair + 1):
            c = step * CB + j
            top = modes_ref[j, pl.ds(pl.multiple_of(pairs_ref[0, c] * BLK, BLK), BLK), :]
            bottom = modes_ref[j, pl.ds(pl.multiple_of(pairs_ref[1, c] * BLK, BLK), BLK), :]
            record = dot(coupling_ref[j], jnp.concatenate([top, bottom], axis=0))
            record = (record * weights_ref[j : j + 1, :].astype(F32)).astype(BF)
            record_ref[j] = record
            records.append(record)
        both = jnp.concatenate(records, axis=0)
        products = dot_nt(both, both)
        for i in range(2):
            c = step * CB + 2 * pair + i
            s = products[i * BLK : (i + 1) * BLK, i * BLK : (i + 1) * BLK]
            cross = side_by_side(s[HALF:, :HALF])
            triangle = side_by_side(jnp.where(lower, s[:HALF, :HALF], s[HALF:, HALF:]))
            own_ref[pl.ds(c, 8, stride=CHILDREN_DEV), :] = jnp.where(first, cross, triangle)
            other_ref[pl.ds(c, 8, stride=CHILDREN_DEV), :] = jnp.where(first, triangle, cross)
            diag = jnp.sum(jnp.where(diagonal, s[HALF:], 0.0), axis=0, keepdims=True)
            zero = jnp.zeros((1, BLK), F32)
            named = zero + (block_ref[c] + 1).astype(F32)
            own_ref[pl.ds(8 * CHILDREN_DEV + c, 1), :] = jnp.concatenate([diag, named], axis=1)
            other_ref[pl.ds(8 * CHILDREN_DEV + c, 1), :] = jnp.concatenate([diag, zero], axis=1)
            p = parent_ref[c]
            k = count_ref[p]
            count_ref[p] = k + 1
            group = (p // (NZ * NX)) * NX + p % NX
            slot = group * SLOTS + ((p // NX) % NZ) * 2 + k
            onehot_ref[pl.ds(c, 1), :] = jnp.where(slots == slot, 1.0, 0.0)


def moments(core, pairs, parent, block, coupling, modes, weights):
    whole = (9 * CHILDREN_DEV, 128)
    onehot = (CHILDREN_DEV, NG * SLOTS)
    return pl.pallas_call(
        moments_kernel,
        grid=(STEPS,),
        in_specs=[
            SMEM,
            SMEM,
            SMEM,
            SMEM,
            pl.BlockSpec((CB, BLK, 128), lambda i: (i, 0, 0)),
            pl.BlockSpec((CB, 256, 128), lambda i: (i, 0, 0)),
            pl.BlockSpec((CB, 128), lambda i: (i, 0)),
        ],
        out_specs=[
            pl.BlockSpec((CB, BLK, 128), lambda i: (i, 0, 0)),
            pl.BlockSpec(whole, lambda i: (0, 0)),
            pl.BlockSpec(whole, lambda i: (0, 0)),
            pl.BlockSpec(onehot, lambda i: (0, 0)),
        ],
        out_shape=[
            jax.ShapeDtypeStruct((CHILDREN_DEV, BLK, 128), BF),
            jax.ShapeDtypeStruct(whole, F32),
            jax.ShapeDtypeStruct(whole, F32),
            jax.ShapeDtypeStruct(onehot, F32),
        ],
        scratch_shapes=[pltpu.SMEM((NG * NZ,), jnp.int32)],
        compiler_params=params(60),
        name="child_moments",
    )(core, pairs, parent, block, coupling, modes, weights)


def dispatch_kernel(onehot_ref, own_ref, recv_ref, out_ref):
    place = onehot_ref[...].T.astype(BF)
    for i in range(9):
        rows = slice(i * CHILDREN_DEV, (i + 1) * CHILDREN_DEV)
        values = (own_ref[rows, :] + recv_ref[rows, :]).astype(BF)
        out_ref[:, i * SLOTS : (i + 1) * SLOTS, :] = dot(place, values).astype(BF).reshape(NG, SLOTS, 128)


def dispatch(onehot, own, recv):
    return pl.pallas_call(
        dispatch_kernel,
        in_specs=[VMEM, VMEM, VMEM],
        out_specs=VMEM,
        out_shape=jax.ShapeDtypeStruct((NG, ROWS, 128), BF),
        compiler_params=params(16),
        name="dispatch",
    )(onehot, own, recv)


def bin_kernel(recv_ref, out_ref, onehot_ref):
    count = NG * SLOTS
    meta = recv_ref[:, 8 * SLOTS : ROWS, :].astype(F32).reshape(count, 128)
    slot = lax.broadcasted_iota(jnp.int32, (count, 128), 0) % SLOTS
    lane = lax.broadcasted_iota(jnp.int32, (count, 128), 1)
    meta = pltpu.roll(meta, 64, 1)
    target = meta + (SB * (slot // 2) - 1).astype(F32)
    hit = (lane < 64) & (meta > 0.5) & (target == lane.astype(F32))
    onehot = jnp.where(hit, 1.0, 0.0).astype(BF)
    onehot_ref[...] = onehot
    values = jnp.concatenate(
        [recv_ref[:, i * SLOTS : (i + 1) * SLOTS, :].reshape(count, 128) for i in range(9)], axis=1
    )
    bins = dot_tn(onehot, values)
    zero = jnp.zeros((8, 128), F32)
    for z in range(NZ):
        rows = [bins[8 * z : 8 * z + 8, 128 * i : 128 * (i + 1)] for i in range(9)] + [zero]
        out_ref[z] = jnp.concatenate(rows, axis=0).astype(BF)


def bin_slots(recv):
    return pl.pallas_call(
        bin_kernel,
        in_specs=[VMEM],
        out_specs=[VMEM, VMEM],
        out_shape=[
            jax.ShapeDtypeStruct((NZ, ZROWS, 128), BF),
            jax.ShapeDtypeStruct((NG * SLOTS, 128), BF),
        ],
        compiler_params=params(16),
        name="bin_slots",
    )(recv)


def invert(a_ref):
    lane = lax.broadcasted_iota(jnp.int32, (PB, MP), 1)
    row = lax.broadcasted_iota(jnp.int32, (PB, MP), 0)
    lane_all = lax.broadcasted_iota(jnp.int32, (MP, MP), 1)
    line = lane[:1]

    def wide(x):
        return jnp.concatenate([x, x], axis=1)

    for b in range(MP // PB):
        r = b * PB
        panel = a_ref[r : r + PB, :]
        for j in range(0, PB, 4):
            k = r + j
            inside = (line >= k) & (line < k + 4)
            c = [jnp.broadcast_to(panel[:, k + i : k + i + 1], (PB, 128)) for i in range(4)]
            p = [
                jnp.where(line == k + i, 1.0, jnp.where(inside, 0.0, panel[j + i : j + i + 1]))
                for i in range(4)
            ]
            a00, a01, a11 = c[0][j : j + 1], c[1][j : j + 1], c[1][j + 1 : j + 2]
            a02, a12, a22 = c[2][j : j + 1], c[2][j + 1 : j + 2], c[2][j + 2 : j + 3]
            a03, a13, a23 = c[3][j : j + 1], c[3][j + 1 : j + 2], c[3][j + 2 : j + 3]
            a33 = c[3][j + 3 : j + 4]
            scale = 1.0 / (a00 * a11 - a01 * a01)
            p00, p01, p11 = a11 * scale, -a01 * scale, a00 * scale
            t00, t10 = p00 * a02 + p01 * a12, p01 * a02 + p11 * a12
            t01, t11 = p00 * a03 + p01 * a13, p01 * a03 + p11 * a13
            s00 = a22 - (a02 * t00 + a12 * t10)
            s01 = a23 - (a02 * t01 + a12 * t11)
            s11 = a33 - (a03 * t01 + a13 * t11)
            scale = 1.0 / (s00 * s11 - s01 * s01)
            q00, q01, q11 = s11 * scale, -s01 * scale, s00 * scale
            t00, t10, t01, t11 = wide(t00), wide(t10), wide(t01), wide(t11)
            p00, p01, p11 = wide(p00), wide(p01), wide(p11)
            q00, q01, q11 = wide(q00), wide(q01), wide(q11)
            u2 = p[2] - (t00 * p[0] + t10 * p[1])
            u3 = p[3] - (t01 * p[0] + t11 * p[1])
            x2, x3 = q00 * u2 + q01 * u3, q01 * u2 + q11 * u3
            x0 = (p00 * p[0] + p01 * p[1]) - (t00 * x2 + t01 * x3)
            x1 = (p01 * p[0] + p11 * p[1]) - (t10 * x2 + t11 * x3)
            c = [wide(v) for v in c]
            rest = jnp.where((lane >= k) & (lane < k + 4), 0.0, panel) - (
                (c[0] * x0 + c[1] * x1) + (c[2] * x2 + c[3] * x3)
            )
            low = jnp.where(row == j, x0, jnp.where(row == j + 1, x1, rest))
            panel = jnp.where(row == j + 2, x2, jnp.where(row == j + 3, x3, low))
        ch, cm, cl = split3(a_ref[:, r : r + PB])
        ph, pm, pw = split3(panel)
        update = dot(
            jnp.concatenate([ch, ch, cm, ch, cm, cl], axis=1),
            jnp.concatenate([ph, pm, ph, pw, pm, ph], axis=0),
        )
        a_ref[...] = jnp.where((lane_all // PB) == b, 0.0, a_ref[...]) - update
        a_ref[r : r + PB, :] = panel


def split3(x):
    high = x.astype(BF)
    rest = x - high.astype(F32)
    mid = rest.astype(BF)
    return high, mid, (rest - mid.astype(F32)).astype(BF)


def split(x):
    high = x.astype(BF)
    return high, (x - high.astype(F32)).astype(BF)


def pencil_kernel(
    core_ref, mine_ref, theirs_ref, q_ref, eigs_ref, out_ref, a_ref, y_ref, pack_ref, own_ref, other_ref
):
    for source, target in ((mine_ref, own_ref), (theirs_ref, other_ref)):
        parts = [source[z].astype(F32) for z in range(NZ)]
        while len(parts) > 1:
            parts = [x + y for x, y in zip(parts[::2], parts[1::2])]
        target[...] = parts[0]
    row, col, same = tile_index()
    first = core_ref[0] == 0
    lane8 = lax.broadcasted_iota(jnp.int32, (8, 128), 1)
    diags = jnp.where(first, other_ref[64:72, :], own_ref[64:72, :])
    diags = jnp.where((lane8 >= 32) & (lane8 < 64), diags, 0.0)
    diags = diags + pltpu.roll(diags, 32, 1)
    diags = diags + pltpu.roll(diags, 64, 1)
    zero = jnp.zeros((HALF, 128), F32)
    for b in range(SB):
        own = own_ref[pl.ds(b, 8, stride=8), :]
        other = other_ref[pl.ds(b, 8, stride=8), :]
        cross = jnp.where(same, four(jnp.where(first, own, other)), 0.0)
        triangle = jnp.where(same, four(jnp.where(first, other, own)), 0.0)
        n11 = jnp.where(row > col, triangle, jnp.where(row == col, 0.5 * triangle, 0.0))
        half = jnp.where(same & (row == col), 0.5 * diags[b : b + 1, :], 0.0)
        n22 = jnp.where(row < col, triangle, half)
        lhs = jnp.concatenate(
            [jnp.concatenate([n11, zero], axis=1), jnp.concatenate([cross, n22], axis=1)], axis=0
        ).astype(BF)
        q1 = q_ref[b * BLK : b * BLK + HALF, :]
        q2 = q_ref[b * BLK + HALF : (b + 1) * BLK, :]
        y_ref[b * BLK : (b + 1) * BLK, :] = dot(lhs, jnp.concatenate([four(q1), four(q2)], axis=0)).astype(BF)
    x = dot_tn(q_ref[...], y_ref[...])
    r = lax.broadcasted_iota(jnp.int32, (MP, MP), 0)
    c = lax.broadcasted_iota(jnp.int32, (MP, MP), 1)
    a_ref[...] = (x + x.T) * (1.0 / 16384.0) + jnp.where(r == c, eigs_ref[...], 0.0)
    invert(a_ref)
    high, low = split(a_ref[...] * (1.0 / MP))
    q = q_ref[...]
    y_high, y_low = split(dot(q, high) + dot(q, low))
    for b in range(SB):
        s = b * BLK
        qb = q_ref[s : s + BLK, :]
        u = dot_nt(qb, four(y_high[s : s + HALF])) + dot_nt(qb, four(y_low[s : s + HALF]))
        v = dot_nt(qb[HALF:], four(y_high[s + HALF : s + BLK])) + dot_nt(
            qb[HALF:], four(y_low[s + HALF : s + BLK])
        )
        cross = pack(2.0 * u[HALF:])
        triangle = pack(
            jnp.where(row > col, 2.0 * u[:HALF], jnp.where(row == col, u[:HALF], 2.0 * v))
        )
        pack_ref[pl.ds(b, 8, stride=8), :] = jnp.where(first, cross, triangle)
        pack_ref[64 + b : 65 + b, :] = jnp.sum(jnp.where(row == col, v, 0.0), axis=0, keepdims=True)
    pack_ref[72:80, :] = jnp.zeros((8, 128), F32)
    result = pack_ref[...].astype(BF)
    for z in range(NZ):
        out_ref[z] = result


def pencil_blocks(core, own, other, q, eigs):
    return pl.pallas_call(
        pencil_kernel,
        in_specs=[SMEM, VMEM, VMEM, VMEM, VMEM],
        out_specs=VMEM,
        out_shape=jax.ShapeDtypeStruct((NZ, ZROWS, 128), BF),
        scratch_shapes=[
            pltpu.VMEM((MP, MP), F32),
            pltpu.VMEM((SB * BLK, MP), BF),
            pltpu.VMEM((ZROWS, 128), F32),
            pltpu.VMEM((ZROWS, 128), F32),
            pltpu.VMEM((ZROWS, 128), F32),
        ],
        compiler_params=params(16),
        name="pencil_blocks",
    )(core, own, other, q, eigs)


def select_kernel(bins_ref, onehot_ref, out_ref):
    onehot = onehot_ref[:, 0:64]
    bins = [bins_ref[z].astype(F32) for z in range(NZ)]
    for i in range(9):
        values = jnp.concatenate([x[8 * i : 8 * i + 8] for x in bins], axis=0).astype(BF)
        picked = dot(onehot, values).astype(BF)
        out_ref[:, i * SLOTS : (i + 1) * SLOTS, :] = picked.reshape(NG, SLOTS, 128)


def select_bins(bins, onehot):
    return pl.pallas_call(
        select_kernel,
        in_specs=[VMEM, VMEM],
        out_specs=VMEM,
        out_shape=jax.ShapeDtypeStruct((NG, ROWS, 128), BF),
        compiler_params=params(16),
        name="select_bins",
    )(bins, onehot)


def collect_kernel(onehot_ref, recv_ref, out_ref):
    onehot = onehot_ref[...].astype(BF)
    for i in range(9):
        values = recv_ref[:, i * SLOTS : (i + 1) * SLOTS, :].reshape(NG * SLOTS, 128)
        out_ref[i * CHILDREN_DEV : (i + 1) * CHILDREN_DEV, :] = dot(onehot, values).astype(BF)


def collect(onehot, recv):
    return pl.pallas_call(
        collect_kernel,
        in_specs=[VMEM, VMEM],
        out_specs=VMEM,
        out_shape=jax.ShapeDtypeStruct((9 * CHILDREN_DEV, 128), BF),
        compiler_params=params(16),
        name="collect",
    )(onehot, recv)


def strength_kernel(core_ref, mine_ref, theirs_ref, record_ref, out_ref, own_ref, other_ref):
    step = pl.program_id(0)

    @pl.when(step == 0)
    def _():
        own_ref[...] = mine_ref[...].astype(F32)
        other_ref[...] = theirs_ref[...].astype(F32)

    row, col, same = tile_index()
    first = core_ref[0] == 0
    lower = same & (row >= col)
    upper = same & (row < col)
    diagonal = same & (row == col)
    zero = jnp.zeros((HALF, 128), F32)
    for j in range(CB):
        c = step * CB + j
        own = own_ref[pl.ds(c, 8, stride=CHILDREN_DEV), :]
        other = other_ref[pl.ds(c, 8, stride=CHILDREN_DEV), :]
        r = pl.ds(8 * CHILDREN_DEV + c, 1)
        diag = jnp.where(first, other_ref[r, :], own_ref[r, :])
        cross = jnp.where(same, four(jnp.where(first, own, other)), 0.0)
        triangle = four(jnp.where(first, other, own))
        m11 = jnp.where(lower, triangle, 0.0)
        m22 = jnp.where(upper, triangle, jnp.where(diagonal, diag, 0.0))
        lhs = jnp.concatenate(
            [jnp.concatenate([m11, zero], axis=1), jnp.concatenate([cross, m22], axis=1)], axis=0
        ).astype(BF)
        record = record_ref[j]
        rhs = jnp.concatenate([four(record[:HALF]), four(record[HALF:])], axis=0)
        rotated = dot(lhs, rhs)
        out_ref[j : j + 1, :] = jnp.sum(rotated * record.astype(F32), axis=0, keepdims=True)


def strengths(core, own, other, record):
    whole = (9 * CHILDREN_DEV, 128)
    return pl.pallas_call(
        strength_kernel,
        grid=(STEPS,),
        in_specs=[
            SMEM,
            pl.BlockSpec(whole, lambda i: (0, 0)),
            pl.BlockSpec(whole, lambda i: (0, 0)),
            pl.BlockSpec((CB, BLK, 128), lambda i: (i, 0, 0)),
        ],
        out_specs=pl.BlockSpec((CB, 128), lambda i: (i, 0)),
        out_shape=jax.ShapeDtypeStruct((CHILDREN_DEV, 128), F32),
        scratch_shapes=[pltpu.VMEM(whole, F32), pltpu.VMEM(whole, F32)],
        compiler_params=params(16),
        name="strengths",
    )(core, own, other, record)


def swap(x):
    return lax.ppermute(x, "mode", [(0, 1), (1, 0)])


def exchange(x, axes):
    return lax.all_to_all(x, axes, split_axis=0, concat_axis=0, tiled=True)


def per_device(coupling, pairs, modes, weights, parent_of, row_block, parent_modes, parent_eigs):
    core = lax.axis_index("mode").astype(jnp.int32).reshape(1)
    parent = parent_of.reshape(CHILDREN_DEV)
    record, own, other, onehot = moments(core, pairs.T, parent, row_block, coupling, modes, weights)
    sent = dispatch(onehot, own, swap(other))
    binned, chosen = bin_slots(exchange(sent, ("y", "x")))
    bins = exchange(binned, "z")
    blocks = pencil_blocks(core, bins, swap(bins), parent_modes[0], parent_eigs)
    picked = select_bins(exchange(blocks, "z"), chosen)
    mine = collect(onehot, exchange(picked, ("y", "x")))
    return strengths(core, mine, swap(mine), record)


def solution(mesh):
    grid = Mesh(mesh.devices.reshape(NY, NZ, NX, 2), ("y", "z", "x", "mode"))
    sub = ("y", "z", "x")
    in_specs = (
        P(sub, None, None),
        P(sub, None),
        P(sub, None, "mode"),
        P(sub, "mode"),
        P(sub, None),
        P(sub),
        P(sub, None, None),
        P(sub, None),
    )
    return jax.shard_map(
        per_device, mesh=grid, in_specs=in_specs, out_specs=P(sub, "mode"), check_vma=False
    )
```

```python
import jax
import jax.numpy as jnp
from jax import lax
from jax.experimental import pallas as pl
from jax.experimental.pallas import tpu as pltpu
from jax.sharding import PartitionSpec as P

MP = 256
BLK = 64
HALF = 32
SB = 8
CHILDREN_DEV = 64
CB = 16
STEPS = CHILDREN_DEV // CB
PARENTS = 128
SLOTS = 2 * PARENTS
ROWS = 24
BROWS = 72
PB = 32
BF = jnp.bfloat16
F32 = jnp.float32
VMEM = pl.BlockSpec(memory_space=pltpu.VMEM)
SMEM = pl.BlockSpec(memory_space=pltpu.SMEM)


def params(mib, **more):
    return pltpu.CompilerParams(vmem_limit_bytes=mib * 1024 * 1024, **more)


def dot(a, b):
    return jnp.dot(a, b, preferred_element_type=F32)


def dot_nt(a, b):
    return lax.dot_general(a, b, (((1,), (1,)), ((), ())), preferred_element_type=F32)


def dot_tn(a, b):
    return lax.dot_general(a, b, (((0,), (0,)), ((), ())), preferred_element_type=F32)


def four(x):
    return jnp.concatenate([x, x, x, x], axis=0)


def tile_index():
    row = lax.broadcasted_iota(jnp.int32, (HALF, 128), 0)
    lane = lax.broadcasted_iota(jnp.int32, (HALF, 128), 1)
    return row, lane % HALF, (lane // HALF) == (row // 8)


def pack(x):
    lane = lax.broadcasted_iota(jnp.int32, (8, 128), 1)
    low = jnp.where(lane < 32, x[0:8], x[8:16])
    high = jnp.where(lane < 96, x[16:24], x[24:32])
    return jnp.where(lane < 64, low, high)


def side_by_side(x):
    return jnp.concatenate([x[0:8], x[8:16], x[16:24], x[24:32]], axis=1)


def moments_kernel(
    core_ref, pairs_ref, parent_ref, block_ref, coupling_hbm, modes_hbm, weights_ref,
    record_ref, own_ref, other_ref, onehot_ref, coupling_ref, modes_ref, count_ref, coupling_sem, modes_sem,
):
    row = lax.broadcasted_iota(jnp.int32, (HALF, HALF), 0)
    col = lax.broadcasted_iota(jnp.int32, (HALF, HALF), 1)
    lower = row >= col
    diagonal = lax.broadcasted_iota(jnp.int32, (HALF, BLK), 1) == (
        lax.broadcasted_iota(jnp.int32, (HALF, BLK), 0) + HALF
    )
    slots = lax.broadcasted_iota(jnp.int32, (1, SLOTS), 1)
    first = core_ref[0] == 0

    def copies(step):
        part = pl.ds(step * CB, CB)
        return (
            pltpu.make_async_copy(modes_hbm.at[part], modes_ref.at[part], modes_sem.at[step]),
            pltpu.make_async_copy(coupling_hbm.at[part], coupling_ref.at[part], coupling_sem.at[step]),
        )

    for step in range(STEPS):
        for copy in copies(step):
            copy.start()
    for p in range(PARENTS):
        count_ref[p] = 0

    @pl.loop(0, STEPS)
    def _(step):
        for copy in copies(step):
            copy.wait()
        weights = weights_ref[pl.ds(pl.multiple_of(step * CB, CB), CB), :].astype(F32)
        for pair in range(CB // 2):
            records = []
            for j in (2 * pair, 2 * pair + 1):
                c = step * CB + j
                top = modes_ref[c, pl.ds(pl.multiple_of(pairs_ref[0, c] * BLK, BLK), BLK), :]
                bottom = modes_ref[c, pl.ds(pl.multiple_of(pairs_ref[1, c] * BLK, BLK), BLK), :]
                record = dot(coupling_ref[c], jnp.concatenate([top, bottom], axis=0))
                record = (record * weights[j : j + 1, :]).astype(BF)
                record_ref[c] = record
                records.append(record)
            both = jnp.concatenate(records, axis=0)
            products = dot_nt(both, both)
            for i in range(2):
                c = step * CB + 2 * pair + i
                s = products[i * BLK : (i + 1) * BLK, i * BLK : (i + 1) * BLK]
                cross = side_by_side(s[HALF:, :HALF])
                triangle = side_by_side(jnp.where(lower, s[:HALF, :HALF], s[HALF:, HALF:]))
                own_ref[pl.ds(c, 8, stride=CHILDREN_DEV), :] = jnp.where(first, cross, triangle)
                other_ref[pl.ds(c, 8, stride=CHILDREN_DEV), :] = jnp.where(first, triangle, cross)
                diag = jnp.sum(jnp.where(diagonal, s[HALF:], 0.0), axis=0, keepdims=True)
                zero = jnp.zeros((1, BLK), F32)
                named = zero + (block_ref[c] + 1).astype(F32)
                own_ref[pl.ds(8 * CHILDREN_DEV + c, 1), :] = jnp.concatenate([diag, named], axis=1)
                other_ref[pl.ds(8 * CHILDREN_DEV + c, 1), :] = jnp.concatenate([diag, zero], axis=1)
                p = parent_ref[c]
                k = count_ref[p]
                count_ref[p] = k + 1
                onehot_ref[pl.ds(c, 1), :] = jnp.where(slots == k * PARENTS + p, 1.0, 0.0)


def moments(core, pairs, parent, block, coupling, modes, weights):
    whole = (9 * CHILDREN_DEV, 128)
    hbm = pl.BlockSpec(memory_space=pltpu.HBM)
    return pl.pallas_call(
        moments_kernel,
        in_specs=[SMEM, SMEM, SMEM, SMEM, hbm, hbm, VMEM],
        out_specs=[VMEM, VMEM, VMEM, VMEM],
        out_shape=[
            jax.ShapeDtypeStruct((CHILDREN_DEV, BLK, 128), BF),
            jax.ShapeDtypeStruct(whole, F32),
            jax.ShapeDtypeStruct(whole, F32),
            jax.ShapeDtypeStruct((CHILDREN_DEV, SLOTS), F32),
        ],
        scratch_shapes=[
            pltpu.VMEM((CHILDREN_DEV, BLK, 128), BF),
            pltpu.VMEM((CHILDREN_DEV, 256, 128), BF),
            pltpu.SMEM((PARENTS,), jnp.int32),
            pltpu.SemaphoreType.DMA((STEPS,)),
            pltpu.SemaphoreType.DMA((STEPS,)),
        ],
        compiler_params=params(52),
        name="child_moments",
    )(core, pairs, parent, block, coupling, modes, weights)


def message_row(i, k):
    return k * 8 + i if i < 8 else 16 + k


def every_device(i, k):
    return pl.ds(message_row(i, k), PARENTS, stride=ROWS)


def dispatch_kernel(onehot_ref, own_ref, recv_ref, out_ref, buf_ref):
    place = onehot_ref[...].T.astype(BF)
    for i in range(9):
        rows = slice(i * CHILDREN_DEV, (i + 1) * CHILDREN_DEV)
        values = dot(place, (own_ref[rows, :] + recv_ref[rows, :]).astype(BF))
        for k in range(2):
            buf_ref[every_device(i, k), :] = values[k * PARENTS : (k + 1) * PARENTS]
    for r in range(18, ROWS):
        buf_ref[pl.ds(r, PARENTS, stride=ROWS), :] = jnp.zeros((PARENTS, 128), F32)
    out_ref[...] = buf_ref[...].astype(BF).reshape(PARENTS, ROWS, 128)


def dispatch(onehot, own, recv):
    return pl.pallas_call(
        dispatch_kernel,
        in_specs=[VMEM, VMEM, VMEM],
        out_specs=VMEM,
        out_shape=jax.ShapeDtypeStruct((PARENTS, ROWS, 128), BF),
        scratch_shapes=[pltpu.VMEM((PARENTS * ROWS, 128), F32)],
        compiler_params=params(16),
        name="dispatch",
    )(onehot, own, recv)


def bin_kernel(recv_ref, out_ref, onehot_ref, buf_ref):
    buf_ref[...] = recv_ref[...].astype(F32).reshape(PARENTS * ROWS, 128)

    def both(i):
        return jnp.concatenate([buf_ref[every_device(i, 0), :], buf_ref[every_device(i, 1), :]], axis=0)

    lane = lax.broadcasted_iota(jnp.int32, (SLOTS, 128), 1)
    last = both(8)
    named = pltpu.roll(last, 64, 1)
    hit = (lane < SB) & (named > 0.5) & (named - 1.0 == lane.astype(F32))
    onehot = jnp.where(hit, 1.0, 0.0).astype(BF)
    onehot_ref[...] = onehot
    values = jnp.concatenate([both(i).astype(BF) for i in range(8)] + [last.astype(BF)], axis=1)
    bins = dot_tn(onehot, values)
    for i in range(9):
        out_ref[i * SB : (i + 1) * SB, :] = bins[:SB, 128 * i : 128 * (i + 1)]


def bin_slots(recv):
    return pl.pallas_call(
        bin_kernel,
        in_specs=[VMEM],
        out_specs=[VMEM, VMEM],
        out_shape=[
            jax.ShapeDtypeStruct((BROWS, 128), F32),
            jax.ShapeDtypeStruct((SLOTS, 128), BF),
        ],
        scratch_shapes=[pltpu.VMEM((PARENTS * ROWS, 128), F32)],
        compiler_params=params(16),
        name="bin_slots",
    )(recv)


def invert(a_ref):
    lane = lax.broadcasted_iota(jnp.int32, (PB, MP), 1)
    row = lax.broadcasted_iota(jnp.int32, (PB, MP), 0)
    lane_all = lax.broadcasted_iota(jnp.int32, (MP, MP), 1)
    line = lane[:1]

    def wide(x):
        return jnp.concatenate([x, x], axis=1)

    for b in range(MP // PB):
        r = b * PB
        panel = a_ref[r : r + PB, :]
        for j in range(0, PB, 4):
            k = r + j
            inside = (line >= k) & (line < k + 4)
            c = [jnp.broadcast_to(panel[:, k + i : k + i + 1], (PB, 128)) for i in range(4)]
            p = [
                jnp.where(line == k + i, 1.0, jnp.where(inside, 0.0, panel[j + i : j + i + 1]))
                for i in range(4)
            ]
            a00, a01, a11 = c[0][j : j + 1], c[1][j : j + 1], c[1][j + 1 : j + 2]
            a02, a12, a22 = c[2][j : j + 1], c[2][j + 1 : j + 2], c[2][j + 2 : j + 3]
            a03, a13, a23 = c[3][j : j + 1], c[3][j + 1 : j + 2], c[3][j + 2 : j + 3]
            a33 = c[3][j + 3 : j + 4]
            scale = 1.0 / (a00 * a11 - a01 * a01)
            p00, p01, p11 = a11 * scale, -a01 * scale, a00 * scale
            t00, t10 = p00 * a02 + p01 * a12, p01 * a02 + p11 * a12
            t01, t11 = p00 * a03 + p01 * a13, p01 * a03 + p11 * a13
            s00 = a22 - (a02 * t00 + a12 * t10)
            s01 = a23 - (a02 * t01 + a12 * t11)
            s11 = a33 - (a03 * t01 + a13 * t11)
            scale = 1.0 / (s00 * s11 - s01 * s01)
            q00, q01, q11 = s11 * scale, -s01 * scale, s00 * scale
            t00, t10, t01, t11 = wide(t00), wide(t10), wide(t01), wide(t11)
            p00, p01, p11 = wide(p00), wide(p01), wide(p11)
            q00, q01, q11 = wide(q00), wide(q01), wide(q11)
            u2 = p[2] - (t00 * p[0] + t10 * p[1])
            u3 = p[3] - (t01 * p[0] + t11 * p[1])
            x2, x3 = q00 * u2 + q01 * u3, q01 * u2 + q11 * u3
            x0 = (p00 * p[0] + p01 * p[1]) - (t00 * x2 + t01 * x3)
            x1 = (p01 * p[0] + p11 * p[1]) - (t10 * x2 + t11 * x3)
            c = [wide(v) for v in c]
            rest = jnp.where((lane >= k) & (lane < k + 4), 0.0, panel) - (
                (c[0] * x0 + c[1] * x1) + (c[2] * x2 + c[3] * x3)
            )
            low = jnp.where(row == j, x0, jnp.where(row == j + 1, x1, rest))
            panel = jnp.where(row == j + 2, x2, jnp.where(row == j + 3, x3, low))
        ch, cm, cl = split3(a_ref[:, r : r + PB])
        ph, pm, pw = split3(panel)
        update = dot(
            jnp.concatenate([ch, ch, cm, ch, cm, cl], axis=1),
            jnp.concatenate([ph, pm, ph, pw, pm, ph], axis=0),
        )
        a_ref[...] = jnp.where((lane_all // PB) == b, 0.0, a_ref[...]) - update
        a_ref[r : r + PB, :] = panel


def split3(x):
    high = x.astype(BF)
    rest = x - high.astype(F32)
    mid = rest.astype(BF)
    return high, mid, (rest - mid.astype(F32)).astype(BF)


def split(x):
    high = x.astype(BF)
    return high, (x - high.astype(F32)).astype(BF)


def pencil_kernel(
    core_ref, own_ref, other_ref, onehot_ref, q_ref, eigs_ref, out_ref, a_ref, y_ref, pack_ref, buf_ref
):
    row, col, same = tile_index()
    first = core_ref[0] == 0
    lane8 = lax.broadcasted_iota(jnp.int32, (8, 128), 1)
    diags = jnp.where(first, other_ref[64:72, :], own_ref[64:72, :])
    diags = jnp.where((lane8 >= 32) & (lane8 < 64), diags, 0.0)
    diags = diags + pltpu.roll(diags, 32, 1)
    diags = diags + pltpu.roll(diags, 64, 1)
    zero = jnp.zeros((HALF, 128), F32)
    for b in range(SB):
        own = own_ref[pl.ds(b, 8, stride=8), :]
        other = other_ref[pl.ds(b, 8, stride=8), :]
        cross = jnp.where(same, four(jnp.where(first, own, other)), 0.0)
        triangle = jnp.where(same, four(jnp.where(first, other, own)), 0.0)
        n11 = jnp.where(row > col, triangle, jnp.where(row == col, 0.5 * triangle, 0.0))
        half = jnp.where(same & (row == col), 0.5 * diags[b : b + 1, :], 0.0)
        n22 = jnp.where(row < col, triangle, half)
        lhs = jnp.concatenate(
            [jnp.concatenate([n11, zero], axis=1), jnp.concatenate([cross, n22], axis=1)], axis=0
        ).astype(BF)
        q1 = q_ref[b * BLK : b * BLK + HALF, :]
        q2 = q_ref[b * BLK + HALF : (b + 1) * BLK, :]
        y_ref[b * BLK : (b + 1) * BLK, :] = dot(lhs, jnp.concatenate([four(q1), four(q2)], axis=0)).astype(BF)
    x = dot_tn(q_ref[...], y_ref[...])
    r = lax.broadcasted_iota(jnp.int32, (MP, MP), 0)
    c = lax.broadcasted_iota(jnp.int32, (MP, MP), 1)
    a_ref[...] = (x + x.T) * (1.0 / 16384.0) + jnp.where(r == c, eigs_ref[...], 0.0)
    invert(a_ref)
    high, low = split(a_ref[...] * (1.0 / MP))
    q = q_ref[...]
    y_high, y_low = split(dot(q, high) + dot(q, low))
    for b in range(SB):
        s = b * BLK
        qb = q_ref[s : s + BLK, :]
        u = dot_nt(qb, four(y_high[s : s + HALF])) + dot_nt(qb, four(y_low[s : s + HALF]))
        v = dot_nt(qb[HALF:], four(y_high[s + HALF : s + BLK])) + dot_nt(
            qb[HALF:], four(y_low[s + HALF : s + BLK])
        )
        cross = pack(2.0 * u[HALF:])
        triangle = pack(
            jnp.where(row > col, 2.0 * u[:HALF], jnp.where(row == col, u[:HALF], 2.0 * v))
        )
        pack_ref[pl.ds(b, 8, stride=8), :] = jnp.where(first, cross, triangle)
        pack_ref[8 * SB + b : 8 * SB + b + 1, :] = jnp.sum(jnp.where(row == col, v, 0.0), axis=0, keepdims=True)
    blocks = jnp.concatenate([pack_ref[i * SB : (i + 1) * SB, :] for i in range(9)], axis=1).astype(BF)
    picked = dot(onehot_ref[:, :SB], blocks)
    for i in range(9):
        for k in range(2):
            buf_ref[every_device(i, k), :] = picked[k * PARENTS : (k + 1) * PARENTS, 128 * i : 128 * (i + 1)]
    for r in range(18, ROWS):
        buf_ref[pl.ds(r, PARENTS, stride=ROWS), :] = jnp.zeros((PARENTS, 128), F32)
    out_ref[...] = buf_ref[...].astype(BF).reshape(PARENTS, ROWS, 128)


def pencil_blocks(core, own, other, onehot, q, eigs):
    return pl.pallas_call(
        pencil_kernel,
        in_specs=[SMEM, VMEM, VMEM, VMEM, VMEM, VMEM],
        out_specs=VMEM,
        out_shape=jax.ShapeDtypeStruct((PARENTS, ROWS, 128), BF),
        scratch_shapes=[
            pltpu.VMEM((MP, MP), F32),
            pltpu.VMEM((SB * BLK, MP), BF),
            pltpu.VMEM((BROWS, 128), F32),
            pltpu.VMEM((PARENTS * ROWS, 128), F32),
        ],
        compiler_params=params(16),
        name="pencil_blocks",
    )(core, own, other, onehot, q, eigs)


def collect_kernel(onehot_ref, recv_ref, out_ref, buf_ref):
    buf_ref[...] = recv_ref[...].astype(F32).reshape(PARENTS * ROWS, 128)
    onehot = onehot_ref[...].astype(BF)
    for i in range(9):
        values = jnp.concatenate([buf_ref[every_device(i, 0), :], buf_ref[every_device(i, 1), :]], axis=0)
        out_ref[i * CHILDREN_DEV : (i + 1) * CHILDREN_DEV, :] = dot(onehot, values.astype(BF)).astype(BF)


def collect(onehot, recv):
    return pl.pallas_call(
        collect_kernel,
        in_specs=[VMEM, VMEM],
        out_specs=VMEM,
        out_shape=jax.ShapeDtypeStruct((9 * CHILDREN_DEV, 128), BF),
        scratch_shapes=[pltpu.VMEM((PARENTS * ROWS, 128), F32)],
        compiler_params=params(16),
        name="collect",
    )(onehot, recv)


def strength_kernel(core_ref, mine_ref, theirs_ref, record_ref, out_ref, own_ref, other_ref):
    step = pl.program_id(0)

    @pl.when(step == 0)
    def _():
        own_ref[...] = mine_ref[...].astype(F32)
        other_ref[...] = theirs_ref[...].astype(F32)

    row, col, same = tile_index()
    first = core_ref[0] == 0
    lower = same & (row >= col)
    upper = same & (row < col)
    diagonal = same & (row == col)
    zero = jnp.zeros((HALF, 128), F32)
    for j in range(CB):
        c = step * CB + j
        own = own_ref[pl.ds(c, 8, stride=CHILDREN_DEV), :]
        other = other_ref[pl.ds(c, 8, stride=CHILDREN_DEV), :]
        r = pl.ds(8 * CHILDREN_DEV + c, 1)
        diag = jnp.where(first, other_ref[r, :], own_ref[r, :])
        cross = jnp.where(same, four(jnp.where(first, own, other)), 0.0)
        triangle = four(jnp.where(first, other, own))
        m11 = jnp.where(lower, triangle, 0.0)
        m22 = jnp.where(upper, triangle, jnp.where(diagonal, diag, 0.0))
        lhs = jnp.concatenate(
            [jnp.concatenate([m11, zero], axis=1), jnp.concatenate([cross, m22], axis=1)], axis=0
        ).astype(BF)
        record = record_ref[j]
        rhs = jnp.concatenate([four(record[:HALF]), four(record[HALF:])], axis=0)
        rotated = dot(lhs, rhs)
        out_ref[j : j + 1, :] = jnp.sum(rotated * record.astype(F32), axis=0, keepdims=True)


def strengths(core, own, other, record):
    whole = (9 * CHILDREN_DEV, 128)
    return pl.pallas_call(
        strength_kernel,
        grid=(STEPS,),
        in_specs=[
            SMEM,
            pl.BlockSpec(whole, lambda i: (0, 0)),
            pl.BlockSpec(whole, lambda i: (0, 0)),
            pl.BlockSpec((CB, BLK, 128), lambda i: (i, 0, 0)),
        ],
        out_specs=pl.BlockSpec((CB, 128), lambda i: (i, 0)),
        out_shape=jax.ShapeDtypeStruct((CHILDREN_DEV, 128), F32),
        scratch_shapes=[pltpu.VMEM(whole, F32), pltpu.VMEM(whole, F32)],
        compiler_params=params(16),
        name="strengths",
    )(core, own, other, record)


def swap(x):
    return lax.ppermute(x, "mode", [(0, 1), (1, 0)])


def exchange(x):
    return lax.all_to_all(x, "sub", split_axis=0, concat_axis=0, tiled=True)


def per_device(coupling, pairs, modes, weights, parent_of, row_block, parent_modes, parent_eigs):
    core = lax.axis_index("mode").astype(jnp.int32).reshape(1)
    parent = parent_of.reshape(CHILDREN_DEV)
    record, own, other, onehot = moments(core, pairs.T, parent, row_block, coupling, modes, weights)
    bins, chosen = bin_slots(exchange(dispatch(onehot, own, swap(other))))
    picked = pencil_blocks(core, bins, swap(bins), chosen, parent_modes[0], parent_eigs)
    mine = collect(onehot, exchange(picked))
    return strengths(core, mine, swap(mine), record)


def solution(mesh):
    in_specs = (
        P("sub", None, None),
        P("sub", None),
        P("sub", None, "mode"),
        P("sub", "mode"),
        P("sub", None),
        P("sub"),
        P("sub", None, None),
        P("sub", None),
    )
    return jax.shard_map(
        per_device, mesh=mesh, in_specs=in_specs, out_specs=P("sub", "mode"), check_vma=False
    )
```

```python
import jax
import jax.numpy as jnp
from jax import lax
from jax.experimental import pallas as pl
from jax.experimental.pallas import tpu as pltpu
from jax.sharding import Mesh, PartitionSpec as P

MP = 256
BLK = 64
HALF = 32
SB = 8
CHILDREN_DEV = 64
CB = 32
STEPS = CHILDREN_DEV // CB
NY, NZ, NX = 4, 8, 4
NG = NY * NX
SLOTS = 2 * NZ
ROWS = 9 * SLOTS
ZROWS = 80
PB = 32
BF = jnp.bfloat16
F32 = jnp.float32
VMEM = pl.BlockSpec(memory_space=pltpu.VMEM)
SMEM = pl.BlockSpec(memory_space=pltpu.SMEM)


def params(mib, **more):
    return pltpu.CompilerParams(vmem_limit_bytes=mib * 1024 * 1024, **more)


def dot(a, b):
    return jnp.dot(a, b, preferred_element_type=F32)


def dot_nt(a, b):
    return lax.dot_general(a, b, (((1,), (1,)), ((), ())), preferred_element_type=F32)


def dot_tn(a, b):
    return lax.dot_general(a, b, (((0,), (0,)), ((), ())), preferred_element_type=F32)


def four(x):
    return jnp.concatenate([x, x, x, x], axis=0)


def tile_index():
    row = lax.broadcasted_iota(jnp.int32, (HALF, 128), 0)
    lane = lax.broadcasted_iota(jnp.int32, (HALF, 128), 1)
    return row, lane % HALF, (lane // HALF) == (row // 8)


def pack(x):
    lane = lax.broadcasted_iota(jnp.int32, (8, 128), 1)
    low = jnp.where(lane < 32, x[0:8], x[8:16])
    high = jnp.where(lane < 96, x[16:24], x[24:32])
    return jnp.where(lane < 64, low, high)


def side_by_side(x):
    return jnp.concatenate([x[0:8], x[8:16], x[16:24], x[24:32]], axis=1)


def moments_kernel(
    core_ref, pairs_ref, parent_ref, block_ref, coupling_hbm, modes_hbm, weights_ref,
    record_ref, own_ref, other_ref, coupling_ref, modes_ref, count_ref, coupling_sem, modes_sem,
):
    row = lax.broadcasted_iota(jnp.int32, (HALF, HALF), 0)
    col = lax.broadcasted_iota(jnp.int32, (HALF, HALF), 1)
    lower = row >= col
    diagonal = lax.broadcasted_iota(jnp.int32, (HALF, BLK), 1) == (
        lax.broadcasted_iota(jnp.int32, (HALF, BLK), 0) + HALF
    )
    slots = lax.broadcasted_iota(jnp.int32, (1, 128), 1)
    first = core_ref[0] == 0

    def copies(step):
        part = pl.ds(step * CB, CB)
        return (
            pltpu.make_async_copy(modes_hbm.at[part], modes_ref.at[part], modes_sem.at[step]),
            pltpu.make_async_copy(coupling_hbm.at[part], coupling_ref.at[part], coupling_sem.at[step]),
        )

    for step in range(STEPS):
        for copy in copies(step):
            copy.start()
    for p in range(NG * NZ):
        count_ref[p] = 0

    @pl.loop(0, STEPS)
    def _(step):
        for copy in copies(step):
            copy.wait()
        weights = weights_ref[pl.ds(pl.multiple_of(step * CB, CB), CB), :].astype(F32)
        for pair in range(CB // 2):
            records = []
            for j in (2 * pair, 2 * pair + 1):
                c = step * CB + j
                top = modes_ref[c, pl.ds(pl.multiple_of(pairs_ref[0, c] * BLK, BLK), BLK), :]
                bottom = modes_ref[c, pl.ds(pl.multiple_of(pairs_ref[1, c] * BLK, BLK), BLK), :]
                record = dot(coupling_ref[c], jnp.concatenate([top, bottom], axis=0))
                record = (record * weights[j : j + 1, :]).astype(BF)
                record_ref[c] = record
                records.append(record)
            both = jnp.concatenate(records, axis=0)
            products = dot_nt(both, both)
            for i in range(2):
                c = step * CB + 2 * pair + i
                s = products[i * BLK : (i + 1) * BLK, i * BLK : (i + 1) * BLK]
                cross = side_by_side(s[HALF:, :HALF])
                triangle = side_by_side(jnp.where(lower, s[:HALF, :HALF], s[HALF:, HALF:]))
                own_ref[pl.ds(c, 8, stride=CHILDREN_DEV), :] = jnp.where(first, cross, triangle)
                other_ref[pl.ds(c, 8, stride=CHILDREN_DEV), :] = jnp.where(first, triangle, cross)
                diag = jnp.sum(jnp.where(diagonal, s[HALF:], 0.0), axis=0, keepdims=True)
                zero = jnp.zeros((1, BLK), F32)
                named = zero + (block_ref[c] + 1).astype(F32)
                own_ref[pl.ds(8 * CHILDREN_DEV + c, 1), :] = jnp.concatenate([diag, named], axis=1)
                other_ref[pl.ds(8 * CHILDREN_DEV + c, 1), :] = jnp.concatenate([diag, zero], axis=1)
                p = parent_ref[c]
                k = count_ref[p]
                count_ref[p] = k + 1
                group = (p // (NZ * NX)) * NX + p % NX
                slot = group * SLOTS + ((p // NX) % NZ) * 2 + k
                for h in range(2):
                    hit = jnp.where(slots == slot - 128 * h, 1.0, 0.0)
                    own_ref[pl.ds((9 + h) * CHILDREN_DEV + c, 1), :] = hit


def moments(core, pairs, parent, block, coupling, modes, weights):
    hbm = pl.BlockSpec(memory_space=pltpu.HBM)
    return pl.pallas_call(
        moments_kernel,
        in_specs=[SMEM, SMEM, SMEM, SMEM, hbm, hbm, VMEM],
        out_specs=[VMEM, VMEM, VMEM],
        out_shape=[
            jax.ShapeDtypeStruct((CHILDREN_DEV, BLK, 128), BF),
            jax.ShapeDtypeStruct((11 * CHILDREN_DEV, 128), F32),
            jax.ShapeDtypeStruct((9 * CHILDREN_DEV, 128), F32),
        ],
        scratch_shapes=[
            pltpu.VMEM((CHILDREN_DEV, BLK, 128), BF),
            pltpu.VMEM((CHILDREN_DEV, 256, 128), BF),
            pltpu.SMEM((NG * NZ,), jnp.int32),
            pltpu.SemaphoreType.DMA((STEPS,)),
            pltpu.SemaphoreType.DMA((STEPS,)),
        ],
        compiler_params=params(60),
        name="child_moments",
    )(core, pairs, parent, block, coupling, modes, weights)


def message_row(i, k):
    return k * 8 + i if i < 8 else 16 + k


def every_device(i, k):
    return pl.ds(message_row(i, k), PARENTS, stride=ROWS)


def stage_kernel(own_ref, sums_ref, place_ref, onehot_ref):
    sums_ref[...] = own_ref[: 9 * CHILDREN_DEV, :]
    onehot = jnp.concatenate(
        [own_ref[9 * CHILDREN_DEV : 10 * CHILDREN_DEV, :], own_ref[10 * CHILDREN_DEV :, :]], axis=1
    )
    place_ref[...] = onehot.T.astype(BF)
    onehot_ref[...] = onehot.astype(BF)


def stage(own):
    return pl.pallas_call(
        stage_kernel,
        in_specs=[VMEM],
        out_specs=[VMEM, VMEM, VMEM],
        out_shape=[
            jax.ShapeDtypeStruct((9 * CHILDREN_DEV, 128), F32),
            jax.ShapeDtypeStruct((NG * SLOTS, CHILDREN_DEV), BF),
            jax.ShapeDtypeStruct((CHILDREN_DEV, NG * SLOTS), BF),
        ],
        compiler_params=params(16),
        name="stage",
    )(own)


def dispatch_kernel(place_ref, own_ref, recv_ref, out_ref):
    place = place_ref[...]
    for i in range(9):
        rows = slice(i * CHILDREN_DEV, (i + 1) * CHILDREN_DEV)
        values = (own_ref[rows, :] + recv_ref[rows, :]).astype(BF)
        out_ref[:, i * SLOTS : (i + 1) * SLOTS, :] = dot(place, values).astype(BF).reshape(NG, SLOTS, 128)


def dispatch(place, own, recv):
    return pl.pallas_call(
        dispatch_kernel,
        in_specs=[VMEM, VMEM, VMEM],
        out_specs=VMEM,
        out_shape=jax.ShapeDtypeStruct((NG, ROWS, 128), BF),
        compiler_params=params(16),
        name="dispatch",
    )(place, own, recv)


def bin_kernel(recv_ref, out_ref, onehot_ref):
    count = NG * SLOTS
    meta = recv_ref[:, 8 * SLOTS : ROWS, :].astype(F32).reshape(count, 128)
    slot = lax.broadcasted_iota(jnp.int32, (count, 128), 0) % SLOTS
    lane = lax.broadcasted_iota(jnp.int32, (count, 128), 1)
    meta = pltpu.roll(meta, 64, 1)
    target = meta + (SB * (slot // 2) - 1).astype(F32)
    hit = (lane < 64) & (meta > 0.5) & (target == lane.astype(F32))
    onehot = jnp.where(hit, 1.0, 0.0).astype(BF)
    onehot_ref[...] = onehot
    values = jnp.concatenate(
        [recv_ref[:, i * SLOTS : (i + 1) * SLOTS, :].reshape(count, 128) for i in range(9)], axis=1
    )
    bins = dot_tn(onehot, values)
    zero = jnp.zeros((8, 128), F32)
    for z in range(NZ):
        rows = [bins[8 * z : 8 * z + 8, 128 * i : 128 * (i + 1)] for i in range(9)] + [zero]
        out_ref[z] = jnp.concatenate(rows, axis=0).astype(BF)


def bin_slots(recv):
    return pl.pallas_call(
        bin_kernel,
        in_specs=[VMEM],
        out_specs=[VMEM, VMEM],
        out_shape=[
            jax.ShapeDtypeStruct((NZ, ZROWS, 128), BF),
            jax.ShapeDtypeStruct((NG * SLOTS, 128), BF),
        ],
        compiler_params=params(16),
        name="bin_slots",
    )(recv)


def wide(x):
    return jnp.concatenate([x, x], axis=1)


def pivot_block(c, j):
    a00, a01, a11 = c[0][j : j + 1], c[1][j : j + 1], c[1][j + 1 : j + 2]
    a02, a12, a22 = c[2][j : j + 1], c[2][j + 1 : j + 2], c[2][j + 2 : j + 3]
    a03, a13, a23 = c[3][j : j + 1], c[3][j + 1 : j + 2], c[3][j + 2 : j + 3]
    a33 = c[3][j + 3 : j + 4]
    scale = 1.0 / (a00 * a11 - a01 * a01)
    p00, p01, p11 = a11 * scale, -a01 * scale, a00 * scale
    t00, t10 = p00 * a02 + p01 * a12, p01 * a02 + p11 * a12
    t01, t11 = p00 * a03 + p01 * a13, p01 * a03 + p11 * a13
    s00 = a22 - (a02 * t00 + a12 * t10)
    s01 = a23 - (a02 * t01 + a12 * t11)
    s11 = a33 - (a03 * t01 + a13 * t11)
    scale = 1.0 / (s00 * s11 - s01 * s01)
    return p00, p01, p11, t00, t10, t01, t11, s11 * scale, -s01 * scale, s00 * scale


def solve_block(block, p):
    p00, p01, p11, t00, t10, t01, t11, q00, q01, q11 = block
    u2 = p[2] - (t00 * p[0] + t10 * p[1])
    u3 = p[3] - (t01 * p[0] + t11 * p[1])
    x2, x3 = q00 * u2 + q01 * u3, q01 * u2 + q11 * u3
    x0 = (p00 * p[0] + p01 * p[1]) - (t00 * x2 + t01 * x3)
    x1 = (p01 * p[0] + p11 * p[1]) - (t10 * x2 + t11 * x3)
    return x0, x1, x2, x3


def eliminate(row, j, rest, c, x):
    rest = rest - ((c[0] * x[0] + c[1] * x[1]) + (c[2] * x[2] + c[3] * x[3]))
    low = jnp.where(row == j, x[0], jnp.where(row == j + 1, x[1], rest))
    return jnp.where(row == j + 2, x[2], jnp.where(row == j + 3, x[3], low))


def invert(a_ref):
    lane = lax.broadcasted_iota(jnp.int32, (PB, MP), 1)
    row = lax.broadcasted_iota(jnp.int32, (PB, MP), 0)
    lane_all = lax.broadcasted_iota(jnp.int32, (MP, MP), 1)
    line = lane[:1]
    for b in range(MP // PB):
        r = b * PB
        panel = a_ref[r : r + PB, :]
        for j8 in range(0, PB, 8):
            c = [jnp.broadcast_to(panel[:, r + j8 + i : r + j8 + i + 1], (PB, 128)) for i in range(8)]
            for h in (0, 4):
                j = j8 + h
                k = r + j
                lead = c[h : h + 4]
                block = pivot_block(lead, j)
                for m in range(h + 4, 8):
                    x = solve_block(block, [c[m][j + i : j + i + 1] for i in range(4)])
                    c[m] = eliminate(row[:, :128], j, c[m], lead, x)
                inside = (line >= k) & (line < k + 4)
                p = [
                    jnp.where(line == k + i, 1.0, jnp.where(inside, 0.0, panel[j + i : j + i + 1]))
                    for i in range(4)
                ]
                x = solve_block([wide(v) for v in block], p)
                rest = jnp.where((lane >= k) & (lane < k + 4), 0.0, panel)
                panel = eliminate(row, j, rest, [wide(v) for v in lead], x)
        ch, cm, cl = split3(a_ref[:, r : r + PB])
        ph, pm, pw = split3(panel)
        update = dot(
            jnp.concatenate([ch, ch, cm, ch, cm, cl], axis=1),
            jnp.concatenate([ph, pm, ph, pw, pm, ph], axis=0),
        )
        a_ref[...] = jnp.where((lane_all // PB) == b, 0.0, a_ref[...]) - update
        a_ref[r : r + PB, :] = panel


def split3(x):
    high = x.astype(BF)
    rest = x - high.astype(F32)
    mid = rest.astype(BF)
    return high, mid, (rest - mid.astype(F32)).astype(BF)


def split(x):
    high = x.astype(BF)
    return high, (x - high.astype(F32)).astype(BF)


def pencil_kernel(
    core_ref, mine_ref, theirs_ref, q_ref, eigs_ref, out_ref, a_ref, y_ref, pack_ref, own_ref, other_ref
):
    for source, target in ((mine_ref, own_ref), (theirs_ref, other_ref)):
        parts = [source[z].astype(F32) for z in range(NZ)]
        while len(parts) > 1:
            parts = [x + y for x, y in zip(parts[::2], parts[1::2])]
        target[...] = parts[0]
    row, col, same = tile_index()
    first = core_ref[0] == 0
    lane8 = lax.broadcasted_iota(jnp.int32, (8, 128), 1)
    diags = jnp.where(first, other_ref[64:72, :], own_ref[64:72, :])
    diags = jnp.where((lane8 >= 32) & (lane8 < 64), diags, 0.0)
    diags = diags + pltpu.roll(diags, 32, 1)
    diags = diags + pltpu.roll(diags, 64, 1)
    zero = jnp.zeros((HALF, 128), F32)
    for b in range(SB):
        own = own_ref[pl.ds(b, 8, stride=8), :]
        other = other_ref[pl.ds(b, 8, stride=8), :]
        cross = jnp.where(same, four(jnp.where(first, own, other)), 0.0)
        triangle = jnp.where(same, four(jnp.where(first, other, own)), 0.0)
        n11 = jnp.where(row > col, triangle, jnp.where(row == col, 0.5 * triangle, 0.0))
        half = jnp.where(same & (row == col), 0.5 * diags[b : b + 1, :], 0.0)
        n22 = jnp.where(row < col, triangle, half)
        lhs = jnp.concatenate(
            [jnp.concatenate([n11, zero], axis=1), jnp.concatenate([cross, n22], axis=1)], axis=0
        ).astype(BF)
        q1 = q_ref[b * BLK : b * BLK + HALF, :]
        q2 = q_ref[b * BLK + HALF : (b + 1) * BLK, :]
        y_ref[b * BLK : (b + 1) * BLK, :] = dot(lhs, jnp.concatenate([four(q1), four(q2)], axis=0)).astype(BF)
    x = dot_tn(q_ref[...], y_ref[...])
    r = lax.broadcasted_iota(jnp.int32, (MP, MP), 0)
    c = lax.broadcasted_iota(jnp.int32, (MP, MP), 1)
    a_ref[...] = (x + x.T) * (1.0 / 16384.0) + jnp.where(r == c, eigs_ref[...], 0.0)
    invert(a_ref)
    high, low = split(a_ref[...] * (1.0 / MP))
    q = q_ref[...]
    y_high, y_low = split(dot(q, high) + dot(q, low))
    for b in range(SB):
        s = b * BLK
        qb = q_ref[s : s + BLK, :]
        u = dot_nt(qb, four(y_high[s : s + HALF])) + dot_nt(qb, four(y_low[s : s + HALF]))
        v = dot_nt(qb[HALF:], four(y_high[s + HALF : s + BLK])) + dot_nt(
            qb[HALF:], four(y_low[s + HALF : s + BLK])
        )
        cross = pack(2.0 * u[HALF:])
        triangle = pack(
            jnp.where(row > col, 2.0 * u[:HALF], jnp.where(row == col, u[:HALF], 2.0 * v))
        )
        pack_ref[pl.ds(b, 8, stride=8), :] = jnp.where(first, cross, triangle)
        pack_ref[64 + b : 65 + b, :] = jnp.sum(jnp.where(row == col, v, 0.0), axis=0, keepdims=True)
    pack_ref[72:80, :] = jnp.zeros((8, 128), F32)
    result = pack_ref[...].astype(BF)
    for z in range(NZ):
        out_ref[z] = result


def pencil_blocks(core, own, other, q, eigs):
    return pl.pallas_call(
        pencil_kernel,
        in_specs=[SMEM, VMEM, VMEM, VMEM, VMEM],
        out_specs=VMEM,
        out_shape=jax.ShapeDtypeStruct((NZ, ZROWS, 128), BF),
        scratch_shapes=[
            pltpu.VMEM((MP, MP), F32),
            pltpu.VMEM((SB * BLK, MP), BF),
            pltpu.VMEM((ZROWS, 128), F32),
            pltpu.VMEM((ZROWS, 128), F32),
            pltpu.VMEM((ZROWS, 128), F32),
        ],
        compiler_params=params(16),
        name="pencil_blocks",
    )(core, own, other, q, eigs)


def select_kernel(bins_ref, onehot_ref, out_ref):
    onehot = onehot_ref[:, 0:64]
    bins = [bins_ref[z].astype(F32) for z in range(NZ)]
    for i in range(9):
        values = jnp.concatenate([x[8 * i : 8 * i + 8] for x in bins], axis=0).astype(BF)
        picked = dot(onehot, values).astype(BF)
        out_ref[:, i * SLOTS : (i + 1) * SLOTS, :] = picked.reshape(NG, SLOTS, 128)


def select_bins(bins, onehot):
    return pl.pallas_call(
        select_kernel,
        in_specs=[VMEM, VMEM],
        out_specs=VMEM,
        out_shape=jax.ShapeDtypeStruct((NG, ROWS, 128), BF),
        compiler_params=params(16),
        name="select_bins",
    )(bins, onehot)


def collect_kernel(onehot_ref, recv_ref, out_ref):
    onehot = onehot_ref[...]
    for i in range(9):
        values = recv_ref[:, i * SLOTS : (i + 1) * SLOTS, :].reshape(NG * SLOTS, 128)
        out_ref[i * CHILDREN_DEV : (i + 1) * CHILDREN_DEV, :] = dot(onehot, values).astype(BF)


def collect(onehot, recv):
    return pl.pallas_call(
        collect_kernel,
        in_specs=[VMEM, VMEM],
        out_specs=VMEM,
        out_shape=jax.ShapeDtypeStruct((9 * CHILDREN_DEV, 128), BF),
        compiler_params=params(16),
        name="collect",
    )(onehot, recv)


def strength_kernel(core_ref, mine_ref, theirs_ref, record_ref, out_ref, own_ref, other_ref):
    step = pl.program_id(0)

    @pl.when(step == 0)
    def _():
        own_ref[...] = mine_ref[...].astype(F32)
        other_ref[...] = theirs_ref[...].astype(F32)

    row, col, same = tile_index()
    first = core_ref[0] == 0
    lower = same & (row >= col)
    upper = same & (row < col)
    diagonal = same & (row == col)
    zero = jnp.zeros((HALF, 128), F32)
    for j in range(CB):
        c = step * CB + j
        own = own_ref[pl.ds(c, 8, stride=CHILDREN_DEV), :]
        other = other_ref[pl.ds(c, 8, stride=CHILDREN_DEV), :]
        r = pl.ds(8 * CHILDREN_DEV + c, 1)
        diag = jnp.where(first, other_ref[r, :], own_ref[r, :])
        cross = jnp.where(same, four(jnp.where(first, own, other)), 0.0)
        triangle = four(jnp.where(first, other, own))
        m11 = jnp.where(lower, triangle, 0.0)
        m22 = jnp.where(upper, triangle, jnp.where(diagonal, diag, 0.0))
        lhs = jnp.concatenate(
            [jnp.concatenate([m11, zero], axis=1), jnp.concatenate([cross, m22], axis=1)], axis=0
        ).astype(BF)
        record = record_ref[j]
        rhs = jnp.concatenate([four(record[:HALF]), four(record[HALF:])], axis=0)
        rotated = dot(lhs, rhs)
        out_ref[j : j + 1, :] = jnp.sum(rotated * record.astype(F32), axis=0, keepdims=True)


def strengths(core, own, other, record):
    whole = (9 * CHILDREN_DEV, 128)
    return pl.pallas_call(
        strength_kernel,
        grid=(STEPS,),
        in_specs=[
            SMEM,
            pl.BlockSpec(whole, lambda i: (0, 0)),
            pl.BlockSpec(whole, lambda i: (0, 0)),
            pl.BlockSpec((CB, BLK, 128), lambda i: (i, 0, 0)),
        ],
        out_specs=pl.BlockSpec((CB, 128), lambda i: (i, 0)),
        out_shape=jax.ShapeDtypeStruct((CHILDREN_DEV, 128), F32),
        scratch_shapes=[pltpu.VMEM(whole, F32), pltpu.VMEM(whole, F32)],
        compiler_params=params(16),
        name="strengths",
    )(core, own, other, record)


def swap(x):
    return lax.ppermute(x, "mode", [(0, 1), (1, 0)])


def exchange(x, axes):
    return lax.all_to_all(x, axes, split_axis=0, concat_axis=0, tiled=True)


def per_device(coupling, pairs, modes, weights, parent_of, row_block, parent_modes, parent_eigs):
    core = lax.axis_index("mode").astype(jnp.int32).reshape(1)
    parent = parent_of.reshape(CHILDREN_DEV)
    record, own, other = moments(core, pairs.T, parent, row_block, coupling, modes, weights)
    sums, place, onehot = stage(own)
    sent = dispatch(place, sums, swap(other))
    binned, chosen = bin_slots(exchange(sent, ("y", "x")))
    bins = exchange(binned, "z")
    blocks = pencil_blocks(core, bins, swap(bins), parent_modes[0], parent_eigs)
    picked = select_bins(exchange(blocks, "z"), chosen)
    mine = collect(onehot, exchange(picked, ("y", "x")))
    return strengths(core, mine, swap(mine), record)


def solution(mesh):
    grid = Mesh(mesh.devices.reshape(NY, NZ, NX, 2), ("y", "z", "x", "mode"))
    sub = ("y", "z", "x")
    in_specs = (
        P(sub, None, None),
        P(sub, None),
        P(sub, None, "mode"),
        P(sub, "mode"),
        P(sub, None),
        P(sub),
        P(sub, None, None),
        P(sub, None),
    )
    return jax.shard_map(
        per_device, mesh=grid, in_specs=in_specs, out_specs=P(sub, "mode"), check_vma=False
    )
```

```python
import jax
import jax.numpy as jnp
from jax import lax
from jax.experimental import pallas as pl
from jax.experimental.pallas import tpu as pltpu
from jax.sharding import Mesh, PartitionSpec as P

MP = 256
BLK = 64
HALF = 32
SB = 8
CHILDREN_DEV = 64
CB = 32
STEPS = CHILDREN_DEV // CB
NY, NZ, NX = 4, 8, 4
NG = NY * NX
SLOTS = 2 * NZ
ROWS = 9 * SLOTS
ZROWS = 80
PB = 32
BF = jnp.bfloat16
F32 = jnp.float32
VMEM = pl.BlockSpec(memory_space=pltpu.VMEM)
SMEM = pl.BlockSpec(memory_space=pltpu.SMEM)


def params(mib, **more):
    return pltpu.CompilerParams(vmem_limit_bytes=mib * 1024 * 1024, **more)


def dot(a, b):
    return jnp.dot(a, b, preferred_element_type=F32)


def dot_nt(a, b):
    return lax.dot_general(a, b, (((1,), (1,)), ((), ())), preferred_element_type=F32)


def dot_tn(a, b):
    return lax.dot_general(a, b, (((0,), (0,)), ((), ())), preferred_element_type=F32)


def four(x):
    return jnp.concatenate([x, x, x, x], axis=0)


def tile_index():
    row = lax.broadcasted_iota(jnp.int32, (HALF, 128), 0)
    lane = lax.broadcasted_iota(jnp.int32, (HALF, 128), 1)
    return row, lane % HALF, (lane // HALF) == (row // 8)


def pack(x):
    lane = lax.broadcasted_iota(jnp.int32, (8, 128), 1)
    low = jnp.where(lane < 32, x[0:8], x[8:16])
    high = jnp.where(lane < 96, x[16:24], x[24:32])
    return jnp.where(lane < 64, low, high)


def side_by_side(x):
    return jnp.concatenate([x[0:8], x[8:16], x[16:24], x[24:32]], axis=1)


def moments_kernel(
    core_ref, pairs_hbm, parent_hbm, block_hbm, coupling_hbm, modes_hbm, weights_hbm,
    record_hbm, own_hbm, other_hbm,
    pairs_ref, parent_ref, block_ref, coupling_ref, modes_ref, weights_ref, record_ref, own_ref, other_ref,
    count_ref, small_sem, coupling_sem, modes_sem, record_sem, result_sem,
):
    small = [
        pltpu.make_async_copy(source, target, small_sem.at[i])
        for i, (source, target) in enumerate(
            (
                (pairs_hbm, pairs_ref),
                (parent_hbm, parent_ref),
                (block_hbm, block_ref),
                (weights_hbm, weights_ref),
            )
        )
    ]
    for copy in small:
        copy.start()
    row = lax.broadcasted_iota(jnp.int32, (HALF, HALF), 0)
    col = lax.broadcasted_iota(jnp.int32, (HALF, HALF), 1)
    lower = row >= col
    diagonal = lax.broadcasted_iota(jnp.int32, (HALF, BLK), 1) == (
        lax.broadcasted_iota(jnp.int32, (HALF, BLK), 0) + HALF
    )
    slots = lax.broadcasted_iota(jnp.int32, (1, 128), 1)
    first = core_ref[0] == 0

    def copies(step):
        part = pl.ds(step * CB, CB)
        return (
            pltpu.make_async_copy(modes_hbm.at[part], modes_ref.at[part], modes_sem.at[step]),
            pltpu.make_async_copy(coupling_hbm.at[part], coupling_ref.at[part], coupling_sem.at[step]),
        )

    def record_copy(step):
        part = pl.ds(step * CB, CB)
        return pltpu.make_async_copy(record_ref.at[part], record_hbm.at[part], record_sem.at[step])

    for step in range(STEPS):
        for copy in copies(step):
            copy.start()
    for p in range(NG * NZ):
        count_ref[p] = 0
    for copy in small:
        copy.wait()

    @pl.loop(0, STEPS)
    def _(step):
        for copy in copies(step):
            copy.wait()
        weights = weights_ref[pl.ds(pl.multiple_of(step * CB, CB), CB), :].astype(F32)
        for pair in range(CB // 2):
            records = []
            for j in (2 * pair, 2 * pair + 1):
                c = step * CB + j
                top = modes_ref[c, pl.ds(pl.multiple_of(pairs_ref[0, c] * BLK, BLK), BLK), :]
                bottom = modes_ref[c, pl.ds(pl.multiple_of(pairs_ref[1, c] * BLK, BLK), BLK), :]
                record = dot(coupling_ref[c], jnp.concatenate([top, bottom], axis=0))
                record = (record * weights[j : j + 1, :]).astype(BF)
                record_ref[c] = record
                records.append(record)
            both = jnp.concatenate(records, axis=0)
            products = dot_nt(both, both)
            for i in range(2):
                c = step * CB + 2 * pair + i
                s = products[i * BLK : (i + 1) * BLK, i * BLK : (i + 1) * BLK]
                cross = side_by_side(s[HALF:, :HALF])
                triangle = side_by_side(jnp.where(lower, s[:HALF, :HALF], s[HALF:, HALF:]))
                own_ref[pl.ds(c, 8, stride=CHILDREN_DEV), :] = jnp.where(first, cross, triangle)
                other_ref[pl.ds(c, 8, stride=CHILDREN_DEV), :] = jnp.where(first, triangle, cross)
                diag = jnp.sum(jnp.where(diagonal, s[HALF:], 0.0), axis=0, keepdims=True)
                zero = jnp.zeros((1, BLK), F32)
                named = zero + (block_ref[c] + 1).astype(F32)
                own_ref[pl.ds(8 * CHILDREN_DEV + c, 1), :] = jnp.concatenate([diag, named], axis=1)
                other_ref[pl.ds(8 * CHILDREN_DEV + c, 1), :] = jnp.concatenate([diag, zero], axis=1)
                p = parent_ref[c]
                k = count_ref[p]
                count_ref[p] = k + 1
                group = (p // (NZ * NX)) * NX + p % NX
                slot = group * SLOTS + ((p // NX) % NZ) * 2 + k
                for h in range(2):
                    hit = jnp.where(slots == slot - 128 * h, 1.0, 0.0)
                    own_ref[pl.ds((9 + h) * CHILDREN_DEV + c, 1), :] = hit
        record_copy(step).start()

    results = (
        pltpu.make_async_copy(other_ref, other_hbm, result_sem.at[0]),
        pltpu.make_async_copy(own_ref, own_hbm, result_sem.at[1]),
    )
    for copy in results:
        copy.start()
    for step in range(STEPS):
        record_copy(step).wait()
    for copy in results:
        copy.wait()


def moments(core, pairs, parent, block, coupling, modes, weights):
    hbm = pl.BlockSpec(memory_space=pltpu.HBM)
    return pl.pallas_call(
        moments_kernel,
        in_specs=[SMEM, hbm, hbm, hbm, hbm, hbm, hbm],
        out_specs=[hbm, hbm, hbm],
        out_shape=[
            jax.ShapeDtypeStruct((CHILDREN_DEV, BLK, 128), BF),
            jax.ShapeDtypeStruct((11 * CHILDREN_DEV, 128), F32),
            jax.ShapeDtypeStruct((9 * CHILDREN_DEV, 128), F32),
        ],
        scratch_shapes=[
            pltpu.SMEM((2, CHILDREN_DEV), jnp.int32),
            pltpu.SMEM((CHILDREN_DEV,), jnp.int32),
            pltpu.SMEM((CHILDREN_DEV,), jnp.int32),
            pltpu.VMEM((CHILDREN_DEV, BLK, 128), BF),
            pltpu.VMEM((CHILDREN_DEV, 256, 128), BF),
            pltpu.VMEM((CHILDREN_DEV, 128), BF),
            pltpu.VMEM((CHILDREN_DEV, BLK, 128), BF),
            pltpu.VMEM((11 * CHILDREN_DEV, 128), F32),
            pltpu.VMEM((9 * CHILDREN_DEV, 128), F32),
            pltpu.SMEM((NG * NZ,), jnp.int32),
            pltpu.SemaphoreType.DMA((4,)),
            pltpu.SemaphoreType.DMA((STEPS,)),
            pltpu.SemaphoreType.DMA((STEPS,)),
            pltpu.SemaphoreType.DMA((STEPS,)),
            pltpu.SemaphoreType.DMA((2,)),
        ],
        compiler_params=params(60),
        name="child_moments",
    )(core, pairs, parent, block, coupling, modes, weights)


def message_row(i, k):
    return k * 8 + i if i < 8 else 16 + k


def every_device(i, k):
    return pl.ds(message_row(i, k), PARENTS, stride=ROWS)


def stage_kernel(own_ref, sums_ref, place_ref, onehot_ref):
    sums_ref[...] = own_ref[: 9 * CHILDREN_DEV, :]
    onehot = jnp.concatenate(
        [own_ref[9 * CHILDREN_DEV : 10 * CHILDREN_DEV, :], own_ref[10 * CHILDREN_DEV :, :]], axis=1
    )
    place_ref[...] = onehot.T.astype(BF)
    onehot_ref[...] = onehot.astype(BF)


def stage(own):
    return pl.pallas_call(
        stage_kernel,
        in_specs=[VMEM],
        out_specs=[VMEM, VMEM, VMEM],
        out_shape=[
            jax.ShapeDtypeStruct((9 * CHILDREN_DEV, 128), F32),
            jax.ShapeDtypeStruct((NG * SLOTS, CHILDREN_DEV), BF),
            jax.ShapeDtypeStruct((CHILDREN_DEV, NG * SLOTS), BF),
        ],
        compiler_params=params(16),
        name="stage",
    )(own)


def dispatch_kernel(place_ref, own_ref, recv_ref, out_ref):
    place = place_ref[...]
    for i in range(9):
        rows = slice(i * CHILDREN_DEV, (i + 1) * CHILDREN_DEV)
        values = (own_ref[rows, :] + recv_ref[rows, :]).astype(BF)
        out_ref[:, i * SLOTS : (i + 1) * SLOTS, :] = dot(place, values).astype(BF).reshape(NG, SLOTS, 128)


def dispatch(place, own, recv):
    return pl.pallas_call(
        dispatch_kernel,
        in_specs=[VMEM, VMEM, VMEM],
        out_specs=VMEM,
        out_shape=jax.ShapeDtypeStruct((NG, ROWS, 128), BF),
        compiler_params=params(16),
        name="dispatch",
    )(place, own, recv)


def bin_kernel(recv_ref, out_ref, onehot_ref):
    count = NG * SLOTS
    meta = recv_ref[:, 8 * SLOTS : ROWS, :].astype(F32).reshape(count, 128)
    slot = lax.broadcasted_iota(jnp.int32, (count, 128), 0) % SLOTS
    lane = lax.broadcasted_iota(jnp.int32, (count, 128), 1)
    meta = pltpu.roll(meta, 64, 1)
    target = meta + (SB * (slot // 2) - 1).astype(F32)
    hit = (lane < 64) & (meta > 0.5) & (target == lane.astype(F32))
    onehot = jnp.where(hit, 1.0, 0.0).astype(BF)
    onehot_ref[...] = onehot
    values = jnp.concatenate(
        [recv_ref[:, i * SLOTS : (i + 1) * SLOTS, :].reshape(count, 128) for i in range(9)], axis=1
    )
    bins = dot_tn(onehot, values)
    zero = jnp.zeros((8, 128), F32)
    for z in range(NZ):
        rows = [bins[8 * z : 8 * z + 8, 128 * i : 128 * (i + 1)] for i in range(9)] + [zero]
        message = jnp.concatenate(rows, axis=0).astype(BF)
        out_ref[2 * z] = message
        out_ref[2 * z + 1] = message


def bin_slots(recv):
    return pl.pallas_call(
        bin_kernel,
        in_specs=[VMEM],
        out_specs=[VMEM, VMEM],
        out_shape=[
            jax.ShapeDtypeStruct((2 * NZ, ZROWS, 128), BF),
            jax.ShapeDtypeStruct((NG * SLOTS, 128), BF),
        ],
        compiler_params=params(16),
        name="bin_slots",
    )(recv)


def wide(x):
    return jnp.concatenate([x, x], axis=1)


def pivot_block(c, j):
    a00, a01, a11 = c[0][j : j + 1], c[1][j : j + 1], c[1][j + 1 : j + 2]
    a02, a12, a22 = c[2][j : j + 1], c[2][j + 1 : j + 2], c[2][j + 2 : j + 3]
    a03, a13, a23 = c[3][j : j + 1], c[3][j + 1 : j + 2], c[3][j + 2 : j + 3]
    a33 = c[3][j + 3 : j + 4]
    scale = 1.0 / (a00 * a11 - a01 * a01)
    p00, p01, p11 = a11 * scale, -a01 * scale, a00 * scale
    t00, t10 = p00 * a02 + p01 * a12, p01 * a02 + p11 * a12
    t01, t11 = p00 * a03 + p01 * a13, p01 * a03 + p11 * a13
    s00 = a22 - (a02 * t00 + a12 * t10)
    s01 = a23 - (a02 * t01 + a12 * t11)
    s11 = a33 - (a03 * t01 + a13 * t11)
    scale = 1.0 / (s00 * s11 - s01 * s01)
    return p00, p01, p11, t00, t10, t01, t11, s11 * scale, -s01 * scale, s00 * scale


def solve_block(block, p):
    p00, p01, p11, t00, t10, t01, t11, q00, q01, q11 = block
    u2 = p[2] - (t00 * p[0] + t10 * p[1])
    u3 = p[3] - (t01 * p[0] + t11 * p[1])
    x2, x3 = q00 * u2 + q01 * u3, q01 * u2 + q11 * u3
    x0 = (p00 * p[0] + p01 * p[1]) - (t00 * x2 + t01 * x3)
    x1 = (p01 * p[0] + p11 * p[1]) - (t10 * x2 + t11 * x3)
    return x0, x1, x2, x3


def eliminate(row, j, rest, c, x):
    rest = rest - ((c[0] * x[0] + c[1] * x[1]) + (c[2] * x[2] + c[3] * x[3]))
    low = jnp.where(row == j, x[0], jnp.where(row == j + 1, x[1], rest))
    return jnp.where(row == j + 2, x[2], jnp.where(row == j + 3, x[3], low))


def invert(a_ref):
    lane = lax.broadcasted_iota(jnp.int32, (PB, MP), 1)
    row = lax.broadcasted_iota(jnp.int32, (PB, MP), 0)
    lane_all = lax.broadcasted_iota(jnp.int32, (MP, MP), 1)
    line = lane[:1]
    for b in range(MP // PB):
        r = b * PB
        panel = a_ref[r : r + PB, :]
        for j8 in range(0, PB, 8):
            c = [jnp.broadcast_to(panel[:, r + j8 + i : r + j8 + i + 1], (PB, 128)) for i in range(8)]
            for h in (0, 4):
                j = j8 + h
                k = r + j
                lead = c[h : h + 4]
                block = pivot_block(lead, j)
                for m in range(h + 4, 8):
                    x = solve_block(block, [c[m][j + i : j + i + 1] for i in range(4)])
                    c[m] = eliminate(row[:, :128], j, c[m], lead, x)
                inside = (line >= k) & (line < k + 4)
                p = [
                    jnp.where(line == k + i, 1.0, jnp.where(inside, 0.0, panel[j + i : j + i + 1]))
                    for i in range(4)
                ]
                x = solve_block([wide(v) for v in block], p)
                rest = jnp.where((lane >= k) & (lane < k + 4), 0.0, panel)
                panel = eliminate(row, j, rest, [wide(v) for v in lead], x)
        ch, cm, cl = split3(a_ref[:, r : r + PB])
        ph, pm, pw = split3(panel)
        update = dot(
            jnp.concatenate([ch, ch, cm, ch, cm, cl], axis=1),
            jnp.concatenate([ph, pm, ph, pw, pm, ph], axis=0),
        )
        a_ref[...] = jnp.where((lane_all // PB) == b, 0.0, a_ref[...]) - update
        a_ref[r : r + PB, :] = panel


def split3(x):
    high = x.astype(BF)
    rest = x - high.astype(F32)
    mid = rest.astype(BF)
    return high, mid, (rest - mid.astype(F32)).astype(BF)


def split(x):
    high = x.astype(BF)
    return high, (x - high.astype(F32)).astype(BF)


def pencil_kernel(
    core_ref, recv_ref, q_ref, eigs_ref, out_ref, a_ref, y_ref, pack_ref, cross_ref, triangle_ref
):
    for half, target in ((0, cross_ref), (1, triangle_ref)):
        parts = [recv_ref[2 * z + half].astype(F32) for z in range(NZ)]
        while len(parts) > 1:
            parts = [x + y for x, y in zip(parts[::2], parts[1::2])]
        target[...] = parts[0]
    row, col, same = tile_index()
    first = core_ref[0] == 0
    lane8 = lax.broadcasted_iota(jnp.int32, (8, 128), 1)
    diags = triangle_ref[64:72, :]
    diags = jnp.where((lane8 >= 32) & (lane8 < 64), diags, 0.0)
    diags = diags + pltpu.roll(diags, 32, 1)
    diags = diags + pltpu.roll(diags, 64, 1)
    zero = jnp.zeros((HALF, 128), F32)
    for b in range(SB):
        cross = jnp.where(same, four(cross_ref[pl.ds(b, 8, stride=8), :]), 0.0)
        triangle = jnp.where(same, four(triangle_ref[pl.ds(b, 8, stride=8), :]), 0.0)
        n11 = jnp.where(row > col, triangle, jnp.where(row == col, 0.5 * triangle, 0.0))
        half = jnp.where(same & (row == col), 0.5 * diags[b : b + 1, :], 0.0)
        n22 = jnp.where(row < col, triangle, half)
        lhs = jnp.concatenate(
            [jnp.concatenate([n11, zero], axis=1), jnp.concatenate([cross, n22], axis=1)], axis=0
        ).astype(BF)
        q1 = q_ref[b * BLK : b * BLK + HALF, :]
        q2 = q_ref[b * BLK + HALF : (b + 1) * BLK, :]
        y_ref[b * BLK : (b + 1) * BLK, :] = dot(lhs, jnp.concatenate([four(q1), four(q2)], axis=0)).astype(BF)
    x = dot_tn(q_ref[...], y_ref[...])
    r = lax.broadcasted_iota(jnp.int32, (MP, MP), 0)
    c = lax.broadcasted_iota(jnp.int32, (MP, MP), 1)
    a_ref[...] = (x + x.T) * (1.0 / 16384.0) + jnp.where(r == c, eigs_ref[...], 0.0)
    invert(a_ref)
    high, low = split(a_ref[...] * (1.0 / MP))
    q = q_ref[...]
    y_high, y_low = split(dot(q, high) + dot(q, low))
    for b in range(SB):
        s = b * BLK
        qb = q_ref[s : s + BLK, :]
        u = dot_nt(qb, four(y_high[s : s + HALF])) + dot_nt(qb, four(y_low[s : s + HALF]))
        v = dot_nt(qb[HALF:], four(y_high[s + HALF : s + BLK])) + dot_nt(
            qb[HALF:], four(y_low[s + HALF : s + BLK])
        )
        cross = pack(2.0 * u[HALF:])
        triangle = pack(
            jnp.where(row > col, 2.0 * u[:HALF], jnp.where(row == col, u[:HALF], 2.0 * v))
        )
        pack_ref[pl.ds(b, 8, stride=8), :] = jnp.where(first, cross, triangle)
        pack_ref[64 + b : 65 + b, :] = jnp.sum(jnp.where(row == col, v, 0.0), axis=0, keepdims=True)
    pack_ref[72:80, :] = jnp.zeros((8, 128), F32)
    result = pack_ref[...].astype(BF)
    for z in range(NZ):
        out_ref[z] = result


def pencil_blocks(core, recv, q, eigs):
    return pl.pallas_call(
        pencil_kernel,
        in_specs=[SMEM, VMEM, VMEM, VMEM],
        out_specs=VMEM,
        out_shape=jax.ShapeDtypeStruct((NZ, ZROWS, 128), BF),
        scratch_shapes=[
            pltpu.VMEM((MP, MP), F32),
            pltpu.VMEM((SB * BLK, MP), BF),
            pltpu.VMEM((ZROWS, 128), F32),
            pltpu.VMEM((ZROWS, 128), F32),
            pltpu.VMEM((ZROWS, 128), F32),
        ],
        compiler_params=params(16),
        name="pencil_blocks",
    )(core, recv, q, eigs)


def select_kernel(bins_ref, onehot_ref, out_ref):
    onehot = onehot_ref[:, 0:64]
    bins = [bins_ref[z].astype(F32) for z in range(NZ)]
    for i in range(9):
        values = jnp.concatenate([x[8 * i : 8 * i + 8] for x in bins], axis=0).astype(BF)
        picked = dot(onehot, values).astype(BF)
        out_ref[:, i * SLOTS : (i + 1) * SLOTS, :] = picked.reshape(NG, SLOTS, 128)


def select_bins(bins, onehot):
    return pl.pallas_call(
        select_kernel,
        in_specs=[VMEM, VMEM],
        out_specs=VMEM,
        out_shape=jax.ShapeDtypeStruct((NG, ROWS, 128), BF),
        compiler_params=params(16),
        name="select_bins",
    )(bins, onehot)


def collect_kernel(onehot_ref, recv_ref, out_ref):
    onehot = onehot_ref[...]
    for i in range(9):
        values = recv_ref[:, i * SLOTS : (i + 1) * SLOTS, :].reshape(NG * SLOTS, 128)
        out_ref[i * CHILDREN_DEV : (i + 1) * CHILDREN_DEV, :] = dot(onehot, values).astype(BF)


def collect(onehot, recv):
    return pl.pallas_call(
        collect_kernel,
        in_specs=[VMEM, VMEM],
        out_specs=VMEM,
        out_shape=jax.ShapeDtypeStruct((9 * CHILDREN_DEV, 128), BF),
        compiler_params=params(16),
        name="collect",
    )(onehot, recv)


def strength_kernel(core_ref, mine_ref, theirs_ref, record_ref, out_ref, own_ref, other_ref):
    step = pl.program_id(0)

    @pl.when(step == 0)
    def _():
        own_ref[...] = mine_ref[...].astype(F32)
        other_ref[...] = theirs_ref[...].astype(F32)

    row, col, same = tile_index()
    first = core_ref[0] == 0
    lower = same & (row >= col)
    upper = same & (row < col)
    diagonal = same & (row == col)
    zero = jnp.zeros((HALF, 128), F32)
    for j in range(CB):
        c = step * CB + j
        own = own_ref[pl.ds(c, 8, stride=CHILDREN_DEV), :]
        other = other_ref[pl.ds(c, 8, stride=CHILDREN_DEV), :]
        r = pl.ds(8 * CHILDREN_DEV + c, 1)
        diag = jnp.where(first, other_ref[r, :], own_ref[r, :])
        cross = jnp.where(same, four(jnp.where(first, own, other)), 0.0)
        triangle = four(jnp.where(first, other, own))
        m11 = jnp.where(lower, triangle, 0.0)
        m22 = jnp.where(upper, triangle, jnp.where(diagonal, diag, 0.0))
        lhs = jnp.concatenate(
            [jnp.concatenate([m11, zero], axis=1), jnp.concatenate([cross, m22], axis=1)], axis=0
        ).astype(BF)
        record = record_ref[j]
        rhs = jnp.concatenate([four(record[:HALF]), four(record[HALF:])], axis=0)
        rotated = dot(lhs, rhs)
        out_ref[j : j + 1, :] = jnp.sum(rotated * record.astype(F32), axis=0, keepdims=True)


def strengths(core, own, other, record):
    whole = (9 * CHILDREN_DEV, 128)
    return pl.pallas_call(
        strength_kernel,
        grid=(STEPS,),
        in_specs=[
            SMEM,
            pl.BlockSpec(whole, lambda i: (0, 0)),
            pl.BlockSpec(whole, lambda i: (0, 0)),
            pl.BlockSpec((CB, BLK, 128), lambda i: (i, 0, 0)),
        ],
        out_specs=pl.BlockSpec((CB, 128), lambda i: (i, 0)),
        out_shape=jax.ShapeDtypeStruct((CHILDREN_DEV, 128), F32),
        scratch_shapes=[pltpu.VMEM(whole, F32), pltpu.VMEM(whole, F32)],
        compiler_params=params(16),
        name="strengths",
    )(core, own, other, record)


def swap(x):
    return lax.ppermute(x, "mode", [(0, 1), (1, 0)])


def exchange(x, axes):
    return lax.all_to_all(x, axes, split_axis=0, concat_axis=0, tiled=True)


def per_device(coupling, pairs, modes, weights, parent_of, row_block, parent_modes, parent_eigs):
    core = lax.axis_index("mode").astype(jnp.int32).reshape(1)
    parent = parent_of.reshape(CHILDREN_DEV)
    record, own, other = moments(core, pairs.T, parent, row_block, coupling, modes, weights)
    sums, place, onehot = stage(own)
    sent = dispatch(place, sums, swap(other))
    binned, chosen = bin_slots(exchange(sent, ("y", "x")))
    bins = exchange(binned, ("z", "mode"))
    blocks = pencil_blocks(core, bins, parent_modes[0], parent_eigs)
    picked = select_bins(exchange(blocks, "z"), chosen)
    mine = collect(onehot, exchange(picked, ("y", "x")))
    return strengths(core, mine, swap(mine), record)


def solution(mesh):
    grid = Mesh(mesh.devices.reshape(NY, NZ, NX, 2), ("y", "z", "x", "mode"))
    sub = ("y", "z", "x")
    in_specs = (
        P(sub, None, None),
        P(sub, None),
        P(sub, None, "mode"),
        P(sub, "mode"),
        P(sub, None),
        P(sub),
        P(sub, None, None),
        P(sub, None),
    )
    return jax.shard_map(
        per_device, mesh=grid, in_specs=in_specs, out_specs=P(sub, "mode"), check_vma=False
    )
```

```python
import jax
import jax.numpy as jnp
from jax import lax
from jax.experimental import pallas as pl
from jax.experimental.pallas import tpu as pltpu
from jax.sharding import Mesh, PartitionSpec as P

MP = 256
BLK = 64
HALF = 32
SB = 8
CHILDREN_DEV = 64
CB = 32
STEPS = CHILDREN_DEV // CB
NY, NZ, NX = 4, 8, 4
NG = NY * NX
SLOTS = 2 * NZ
ROWS = 9 * SLOTS
ZROWS = 80
PB = 64
BF = jnp.bfloat16
F32 = jnp.float32
VMEM = pl.BlockSpec(memory_space=pltpu.VMEM)
SMEM = pl.BlockSpec(memory_space=pltpu.SMEM)


def params(mib, **more):
    return pltpu.CompilerParams(vmem_limit_bytes=mib * 1024 * 1024, **more)


def dot(a, b):
    return jnp.dot(a, b, preferred_element_type=F32)


def dot_nt(a, b):
    return lax.dot_general(a, b, (((1,), (1,)), ((), ())), preferred_element_type=F32)


def dot_tn(a, b):
    return lax.dot_general(a, b, (((0,), (0,)), ((), ())), preferred_element_type=F32)


def four(x):
    return jnp.concatenate([x, x, x, x], axis=0)


def tile_index():
    row = lax.broadcasted_iota(jnp.int32, (HALF, 128), 0)
    lane = lax.broadcasted_iota(jnp.int32, (HALF, 128), 1)
    return row, lane % HALF, (lane // HALF) == (row // 8)


def pack(x):
    lane = lax.broadcasted_iota(jnp.int32, (8, 128), 1)
    low = jnp.where(lane < 32, x[0:8], x[8:16])
    high = jnp.where(lane < 96, x[16:24], x[24:32])
    return jnp.where(lane < 64, low, high)


def side_by_side(x):
    return jnp.concatenate([x[0:8], x[8:16], x[16:24], x[24:32]], axis=1)


def moments_kernel(
    core_ref, pairs_hbm, parent_hbm, block_hbm, coupling_hbm, modes_hbm, weights_hbm,
    record_hbm, own_hbm, other_hbm,
    pairs_ref, parent_ref, block_ref, coupling_ref, modes_ref, weights_ref, record_ref, own_ref, other_ref,
    count_ref, small_sem, coupling_sem, modes_sem, record_sem, result_sem,
):
    small = [
        pltpu.make_async_copy(source, target, small_sem.at[i])
        for i, (source, target) in enumerate(
            (
                (pairs_hbm, pairs_ref),
                (parent_hbm, parent_ref),
                (block_hbm, block_ref),
                (weights_hbm, weights_ref),
            )
        )
    ]
    for copy in small:
        copy.start()
    row = lax.broadcasted_iota(jnp.int32, (HALF, HALF), 0)
    col = lax.broadcasted_iota(jnp.int32, (HALF, HALF), 1)
    lower = row >= col
    diagonal = lax.broadcasted_iota(jnp.int32, (HALF, BLK), 1) == (
        lax.broadcasted_iota(jnp.int32, (HALF, BLK), 0) + HALF
    )
    slots = lax.broadcasted_iota(jnp.int32, (1, 128), 1)
    first = core_ref[0] == 0

    def copies(step):
        part = pl.ds(step * CB, CB)
        return (
            pltpu.make_async_copy(modes_hbm.at[part], modes_ref.at[part], modes_sem.at[step]),
            pltpu.make_async_copy(coupling_hbm.at[part], coupling_ref.at[part], coupling_sem.at[step]),
        )

    def record_copy(step):
        part = pl.ds(step * CB, CB)
        return pltpu.make_async_copy(record_ref.at[part], record_hbm.at[part], record_sem.at[step])

    for step in range(STEPS):
        for copy in copies(step):
            copy.start()
    for p in range(NG * NZ):
        count_ref[p] = 0
    for copy in small:
        copy.wait()

    @pl.loop(0, STEPS)
    def _(step):
        for copy in copies(step):
            copy.wait()
        weights = weights_ref[pl.ds(pl.multiple_of(step * CB, CB), CB), :].astype(F32)
        for pair in range(CB // 2):
            records = []
            for j in (2 * pair, 2 * pair + 1):
                c = step * CB + j
                top = modes_ref[c, pl.ds(pl.multiple_of(pairs_ref[0, c] * BLK, BLK), BLK), :]
                bottom = modes_ref[c, pl.ds(pl.multiple_of(pairs_ref[1, c] * BLK, BLK), BLK), :]
                record = dot(coupling_ref[c], jnp.concatenate([top, bottom], axis=0))
                record = (record * weights[j : j + 1, :]).astype(BF)
                record_ref[c] = record
                records.append(record)
            both = jnp.concatenate(records, axis=0)
            products = dot_nt(both, both)
            for i in range(2):
                c = step * CB + 2 * pair + i
                s = products[i * BLK : (i + 1) * BLK, i * BLK : (i + 1) * BLK]
                cross = side_by_side(s[HALF:, :HALF])
                triangle = side_by_side(jnp.where(lower, s[:HALF, :HALF], s[HALF:, HALF:]))
                own_ref[pl.ds(c, 8, stride=CHILDREN_DEV), :] = jnp.where(first, cross, triangle)
                other_ref[pl.ds(c, 8, stride=CHILDREN_DEV), :] = jnp.where(first, triangle, cross)
                diag = jnp.sum(jnp.where(diagonal, s[HALF:], 0.0), axis=0, keepdims=True)
                zero = jnp.zeros((1, BLK), F32)
                named = zero + (block_ref[c] + 1).astype(F32)
                own_ref[pl.ds(8 * CHILDREN_DEV + c, 1), :] = jnp.concatenate([diag, named], axis=1)
                other_ref[pl.ds(8 * CHILDREN_DEV + c, 1), :] = jnp.concatenate([diag, zero], axis=1)
                p = parent_ref[c]
                k = count_ref[p]
                count_ref[p] = k + 1
                group = (p // (NZ * NX)) * NX + p % NX
                slot = group * SLOTS + ((p // NX) % NZ) * 2 + k
                for h in range(2):
                    hit = jnp.where(slots == slot - 128 * h, 1.0, 0.0)
                    own_ref[pl.ds((9 + h) * CHILDREN_DEV + c, 1), :] = hit
        record_copy(step).start()

    results = (
        pltpu.make_async_copy(other_ref, other_hbm, result_sem.at[0]),
        pltpu.make_async_copy(own_ref, own_hbm, result_sem.at[1]),
    )
    for copy in results:
        copy.start()
    for step in range(STEPS):
        record_copy(step).wait()
    for copy in results:
        copy.wait()


def moments(core, pairs, parent, block, coupling, modes, weights):
    hbm = pl.BlockSpec(memory_space=pltpu.HBM)
    return pl.pallas_call(
        moments_kernel,
        in_specs=[SMEM, hbm, hbm, hbm, hbm, hbm, hbm],
        out_specs=[hbm, hbm, hbm],
        out_shape=[
            jax.ShapeDtypeStruct((CHILDREN_DEV, BLK, 128), BF),
            jax.ShapeDtypeStruct((11 * CHILDREN_DEV, 128), F32),
            jax.ShapeDtypeStruct((9 * CHILDREN_DEV, 128), F32),
        ],
        scratch_shapes=[
            pltpu.SMEM((2, CHILDREN_DEV), jnp.int32),
            pltpu.SMEM((CHILDREN_DEV,), jnp.int32),
            pltpu.SMEM((CHILDREN_DEV,), jnp.int32),
            pltpu.VMEM((CHILDREN_DEV, BLK, 128), BF),
            pltpu.VMEM((CHILDREN_DEV, 256, 128), BF),
            pltpu.VMEM((CHILDREN_DEV, 128), BF),
            pltpu.VMEM((CHILDREN_DEV, BLK, 128), BF),
            pltpu.VMEM((11 * CHILDREN_DEV, 128), F32),
            pltpu.VMEM((9 * CHILDREN_DEV, 128), F32),
            pltpu.SMEM((NG * NZ,), jnp.int32),
            pltpu.SemaphoreType.DMA((4,)),
            pltpu.SemaphoreType.DMA((STEPS,)),
            pltpu.SemaphoreType.DMA((STEPS,)),
            pltpu.SemaphoreType.DMA((STEPS,)),
            pltpu.SemaphoreType.DMA((2,)),
        ],
        compiler_params=params(60),
        name="child_moments",
    )(core, pairs, parent, block, coupling, modes, weights)


def message_row(i, k):
    return k * 8 + i if i < 8 else 16 + k


def every_device(i, k):
    return pl.ds(message_row(i, k), PARENTS, stride=ROWS)


def stage_kernel(own_ref, sums_ref, place_ref, onehot_ref):
    sums_ref[...] = own_ref[: 9 * CHILDREN_DEV, :]
    onehot = jnp.concatenate(
        [own_ref[9 * CHILDREN_DEV : 10 * CHILDREN_DEV, :], own_ref[10 * CHILDREN_DEV :, :]], axis=1
    )
    place_ref[...] = onehot.T.astype(BF)
    onehot_ref[...] = onehot.astype(BF)


def stage(own):
    return pl.pallas_call(
        stage_kernel,
        in_specs=[VMEM],
        out_specs=[VMEM, VMEM, VMEM],
        out_shape=[
            jax.ShapeDtypeStruct((9 * CHILDREN_DEV, 128), F32),
            jax.ShapeDtypeStruct((NG * SLOTS, CHILDREN_DEV), BF),
            jax.ShapeDtypeStruct((CHILDREN_DEV, NG * SLOTS), BF),
        ],
        compiler_params=params(16),
        name="stage",
    )(own)


def dispatch_kernel(place_ref, own_ref, recv_ref, out_ref):
    place = place_ref[...]
    for i in range(9):
        rows = slice(i * CHILDREN_DEV, (i + 1) * CHILDREN_DEV)
        values = (own_ref[rows, :] + recv_ref[rows, :]).astype(BF)
        out_ref[:, i * SLOTS : (i + 1) * SLOTS, :] = dot(place, values).astype(BF).reshape(NG, SLOTS, 128)


def dispatch(place, own, recv):
    return pl.pallas_call(
        dispatch_kernel,
        in_specs=[VMEM, VMEM, VMEM],
        out_specs=VMEM,
        out_shape=jax.ShapeDtypeStruct((NG, ROWS, 128), BF),
        compiler_params=params(16),
        name="dispatch",
    )(place, own, recv)


def bin_kernel(recv_ref, out_ref, onehot_ref):
    count = NG * SLOTS
    meta = recv_ref[:, 8 * SLOTS : ROWS, :].astype(F32).reshape(count, 128)
    slot = lax.broadcasted_iota(jnp.int32, (count, 128), 0) % SLOTS
    lane = lax.broadcasted_iota(jnp.int32, (count, 128), 1)
    meta = pltpu.roll(meta, 64, 1)
    target = meta + (SB * (slot // 2) - 1).astype(F32)
    hit = (lane < 64) & (meta > 0.5) & (target == lane.astype(F32))
    onehot = jnp.where(hit, 1.0, 0.0).astype(BF)
    onehot_ref[...] = onehot
    values = jnp.concatenate(
        [recv_ref[:, i * SLOTS : (i + 1) * SLOTS, :].reshape(count, 128) for i in range(9)], axis=1
    )
    bins = dot_tn(onehot, values)
    zero = jnp.zeros((8, 128), F32)
    for z in range(NZ):
        rows = [bins[8 * z : 8 * z + 8, 128 * i : 128 * (i + 1)] for i in range(9)] + [zero]
        out_ref[z] = jnp.concatenate(rows, axis=0).astype(BF)


def bin_slots(recv):
    return pl.pallas_call(
        bin_kernel,
        in_specs=[VMEM],
        out_specs=[VMEM, VMEM],
        out_shape=[
            jax.ShapeDtypeStruct((NZ, ZROWS, 128), BF),
            jax.ShapeDtypeStruct((NG * SLOTS, 128), BF),
        ],
        compiler_params=params(16),
        name="bin_slots",
    )(recv)


def wide(x):
    return jnp.concatenate([x, x], axis=1)


def pivot_block(c, row, j):
    a00, a01, a11 = c[0][j : j + 1], c[1][j : j + 1], c[1][j + 1 : j + 2]
    a02, a12, a22 = c[2][j : j + 1], c[2][j + 1 : j + 2], c[2][j + 2 : j + 3]
    a03, a13, a23 = c[3][j : j + 1], c[3][j + 1 : j + 2], c[3][j + 2 : j + 3]
    a33 = c[3][j + 3 : j + 4]
    scale = 1.0 / (a00 * a11 - a01 * a01)
    p00, p01, p11 = a11 * scale, -a01 * scale, a00 * scale
    t00, t10 = p00 * a02 + p01 * a12, p01 * a02 + p11 * a12
    t01, t11 = p00 * a03 + p01 * a13, p01 * a03 + p11 * a13
    s00 = a22 - (a02 * t00 + a12 * t10)
    s01 = a23 - (a02 * t01 + a12 * t11)
    s11 = a33 - (a03 * t01 + a13 * t11)
    scale = 1.0 / (s00 * s11 - s01 * s01)
    inside = (row >= j) & (row < j + 4)
    m = [jnp.where(row == j + i, -1.0, jnp.where(inside, 0.0, c[i])) for i in range(4)]
    m[2] = m[2] - (m[0] * t00 + m[1] * t10)
    m[3] = m[3] - (m[0] * t01 + m[1] * t11)
    return (p00, p01, p11), (t00, t10, t01, t11), (s11 * scale, -s01 * scale, s00 * scale), m


def eliminate(rest, block, p, spread):
    (p00, p01, p11), (t00, t10, t01, t11), (q00, q01, q11), m = (
        [spread(v) for v in part] for part in block
    )
    y0, y1 = p00 * p[0] + p01 * p[1], p01 * p[0] + p11 * p[1]
    u2 = p[2] - (t00 * p[0] + t10 * p[1])
    u3 = p[3] - (t01 * p[0] + t11 * p[1])
    rest = rest - (m[0] * y0 + m[1] * y1)
    x2, x3 = q00 * u2 + q01 * u3, q01 * u2 + q11 * u3
    return (rest - m[2] * x2) - m[3] * x3


def invert(a_ref):
    lane = lax.broadcasted_iota(jnp.int32, (PB, MP), 1)
    row = lax.broadcasted_iota(jnp.int32, (PB, MP), 0)
    row_half = row[:, :128]
    lane_all = lax.broadcasted_iota(jnp.int32, (MP, MP), 1)
    line = lane[:1]
    for b in range(MP // PB):
        r = b * PB
        panel = a_ref[r : r + PB, :]
        for j8 in range(0, PB, 8):
            c = [jnp.broadcast_to(panel[:, r + j8 + i : r + j8 + i + 1], (PB, 128)) for i in range(8)]
            for h in (0, 4):
                j = j8 + h
                k = r + j
                block = pivot_block(c[h : h + 4], row_half, j)
                for m in range(h + 4, 8):
                    rest = jnp.where((row_half >= j) & (row_half < j + 4), 0.0, c[m])
                    c[m] = eliminate(rest, block, [c[m][j + i : j + i + 1] for i in range(4)], lambda v: v)
                inside = (line >= k) & (line < k + 4)
                p = [
                    jnp.where(line == k + i, 1.0, jnp.where(inside, 0.0, panel[j + i : j + i + 1]))
                    for i in range(4)
                ]
                cleared = ((lane >= k) & (lane < k + 4)) | ((row >= j) & (row < j + 4))
                panel = eliminate(jnp.where(cleared, 0.0, panel), block, p, wide)
        ch, cm, cl = split3(a_ref[:, r : r + PB])
        ph, pm, pw = split3(panel)
        update = dot(
            jnp.concatenate([ch, ch, cm, ch, cm, cl], axis=1),
            jnp.concatenate([ph, pm, ph, pw, pm, ph], axis=0),
        )
        a_ref[...] = jnp.where((lane_all // PB) == b, 0.0, a_ref[...]) - update
        a_ref[r : r + PB, :] = panel


def split3(x):
    high = x.astype(BF)
    rest = x - high.astype(F32)
    mid = rest.astype(BF)
    return high, mid, (rest - mid.astype(F32)).astype(BF)


def split(x):
    high = x.astype(BF)
    return high, (x - high.astype(F32)).astype(BF)


def pencil_kernel(
    core_ref, mine_ref, theirs_ref, q_ref, eigs_ref, out_ref, a_ref, y_ref, pack_ref, own_ref, other_ref
):
    for source, target in ((mine_ref, own_ref), (theirs_ref, other_ref)):
        parts = [source[z].astype(F32) for z in range(NZ)]
        while len(parts) > 1:
            parts = [x + y for x, y in zip(parts[::2], parts[1::2])]
        target[...] = parts[0]
    row, col, same = tile_index()
    first = core_ref[0] == 0
    lane8 = lax.broadcasted_iota(jnp.int32, (8, 128), 1)
    diags = jnp.where(first, other_ref[64:72, :], own_ref[64:72, :])
    diags = jnp.where((lane8 >= 32) & (lane8 < 64), diags, 0.0)
    diags = diags + pltpu.roll(diags, 32, 1)
    diags = diags + pltpu.roll(diags, 64, 1)
    zero = jnp.zeros((HALF, 128), F32)
    for b in range(SB):
        own = own_ref[pl.ds(b, 8, stride=8), :]
        other = other_ref[pl.ds(b, 8, stride=8), :]
        cross = jnp.where(same, four(jnp.where(first, own, other)), 0.0)
        triangle = jnp.where(same, four(jnp.where(first, other, own)), 0.0)
        n11 = jnp.where(row > col, triangle, jnp.where(row == col, 0.5 * triangle, 0.0))
        half = jnp.where(same & (row == col), 0.5 * diags[b : b + 1, :], 0.0)
        n22 = jnp.where(row < col, triangle, half)
        lhs = jnp.concatenate(
            [jnp.concatenate([n11, zero], axis=1), jnp.concatenate([cross, n22], axis=1)], axis=0
        ).astype(BF)
        q1 = q_ref[b * BLK : b * BLK + HALF, :]
        q2 = q_ref[b * BLK + HALF : (b + 1) * BLK, :]
        y_ref[b * BLK : (b + 1) * BLK, :] = dot(lhs, jnp.concatenate([four(q1), four(q2)], axis=0)).astype(BF)
    x = dot_tn(q_ref[...], y_ref[...])
    r = lax.broadcasted_iota(jnp.int32, (MP, MP), 0)
    c = lax.broadcasted_iota(jnp.int32, (MP, MP), 1)
    a_ref[...] = (x + x.T) * (1.0 / 16384.0) + jnp.where(r == c, eigs_ref[...], 0.0)
    invert(a_ref)
    high, low = split(a_ref[...] * (1.0 / MP))
    q = q_ref[...]
    y_high, y_low = split(dot(q, high) + dot(q, low))
    for b in range(SB):
        s = b * BLK
        qb = q_ref[s : s + BLK, :]
        u = dot_nt(qb, four(y_high[s : s + HALF])) + dot_nt(qb, four(y_low[s : s + HALF]))
        v = dot_nt(qb[HALF:], four(y_high[s + HALF : s + BLK])) + dot_nt(
            qb[HALF:], four(y_low[s + HALF : s + BLK])
        )
        cross = pack(2.0 * u[HALF:])
        triangle = pack(
            jnp.where(row > col, 2.0 * u[:HALF], jnp.where(row == col, u[:HALF], 2.0 * v))
        )
        pack_ref[pl.ds(b, 8, stride=8), :] = jnp.where(first, cross, triangle)
        pack_ref[64 + b : 65 + b, :] = jnp.sum(jnp.where(row == col, v, 0.0), axis=0, keepdims=True)
    pack_ref[72:80, :] = jnp.zeros((8, 128), F32)
    result = pack_ref[...].astype(BF)
    for z in range(NZ):
        out_ref[z] = result


def pencil_blocks(core, own, other, q, eigs):
    return pl.pallas_call(
        pencil_kernel,
        in_specs=[SMEM, VMEM, VMEM, VMEM, VMEM],
        out_specs=VMEM,
        out_shape=jax.ShapeDtypeStruct((NZ, ZROWS, 128), BF),
        scratch_shapes=[
            pltpu.VMEM((MP, MP), F32),
            pltpu.VMEM((SB * BLK, MP), BF),
            pltpu.VMEM((ZROWS, 128), F32),
            pltpu.VMEM((ZROWS, 128), F32),
            pltpu.VMEM((ZROWS, 128), F32),
        ],
        compiler_params=params(16),
        name="pencil_blocks",
    )(core, own, other, q, eigs)


def select_kernel(bins_ref, onehot_ref, out_ref):
    onehot = onehot_ref[:, 0:64]
    bins = [bins_ref[z].astype(F32) for z in range(NZ)]
    for i in range(9):
        values = jnp.concatenate([x[8 * i : 8 * i + 8] for x in bins], axis=0).astype(BF)
        picked = dot(onehot, values).astype(BF)
        out_ref[:, i * SLOTS : (i + 1) * SLOTS, :] = picked.reshape(NG, SLOTS, 128)


def select_bins(bins, onehot):
    return pl.pallas_call(
        select_kernel,
        in_specs=[VMEM, VMEM],
        out_specs=VMEM,
        out_shape=jax.ShapeDtypeStruct((NG, ROWS, 128), BF),
        compiler_params=params(16),
        name="select_bins",
    )(bins, onehot)


def collect_kernel(onehot_ref, recv_ref, out_ref):
    onehot = onehot_ref[...]
    for i in range(9):
        values = recv_ref[:, i * SLOTS : (i + 1) * SLOTS, :].reshape(NG * SLOTS, 128)
        out_ref[i * CHILDREN_DEV : (i + 1) * CHILDREN_DEV, :] = dot(onehot, values).astype(BF)


def collect(onehot, recv):
    return pl.pallas_call(
        collect_kernel,
        in_specs=[VMEM, VMEM],
        out_specs=VMEM,
        out_shape=jax.ShapeDtypeStruct((9 * CHILDREN_DEV, 128), BF),
        compiler_params=params(16),
        name="collect",
    )(onehot, recv)


def strength_kernel(core_ref, mine_ref, theirs_ref, record_ref, out_ref, own_ref, other_ref):
    step = pl.program_id(0)

    @pl.when(step == 0)
    def _():
        own_ref[...] = mine_ref[...].astype(F32)
        other_ref[...] = theirs_ref[...].astype(F32)

    row, col, same = tile_index()
    first = core_ref[0] == 0
    lower = same & (row >= col)
    upper = same & (row < col)
    diagonal = same & (row == col)
    zero = jnp.zeros((HALF, 128), F32)
    for j in range(CB):
        c = step * CB + j
        own = own_ref[pl.ds(c, 8, stride=CHILDREN_DEV), :]
        other = other_ref[pl.ds(c, 8, stride=CHILDREN_DEV), :]
        r = pl.ds(8 * CHILDREN_DEV + c, 1)
        diag = jnp.where(first, other_ref[r, :], own_ref[r, :])
        cross = jnp.where(same, four(jnp.where(first, own, other)), 0.0)
        triangle = four(jnp.where(first, other, own))
        m11 = jnp.where(lower, triangle, 0.0)
        m22 = jnp.where(upper, triangle, jnp.where(diagonal, diag, 0.0))
        lhs = jnp.concatenate(
            [jnp.concatenate([m11, zero], axis=1), jnp.concatenate([cross, m22], axis=1)], axis=0
        ).astype(BF)
        record = record_ref[j]
        rhs = jnp.concatenate([four(record[:HALF]), four(record[HALF:])], axis=0)
        rotated = dot(lhs, rhs)
        out_ref[j : j + 1, :] = jnp.sum(rotated * record.astype(F32), axis=0, keepdims=True)


def strengths(core, own, other, record):
    whole = (9 * CHILDREN_DEV, 128)
    return pl.pallas_call(
        strength_kernel,
        grid=(STEPS,),
        in_specs=[
            SMEM,
            pl.BlockSpec(whole, lambda i: (0, 0)),
            pl.BlockSpec(whole, lambda i: (0, 0)),
            pl.BlockSpec((CB, BLK, 128), lambda i: (i, 0, 0)),
        ],
        out_specs=pl.BlockSpec((CB, 128), lambda i: (i, 0)),
        out_shape=jax.ShapeDtypeStruct((CHILDREN_DEV, 128), F32),
        scratch_shapes=[pltpu.VMEM(whole, F32), pltpu.VMEM(whole, F32)],
        compiler_params=params(16),
        name="strengths",
    )(core, own, other, record)


def swap(x):
    return lax.ppermute(x, "mode", [(0, 1), (1, 0)])


def exchange(x, axes):
    return lax.all_to_all(x, axes, split_axis=0, concat_axis=0, tiled=True)


def per_device(coupling, pairs, modes, weights, parent_of, row_block, parent_modes, parent_eigs):
    core = lax.axis_index("mode").astype(jnp.int32).reshape(1)
    parent = parent_of.reshape(CHILDREN_DEV)
    record, own, other = moments(core, pairs.T, parent, row_block, coupling, modes, weights)
    sums, place, onehot = stage(own)
    sent = dispatch(place, sums, swap(other))
    binned, chosen = bin_slots(exchange(sent, ("y", "x")))
    bins = exchange(binned, "z")
    blocks = pencil_blocks(core, bins, swap(bins), parent_modes[0], parent_eigs)
    picked = select_bins(exchange(blocks, "z"), chosen)
    mine = collect(onehot, exchange(picked, ("y", "x")))
    return strengths(core, mine, swap(mine), record)


def solution(mesh):
    grid = Mesh(mesh.devices.reshape(NY, NZ, NX, 2), ("y", "z", "x", "mode"))
    sub = ("y", "z", "x")
    in_specs = (
        P(sub, None, None),
        P(sub, None),
        P(sub, None, "mode"),
        P(sub, "mode"),
        P(sub, None),
        P(sub),
        P(sub, None, None),
        P(sub, None),
    )
    return jax.shard_map(
        per_device, mesh=grid, in_specs=in_specs, out_specs=P(sub, "mode"), check_vma=False
    )
```

```python
import jax
import jax.numpy as jnp
from jax import lax
from jax.experimental import pallas as pl
from jax.experimental.pallas import tpu as pltpu
from jax.sharding import Mesh, PartitionSpec as P

MP = 256
BLK = 64
HALF = 32
SB = 8
CHILDREN_DEV = 64
CB = 32
STEPS = CHILDREN_DEV // CB
NY, NZ, NX = 4, 8, 4
NG = NY * NX
SLOTS = 2 * NZ
ROWS = 9 * SLOTS
ZROWS = 80
PB = 32
BF = jnp.bfloat16
F32 = jnp.float32
VMEM = pl.BlockSpec(memory_space=pltpu.VMEM)
SMEM = pl.BlockSpec(memory_space=pltpu.SMEM)


def params(mib, **more):
    return pltpu.CompilerParams(vmem_limit_bytes=mib * 1024 * 1024, **more)


def dot(a, b):
    return jnp.dot(a, b, preferred_element_type=F32)


def dot_nt(a, b):
    return lax.dot_general(a, b, (((1,), (1,)), ((), ())), preferred_element_type=F32)


def dot_tn(a, b):
    return lax.dot_general(a, b, (((0,), (0,)), ((), ())), preferred_element_type=F32)


def square_index():
    return (
        lax.broadcasted_iota(jnp.int32, (HALF, HALF), 0),
        lax.broadcasted_iota(jnp.int32, (HALF, HALF), 1),
    )


def stacked(x):
    return jnp.concatenate([x[:, 0:32], x[:, 32:64], x[:, 64:96], x[:, 96:128]], axis=0)


def side_by_side(x):
    return jnp.concatenate([x[0:8], x[8:16], x[16:24], x[24:32]], axis=1)


def moments_kernel(
    core_ref, pairs_hbm, parent_hbm, block_hbm, coupling_hbm, modes_hbm, weights_hbm,
    record_hbm, own_hbm, other_hbm,
    pairs_ref, parent_ref, block_ref, coupling_ref, modes_ref, weights_ref, record_ref, own_ref, other_ref,
    count_ref, small_sem, coupling_sem, modes_sem, record_sem, result_sem,
):
    small = [
        pltpu.make_async_copy(source, target, small_sem.at[i])
        for i, (source, target) in enumerate(
            (
                (pairs_hbm, pairs_ref),
                (parent_hbm, parent_ref),
                (block_hbm, block_ref),
                (weights_hbm, weights_ref),
            )
        )
    ]
    for copy in small:
        copy.start()
    row, col = square_index()
    lower = row >= col
    diagonal = lax.broadcasted_iota(jnp.int32, (HALF, BLK), 1) == (
        lax.broadcasted_iota(jnp.int32, (HALF, BLK), 0) + HALF
    )
    slots = lax.broadcasted_iota(jnp.int32, (1, 128), 1)
    first = core_ref[0] == 0

    def copies(step):
        part = pl.ds(step * CB, CB)
        return (
            pltpu.make_async_copy(modes_hbm.at[part], modes_ref.at[part], modes_sem.at[step]),
            pltpu.make_async_copy(coupling_hbm.at[part], coupling_ref.at[part], coupling_sem.at[step]),
        )

    def record_copy(step):
        part = pl.ds(step * CB, CB)
        return pltpu.make_async_copy(record_ref.at[part], record_hbm.at[part], record_sem.at[step])

    for step in range(STEPS):
        for copy in copies(step):
            copy.start()
    for p in range(NG * NZ):
        count_ref[p] = 0
    for copy in small:
        copy.wait()

    @pl.loop(0, STEPS)
    def _(step):
        for copy in copies(step):
            copy.wait()
        weights = weights_ref[pl.ds(pl.multiple_of(step * CB, CB), CB), :].astype(F32)
        for pair in range(CB // 2):
            records = []
            for j in (2 * pair, 2 * pair + 1):
                c = step * CB + j
                top = modes_ref[c, pl.ds(pl.multiple_of(pairs_ref[0, c] * BLK, BLK), BLK), :]
                bottom = modes_ref[c, pl.ds(pl.multiple_of(pairs_ref[1, c] * BLK, BLK), BLK), :]
                record = dot(coupling_ref[c], jnp.concatenate([top, bottom], axis=0))
                record = (record * weights[j : j + 1, :]).astype(BF)
                record_ref[c] = record
                records.append(record)
            both = jnp.concatenate(records, axis=0)
            products = dot_nt(both, both)
            for i in range(2):
                c = step * CB + 2 * pair + i
                s = products[i * BLK : (i + 1) * BLK, i * BLK : (i + 1) * BLK]
                cross = side_by_side(s[HALF:, :HALF])
                triangle = side_by_side(jnp.where(lower, s[:HALF, :HALF], s[HALF:, HALF:]))
                own_ref[pl.ds(c, 8, stride=CHILDREN_DEV), :] = jnp.where(first, cross, triangle)
                other_ref[pl.ds(c, 8, stride=CHILDREN_DEV), :] = jnp.where(first, triangle, cross)
                diag = jnp.sum(jnp.where(diagonal, s[HALF:], 0.0), axis=0, keepdims=True)
                zero = jnp.zeros((1, BLK), F32)
                named = zero + (block_ref[c] + 1).astype(F32)
                own_ref[pl.ds(8 * CHILDREN_DEV + c, 1), :] = jnp.concatenate([diag, named], axis=1)
                other_ref[pl.ds(8 * CHILDREN_DEV + c, 1), :] = jnp.concatenate([diag, zero], axis=1)
                p = parent_ref[c]
                k = count_ref[p]
                count_ref[p] = k + 1
                group = (p // (NZ * NX)) * NX + p % NX
                slot = group * SLOTS + ((p // NX) % NZ) * 2 + k
                for h in range(2):
                    hit = jnp.where(slots == slot - 128 * h, 1.0, 0.0)
                    own_ref[pl.ds((9 + h) * CHILDREN_DEV + c, 1), :] = hit
        record_copy(step).start()

    results = (
        pltpu.make_async_copy(other_ref, other_hbm, result_sem.at[0]),
        pltpu.make_async_copy(own_ref, own_hbm, result_sem.at[1]),
    )
    for copy in results:
        copy.start()
    for step in range(STEPS):
        record_copy(step).wait()
    for copy in results:
        copy.wait()


def moments(core, pairs, parent, block, coupling, modes, weights):
    hbm = pl.BlockSpec(memory_space=pltpu.HBM)
    return pl.pallas_call(
        moments_kernel,
        in_specs=[SMEM, hbm, hbm, hbm, hbm, hbm, hbm],
        out_specs=[hbm, hbm, hbm],
        out_shape=[
            jax.ShapeDtypeStruct((CHILDREN_DEV, BLK, 128), BF),
            jax.ShapeDtypeStruct((11 * CHILDREN_DEV, 128), F32),
            jax.ShapeDtypeStruct((9 * CHILDREN_DEV, 128), F32),
        ],
        scratch_shapes=[
            pltpu.SMEM((2, CHILDREN_DEV), jnp.int32),
            pltpu.SMEM((CHILDREN_DEV,), jnp.int32),
            pltpu.SMEM((CHILDREN_DEV,), jnp.int32),
            pltpu.VMEM((CHILDREN_DEV, BLK, 128), BF),
            pltpu.VMEM((CHILDREN_DEV, 256, 128), BF),
            pltpu.VMEM((CHILDREN_DEV, 128), BF),
            pltpu.VMEM((CHILDREN_DEV, BLK, 128), BF),
            pltpu.VMEM((11 * CHILDREN_DEV, 128), F32),
            pltpu.VMEM((9 * CHILDREN_DEV, 128), F32),
            pltpu.SMEM((NG * NZ,), jnp.int32),
            pltpu.SemaphoreType.DMA((4,)),
            pltpu.SemaphoreType.DMA((STEPS,)),
            pltpu.SemaphoreType.DMA((STEPS,)),
            pltpu.SemaphoreType.DMA((STEPS,)),
            pltpu.SemaphoreType.DMA((2,)),
        ],
        compiler_params=params(60),
        name="child_moments",
    )(core, pairs, parent, block, coupling, modes, weights)


def message_row(i, k):
    return k * 8 + i if i < 8 else 16 + k


def every_device(i, k):
    return pl.ds(message_row(i, k), PARENTS, stride=ROWS)


def stage_kernel(own_ref, sums_ref, place_ref, onehot_ref):
    sums_ref[...] = own_ref[: 9 * CHILDREN_DEV, :]
    onehot = jnp.concatenate(
        [own_ref[9 * CHILDREN_DEV : 10 * CHILDREN_DEV, :], own_ref[10 * CHILDREN_DEV :, :]], axis=1
    )
    place_ref[...] = onehot.T.astype(BF)
    onehot_ref[...] = onehot.astype(BF)


def stage(own):
    return pl.pallas_call(
        stage_kernel,
        in_specs=[VMEM],
        out_specs=[VMEM, VMEM, VMEM],
        out_shape=[
            jax.ShapeDtypeStruct((9 * CHILDREN_DEV, 128), F32),
            jax.ShapeDtypeStruct((NG * SLOTS, CHILDREN_DEV), BF),
            jax.ShapeDtypeStruct((CHILDREN_DEV, NG * SLOTS), BF),
        ],
        compiler_params=params(16),
        name="stage",
    )(own)


def dispatch_kernel(place_ref, own_ref, recv_ref, out_ref):
    place = place_ref[...]
    for i in range(9):
        rows = slice(i * CHILDREN_DEV, (i + 1) * CHILDREN_DEV)
        values = (own_ref[rows, :] + recv_ref[rows, :]).astype(BF)
        out_ref[:, i * SLOTS : (i + 1) * SLOTS, :] = dot(place, values).astype(BF).reshape(NG, SLOTS, 128)


def dispatch(place, own, recv):
    return pl.pallas_call(
        dispatch_kernel,
        in_specs=[VMEM, VMEM, VMEM],
        out_specs=VMEM,
        out_shape=jax.ShapeDtypeStruct((NG, ROWS, 128), BF),
        compiler_params=params(16),
        name="dispatch",
    )(place, own, recv)


def bin_kernel(recv_ref, out_ref, onehot_ref):
    count = NG * SLOTS
    meta = recv_ref[:, 8 * SLOTS : ROWS, :].astype(F32).reshape(count, 128)
    slot = lax.broadcasted_iota(jnp.int32, (count, 128), 0) % SLOTS
    lane = lax.broadcasted_iota(jnp.int32, (count, 128), 1)
    meta = pltpu.roll(meta, 64, 1)
    target = meta + (SB * (slot // 2) - 1).astype(F32)
    hit = (lane < 64) & (meta > 0.5) & (target == lane.astype(F32))
    onehot = jnp.where(hit, 1.0, 0.0).astype(BF)
    onehot_ref[...] = onehot
    values = jnp.concatenate(
        [recv_ref[:, i * SLOTS : (i + 1) * SLOTS, :].reshape(count, 128) for i in range(9)], axis=1
    )
    bins = dot_tn(onehot, values)
    zero = jnp.zeros((8, 128), F32)
    for z in range(NZ):
        rows = [bins[8 * z : 8 * z + 8, 128 * i : 128 * (i + 1)] for i in range(9)] + [zero]
        out_ref[z] = jnp.concatenate(rows, axis=0).astype(BF)


def bin_slots(recv):
    return pl.pallas_call(
        bin_kernel,
        in_specs=[VMEM],
        out_specs=[VMEM, VMEM],
        out_shape=[
            jax.ShapeDtypeStruct((NZ, ZROWS, 128), BF),
            jax.ShapeDtypeStruct((NG * SLOTS, 128), BF),
        ],
        compiler_params=params(16),
        name="bin_slots",
    )(recv)


def wide(x):
    return jnp.concatenate([x, x], axis=1)


def pivot_block(c, row, j):
    a00, a01, a11 = c[0][j : j + 1], c[1][j : j + 1], c[1][j + 1 : j + 2]
    a02, a12, a22 = c[2][j : j + 1], c[2][j + 1 : j + 2], c[2][j + 2 : j + 3]
    a03, a13, a23 = c[3][j : j + 1], c[3][j + 1 : j + 2], c[3][j + 2 : j + 3]
    a33 = c[3][j + 3 : j + 4]
    scale = 1.0 / (a00 * a11 - a01 * a01)
    p00, p01, p11 = a11 * scale, -a01 * scale, a00 * scale
    t00, t10 = p00 * a02 + p01 * a12, p01 * a02 + p11 * a12
    t01, t11 = p00 * a03 + p01 * a13, p01 * a03 + p11 * a13
    s00 = a22 - (a02 * t00 + a12 * t10)
    s01 = a23 - (a02 * t01 + a12 * t11)
    s11 = a33 - (a03 * t01 + a13 * t11)
    scale = 1.0 / (s00 * s11 - s01 * s01)
    inside = (row >= j) & (row < j + 4)
    m = [jnp.where(row == j + i, -1.0, jnp.where(inside, 0.0, c[i])) for i in range(4)]
    m[2] = m[2] - (m[0] * t00 + m[1] * t10)
    m[3] = m[3] - (m[0] * t01 + m[1] * t11)
    return (p00, p01, p11), (t00, t10, t01, t11), (s11 * scale, -s01 * scale, s00 * scale), m


def eliminate(rest, block, p, spread):
    (p00, p01, p11), (t00, t10, t01, t11), (q00, q01, q11), m = (
        [spread(v) for v in part] for part in block
    )
    y0, y1 = p00 * p[0] + p01 * p[1], p01 * p[0] + p11 * p[1]
    u2 = p[2] - (t00 * p[0] + t10 * p[1])
    u3 = p[3] - (t01 * p[0] + t11 * p[1])
    rest = rest - (m[0] * y0 + m[1] * y1)
    x2, x3 = q00 * u2 + q01 * u3, q01 * u2 + q11 * u3
    return (rest - m[2] * x2) - m[3] * x3


def invert(a_ref):
    lane = lax.broadcasted_iota(jnp.int32, (PB, MP), 1)
    row = lax.broadcasted_iota(jnp.int32, (PB, MP), 0)
    row_half = row[:, :128]
    lane_all = lax.broadcasted_iota(jnp.int32, (MP, MP), 1)
    line = lane[:1]
    for b in range(MP // PB):
        r = b * PB
        panel = a_ref[r : r + PB, :]
        for j8 in range(0, PB, 8):
            c = [jnp.broadcast_to(panel[:, r + j8 + i : r + j8 + i + 1], (PB, 128)) for i in range(8)]
            for h in (0, 4):
                j = j8 + h
                k = r + j
                block = pivot_block(c[h : h + 4], row_half, j)
                for m in range(h + 4, 8):
                    rest = jnp.where((row_half >= j) & (row_half < j + 4), 0.0, c[m])
                    c[m] = eliminate(rest, block, [c[m][j + i : j + i + 1] for i in range(4)], lambda v: v)
                inside = (line >= k) & (line < k + 4)
                p = [
                    jnp.where(line == k + i, 1.0, jnp.where(inside, 0.0, panel[j + i : j + i + 1]))
                    for i in range(4)
                ]
                cleared = ((lane >= k) & (lane < k + 4)) | ((row >= j) & (row < j + 4))
                panel = eliminate(jnp.where(cleared, 0.0, panel), block, p, wide)
        ch, cm, cl = split3(a_ref[:, r : r + PB])
        ph, pm, pw = split3(panel)
        update = dot(
            jnp.concatenate([ch, ch, cm, ch, cm, cl], axis=1),
            jnp.concatenate([ph, pm, ph, pw, pm, ph], axis=0),
        )
        a_ref[...] = jnp.where((lane_all // PB) == b, 0.0, a_ref[...]) - update
        a_ref[r : r + PB, :] = panel


def split3(x):
    high = x.astype(BF)
    rest = x - high.astype(F32)
    mid = rest.astype(BF)
    return high, mid, (rest - mid.astype(F32)).astype(BF)


def split(x):
    high = x.astype(BF)
    return high, (x - high.astype(F32)).astype(BF)


def pencil_kernel(
    core_ref, mine_ref, theirs_ref, q_ref, eigs_ref, out_ref, a_ref, y_ref, pack_ref, own_ref, other_ref
):
    for source, target in ((mine_ref, own_ref), (theirs_ref, other_ref)):
        parts = [source[z].astype(F32) for z in range(NZ)]
        while len(parts) > 1:
            parts = [x + y for x, y in zip(parts[::2], parts[1::2])]
        target[...] = parts[0]
    row, col = square_index()
    first = core_ref[0] == 0
    diags = jnp.where(first, other_ref[64:72, 32:64], own_ref[64:72, 32:64])
    for b in range(SB):
        own = own_ref[pl.ds(b, 8, stride=8), :]
        other = other_ref[pl.ds(b, 8, stride=8), :]
        cross = stacked(jnp.where(first, own, other))
        triangle = stacked(jnp.where(first, other, own))
        n11 = jnp.where(row > col, triangle, jnp.where(row == col, 0.5 * triangle, 0.0))
        n22 = jnp.where(row < col, triangle, jnp.where(row == col, 0.5 * diags[b : b + 1, :], 0.0))
        q1 = q_ref[b * BLK : b * BLK + HALF, :]
        q2 = q_ref[b * BLK + HALF : (b + 1) * BLK, :]
        y = dot(jnp.concatenate([n11, cross], axis=0).astype(BF), q1)
        bottom = y[HALF:] + dot(n22.astype(BF), q2)
        y_ref[b * BLK : (b + 1) * BLK, :] = jnp.concatenate([y[:HALF], bottom], axis=0).astype(BF)
    x = dot_tn(q_ref[...], y_ref[...])
    r = lax.broadcasted_iota(jnp.int32, (MP, MP), 0)
    c = lax.broadcasted_iota(jnp.int32, (MP, MP), 1)
    a_ref[...] = (x + x.T) * (1.0 / 16384.0) + jnp.where(r == c, eigs_ref[...], 0.0)
    invert(a_ref)
    high, low = split(a_ref[...] * (1.0 / MP))
    q = q_ref[...]
    y_high, y_low = split(dot(q, high) + dot(q, low))
    for b in range(SB):
        s = b * BLK
        qb = q_ref[s : s + BLK, :]
        h = dot_nt(qb, y_high[s : s + BLK]) + dot_nt(qb, y_low[s : s + BLK])
        h11, h22 = h[:HALF, :HALF], h[HALF:, HALF:]
        cross = side_by_side(2.0 * h[HALF:, :HALF])
        triangle = side_by_side(jnp.where(row > col, 2.0 * h11, jnp.where(row == col, h11, 2.0 * h22)))
        diag = jnp.sum(jnp.where(row == col, h22, 0.0), axis=0, keepdims=True)
        pack_ref[pl.ds(b, 8, stride=8), :] = jnp.where(first, cross, triangle)
        pack_ref[64 + b : 65 + b, :] = jnp.concatenate([diag, jnp.zeros((1, 96), F32)], axis=1)
    pack_ref[72:80, :] = jnp.zeros((8, 128), F32)
    result = pack_ref[...].astype(BF)
    for z in range(NZ):
        out_ref[z] = result


def pencil_blocks(core, own, other, q, eigs):
    return pl.pallas_call(
        pencil_kernel,
        in_specs=[SMEM, VMEM, VMEM, VMEM, VMEM],
        out_specs=VMEM,
        out_shape=jax.ShapeDtypeStruct((NZ, ZROWS, 128), BF),
        scratch_shapes=[
            pltpu.VMEM((MP, MP), F32),
            pltpu.VMEM((SB * BLK, MP), BF),
            pltpu.VMEM((ZROWS, 128), F32),
            pltpu.VMEM((ZROWS, 128), F32),
            pltpu.VMEM((ZROWS, 128), F32),
        ],
        compiler_params=params(16),
        name="pencil_blocks",
    )(core, own, other, q, eigs)


def select_kernel(bins_ref, onehot_ref, out_ref):
    onehot = onehot_ref[:, 0:64]
    bins = [bins_ref[z].astype(F32) for z in range(NZ)]
    for i in range(9):
        values = jnp.concatenate([x[8 * i : 8 * i + 8] for x in bins], axis=0).astype(BF)
        picked = dot(onehot, values).astype(BF)
        out_ref[:, i * SLOTS : (i + 1) * SLOTS, :] = picked.reshape(NG, SLOTS, 128)


def select_bins(bins, onehot):
    return pl.pallas_call(
        select_kernel,
        in_specs=[VMEM, VMEM],
        out_specs=VMEM,
        out_shape=jax.ShapeDtypeStruct((NG, ROWS, 128), BF),
        compiler_params=params(16),
        name="select_bins",
    )(bins, onehot)


def collect_kernel(onehot_ref, recv_ref, out_ref):
    onehot = onehot_ref[...]
    for i in range(9):
        values = recv_ref[:, i * SLOTS : (i + 1) * SLOTS, :].reshape(NG * SLOTS, 128)
        out_ref[i * CHILDREN_DEV : (i + 1) * CHILDREN_DEV, :] = dot(onehot, values).astype(BF)


def collect(onehot, recv):
    return pl.pallas_call(
        collect_kernel,
        in_specs=[VMEM, VMEM],
        out_specs=VMEM,
        out_shape=jax.ShapeDtypeStruct((9 * CHILDREN_DEV, 128), BF),
        compiler_params=params(16),
        name="collect",
    )(onehot, recv)


def strength_kernel(core_ref, mine_ref, theirs_ref, record_ref, out_ref, own_ref, other_ref):
    step = pl.program_id(0)

    @pl.when(step == 0)
    def _():
        own_ref[...] = mine_ref[...].astype(F32)
        other_ref[...] = theirs_ref[...].astype(F32)

    row, col = square_index()
    first = core_ref[0] == 0
    for j in range(CB):
        c = step * CB + j
        own = own_ref[pl.ds(c, 8, stride=CHILDREN_DEV), :]
        other = other_ref[pl.ds(c, 8, stride=CHILDREN_DEV), :]
        r = pl.ds(8 * CHILDREN_DEV + c, 1)
        diag = jnp.where(first, other_ref[r, :], own_ref[r, :])[:, :HALF]
        cross = stacked(jnp.where(first, own, other))
        triangle = stacked(jnp.where(first, other, own))
        m11 = jnp.where(row >= col, triangle, 0.0)
        m22 = jnp.where(row < col, triangle, jnp.where(row == col, diag, 0.0))
        record = record_ref[j]
        left = dot(jnp.concatenate([m11, cross], axis=0).astype(BF), record[:HALF])
        right = dot(m22.astype(BF), record[HALF:])
        wide_record = record.astype(F32)
        terms = left[:HALF] * wide_record[:HALF] + (left[HALF:] + right) * wide_record[HALF:]
        out_ref[j : j + 1, :] = jnp.sum(terms, axis=0, keepdims=True)


def strengths(core, own, other, record):
    whole = (9 * CHILDREN_DEV, 128)
    return pl.pallas_call(
        strength_kernel,
        grid=(STEPS,),
        in_specs=[
            SMEM,
            pl.BlockSpec(whole, lambda i: (0, 0)),
            pl.BlockSpec(whole, lambda i: (0, 0)),
            pl.BlockSpec((CB, BLK, 128), lambda i: (i, 0, 0)),
        ],
        out_specs=pl.BlockSpec((CB, 128), lambda i: (i, 0)),
        out_shape=jax.ShapeDtypeStruct((CHILDREN_DEV, 128), F32),
        scratch_shapes=[pltpu.VMEM(whole, F32), pltpu.VMEM(whole, F32)],
        compiler_params=params(16),
        name="strengths",
    )(core, own, other, record)


def swap(x):
    return lax.ppermute(x, "mode", [(0, 1), (1, 0)])


def exchange(x, axes):
    return lax.all_to_all(x, axes, split_axis=0, concat_axis=0, tiled=True)


def per_device(coupling, pairs, modes, weights, parent_of, row_block, parent_modes, parent_eigs):
    core = lax.axis_index("mode").astype(jnp.int32).reshape(1)
    parent = parent_of.reshape(CHILDREN_DEV)
    record, own, other = moments(core, pairs.T, parent, row_block, coupling, modes, weights)
    sums, place, onehot = stage(own)
    sent = dispatch(place, sums, swap(other))
    binned, chosen = bin_slots(exchange(sent, ("y", "x")))
    bins = exchange(binned, "z")
    blocks = pencil_blocks(core, bins, swap(bins), parent_modes[0], parent_eigs)
    picked = select_bins(exchange(blocks, "z"), chosen)
    mine = collect(onehot, exchange(picked, ("y", "x")))
    return strengths(core, mine, swap(mine), record)


def solution(mesh):
    grid = Mesh(mesh.devices.reshape(NY, NZ, NX, 2), ("y", "z", "x", "mode"))
    sub = ("y", "z", "x")
    in_specs = (
        P(sub, None, None),
        P(sub, None),
        P(sub, None, "mode"),
        P(sub, "mode"),
        P(sub, None),
        P(sub),
        P(sub, None, None),
        P(sub, None),
    )
    return jax.shard_map(
        per_device, mesh=grid, in_specs=in_specs, out_specs=P(sub, "mode"), check_vma=False
    )
```

```python
import jax
import jax.numpy as jnp
from jax import lax
from jax.experimental import pallas as pl
from jax.experimental.pallas import tpu as pltpu
from jax.sharding import Mesh, PartitionSpec as P

MP = 256
BLK = 64
HALF = 32
SB = 8
CHILDREN_DEV = 64
CB = 32
STEPS = CHILDREN_DEV // CB
NY, NZ, NX = 4, 8, 4
NG = NY * NX
SLOTS = 2 * NZ
ROWS = 9 * SLOTS
ZROWS = 80
PB = 32
BF = jnp.bfloat16
F32 = jnp.float32
VMEM = pl.BlockSpec(memory_space=pltpu.VMEM)
SMEM = pl.BlockSpec(memory_space=pltpu.SMEM)


def params(mib, **more):
    return pltpu.CompilerParams(vmem_limit_bytes=mib * 1024 * 1024, **more)


def dot(a, b):
    return jnp.dot(a, b, preferred_element_type=F32)


def dot_nt(a, b):
    return lax.dot_general(a, b, (((1,), (1,)), ((), ())), preferred_element_type=F32)


def dot_tn(a, b):
    return lax.dot_general(a, b, (((0,), (0,)), ((), ())), preferred_element_type=F32)


def square_index():
    return (
        lax.broadcasted_iota(jnp.int32, (HALF, HALF), 0),
        lax.broadcasted_iota(jnp.int32, (HALF, HALF), 1),
    )


def stacked(x):
    return jnp.concatenate([x[:, 0:32], x[:, 32:64], x[:, 64:96], x[:, 96:128]], axis=0)


def side_by_side(x):
    return jnp.concatenate([x[0:8], x[8:16], x[16:24], x[24:32]], axis=1)


def moments_kernel(
    core_ref, pairs_hbm, parent_hbm, block_hbm, coupling_hbm, modes_hbm, weights_hbm,
    record_hbm, own_hbm, other_hbm,
    pairs_ref, parent_ref, block_ref, coupling_ref, modes_ref, weights_ref, record_ref, own_ref, other_ref,
    sent_ref, count_ref, small_sem, coupling_sem, modes_sem, record_sem, result_sem,
):
    small = [
        pltpu.make_async_copy(source, target, small_sem.at[i])
        for i, (source, target) in enumerate(
            (
                (pairs_hbm, pairs_ref),
                (parent_hbm, parent_ref),
                (block_hbm, block_ref),
                (weights_hbm, weights_ref),
            )
        )
    ]
    for copy in small:
        copy.start()
    row, col = square_index()
    lower = row >= col
    diagonal = lax.broadcasted_iota(jnp.int32, (HALF, BLK), 1) == (
        lax.broadcasted_iota(jnp.int32, (HALF, BLK), 0) + HALF
    )
    slots = lax.broadcasted_iota(jnp.int32, (1, 128), 1)
    first = core_ref[0] == 0

    def copies(step):
        part = pl.ds(step * CB, CB)
        return (
            pltpu.make_async_copy(modes_hbm.at[part], modes_ref.at[part], modes_sem.at[step]),
            pltpu.make_async_copy(coupling_hbm.at[part], coupling_ref.at[part], coupling_sem.at[step]),
        )

    def record_copy(step):
        part = pl.ds(step * CB, CB)
        return pltpu.make_async_copy(record_ref.at[part], record_hbm.at[part], record_sem.at[step])

    for step in range(STEPS):
        for copy in copies(step):
            copy.start()
    for p in range(NG * NZ):
        count_ref[p] = 0
    for copy in small:
        copy.wait()

    @pl.loop(0, STEPS)
    def _(step):
        for copy in copies(step):
            copy.wait()
        weights = weights_ref[pl.ds(pl.multiple_of(step * CB, CB), CB), :].astype(F32)
        for pair in range(CB // 2):
            records = []
            for j in (2 * pair, 2 * pair + 1):
                c = step * CB + j
                top = modes_ref[c, pl.ds(pl.multiple_of(pairs_ref[0, c] * BLK, BLK), BLK), :]
                bottom = modes_ref[c, pl.ds(pl.multiple_of(pairs_ref[1, c] * BLK, BLK), BLK), :]
                record = dot(coupling_ref[c], jnp.concatenate([top, bottom], axis=0))
                record = (record * weights[j : j + 1, :]).astype(BF)
                record_ref[c] = record
                records.append(record)
            both = jnp.concatenate(records, axis=0)
            products = dot_nt(both, both)
            for i in range(2):
                c = step * CB + 2 * pair + i
                s = products[i * BLK : (i + 1) * BLK, i * BLK : (i + 1) * BLK]
                cross = side_by_side(s[HALF:, :HALF])
                triangle = side_by_side(jnp.where(lower, s[:HALF, :HALF], s[HALF:, HALF:]))
                own_ref[pl.ds(c, 8, stride=CHILDREN_DEV), :] = jnp.where(first, cross, triangle)
                other_ref[pl.ds(c, 8, stride=CHILDREN_DEV), :] = jnp.where(first, triangle, cross)
                diag = jnp.sum(jnp.where(diagonal, s[HALF:], 0.0), axis=0, keepdims=True)
                zero = jnp.zeros((1, BLK), F32)
                named = zero + (block_ref[c] + 1).astype(F32)
                own_ref[pl.ds(8 * CHILDREN_DEV + c, 1), :] = jnp.concatenate([diag, named], axis=1)
                other_ref[pl.ds(8 * CHILDREN_DEV + c, 1), :] = jnp.concatenate([diag, zero], axis=1)
                p = parent_ref[c]
                k = count_ref[p]
                count_ref[p] = k + 1
                group = (p // (NZ * NX)) * NX + p % NX
                slot = group * SLOTS + ((p // NX) % NZ) * 2 + k
                for h in range(2):
                    hit = jnp.where(slots == slot - 128 * h, 1.0, 0.0)
                    own_ref[pl.ds((9 + h) * CHILDREN_DEV + c, 1), :] = hit
        record_copy(step).start()

    sent_ref[...] = other_ref[...].astype(BF)
    results = (
        pltpu.make_async_copy(sent_ref, other_hbm, result_sem.at[0]),
        pltpu.make_async_copy(own_ref, own_hbm, result_sem.at[1]),
    )
    for copy in results:
        copy.start()
    for step in range(STEPS):
        record_copy(step).wait()
    for copy in results:
        copy.wait()


def moments(core, pairs, parent, block, coupling, modes, weights):
    hbm = pl.BlockSpec(memory_space=pltpu.HBM)
    return pl.pallas_call(
        moments_kernel,
        in_specs=[SMEM, hbm, hbm, hbm, hbm, hbm, hbm],
        out_specs=[hbm, hbm, hbm],
        out_shape=[
            jax.ShapeDtypeStruct((CHILDREN_DEV, BLK, 128), BF),
            jax.ShapeDtypeStruct((11 * CHILDREN_DEV, 128), F32),
            jax.ShapeDtypeStruct((9 * CHILDREN_DEV, 128), BF),
        ],
        scratch_shapes=[
            pltpu.SMEM((2, CHILDREN_DEV), jnp.int32),
            pltpu.SMEM((CHILDREN_DEV,), jnp.int32),
            pltpu.SMEM((CHILDREN_DEV,), jnp.int32),
            pltpu.VMEM((CHILDREN_DEV, BLK, 128), BF),
            pltpu.VMEM((CHILDREN_DEV, 256, 128), BF),
            pltpu.VMEM((CHILDREN_DEV, 128), BF),
            pltpu.VMEM((CHILDREN_DEV, BLK, 128), BF),
            pltpu.VMEM((11 * CHILDREN_DEV, 128), F32),
            pltpu.VMEM((9 * CHILDREN_DEV, 128), F32),
            pltpu.VMEM((9 * CHILDREN_DEV, 128), BF),
            pltpu.SMEM((NG * NZ,), jnp.int32),
            pltpu.SemaphoreType.DMA((4,)),
            pltpu.SemaphoreType.DMA((STEPS,)),
            pltpu.SemaphoreType.DMA((STEPS,)),
            pltpu.SemaphoreType.DMA((STEPS,)),
            pltpu.SemaphoreType.DMA((2,)),
        ],
        compiler_params=params(60),
        name="child_moments",
    )(core, pairs, parent, block, coupling, modes, weights)


def message_row(i, k):
    return k * 8 + i if i < 8 else 16 + k


def every_device(i, k):
    return pl.ds(message_row(i, k), PARENTS, stride=ROWS)


def stage_kernel(own_ref, sums_ref, place_ref, onehot_ref):
    sums_ref[...] = own_ref[: 9 * CHILDREN_DEV, :]
    onehot = jnp.concatenate(
        [own_ref[9 * CHILDREN_DEV : 10 * CHILDREN_DEV, :], own_ref[10 * CHILDREN_DEV :, :]], axis=1
    )
    place_ref[...] = onehot.T.astype(BF)
    onehot_ref[...] = onehot.astype(BF)


def stage(own):
    return pl.pallas_call(
        stage_kernel,
        in_specs=[VMEM],
        out_specs=[VMEM, VMEM, VMEM],
        out_shape=[
            jax.ShapeDtypeStruct((9 * CHILDREN_DEV, 128), F32),
            jax.ShapeDtypeStruct((NG * SLOTS, CHILDREN_DEV), BF),
            jax.ShapeDtypeStruct((CHILDREN_DEV, NG * SLOTS), BF),
        ],
        compiler_params=params(16),
        name="stage",
    )(own)


def dispatch_kernel(place_ref, own_ref, recv_ref, out_ref):
    place = place_ref[...]
    for i in range(9):
        rows = slice(i * CHILDREN_DEV, (i + 1) * CHILDREN_DEV)
        values = (own_ref[rows, :] + recv_ref[rows, :].astype(F32)).astype(BF)
        out_ref[:, i * SLOTS : (i + 1) * SLOTS, :] = dot(place, values).astype(BF).reshape(NG, SLOTS, 128)


def dispatch(place, own, recv):
    return pl.pallas_call(
        dispatch_kernel,
        in_specs=[VMEM, VMEM, VMEM],
        out_specs=VMEM,
        out_shape=jax.ShapeDtypeStruct((NG, ROWS, 128), BF),
        compiler_params=params(16),
        name="dispatch",
    )(place, own, recv)


def bin_kernel(recv_ref, out_ref, onehot_ref):
    count = NG * SLOTS
    meta = recv_ref[:, 8 * SLOTS : ROWS, :].astype(F32).reshape(count, 128)
    slot = lax.broadcasted_iota(jnp.int32, (count, 128), 0) % SLOTS
    lane = lax.broadcasted_iota(jnp.int32, (count, 128), 1)
    meta = pltpu.roll(meta, 64, 1)
    target = meta + (SB * (slot // 2) - 1).astype(F32)
    hit = (lane < 64) & (meta > 0.5) & (target == lane.astype(F32))
    onehot = jnp.where(hit, 1.0, 0.0).astype(BF)
    onehot_ref[...] = onehot
    values = jnp.concatenate(
        [recv_ref[:, i * SLOTS : (i + 1) * SLOTS, :].reshape(count, 128) for i in range(9)], axis=1
    )
    bins = dot_tn(onehot, values)
    zero = jnp.zeros((8, 128), F32)
    for z in range(NZ):
        rows = [bins[8 * z : 8 * z + 8, 128 * i : 128 * (i + 1)] for i in range(9)] + [zero]
        out_ref[z] = jnp.concatenate(rows, axis=0).astype(BF)


def bin_slots(recv):
    return pl.pallas_call(
        bin_kernel,
        in_specs=[VMEM],
        out_specs=[VMEM, VMEM],
        out_shape=[
            jax.ShapeDtypeStruct((NZ, ZROWS, 128), BF),
            jax.ShapeDtypeStruct((NG * SLOTS, 128), BF),
        ],
        compiler_params=params(16),
        name="bin_slots",
    )(recv)


def wide(x):
    return jnp.concatenate([x, x], axis=1)


def pivot_block(c, row, j):
    a00, a01, a11 = c[0][j : j + 1], c[1][j : j + 1], c[1][j + 1 : j + 2]
    a02, a12, a22 = c[2][j : j + 1], c[2][j + 1 : j + 2], c[2][j + 2 : j + 3]
    a03, a13, a23 = c[3][j : j + 1], c[3][j + 1 : j + 2], c[3][j + 2 : j + 3]
    a33 = c[3][j + 3 : j + 4]
    scale = 1.0 / (a00 * a11 - a01 * a01)
    p00, p01, p11 = a11 * scale, -a01 * scale, a00 * scale
    t00, t10 = p00 * a02 + p01 * a12, p01 * a02 + p11 * a12
    t01, t11 = p00 * a03 + p01 * a13, p01 * a03 + p11 * a13
    s00 = a22 - (a02 * t00 + a12 * t10)
    s01 = a23 - (a02 * t01 + a12 * t11)
    s11 = a33 - (a03 * t01 + a13 * t11)
    scale = 1.0 / (s00 * s11 - s01 * s01)
    inside = (row >= j) & (row < j + 4)
    m = [jnp.where(row == j + i, -1.0, jnp.where(inside, 0.0, c[i])) for i in range(4)]
    m[2] = m[2] - (m[0] * t00 + m[1] * t10)
    m[3] = m[3] - (m[0] * t01 + m[1] * t11)
    return (p00, p01, p11), (t00, t10, t01, t11), (s11 * scale, -s01 * scale, s00 * scale), m


def eliminate(rest, block, p, spread):
    (p00, p01, p11), (t00, t10, t01, t11), (q00, q01, q11), m = (
        [spread(v) for v in part] for part in block
    )
    y0, y1 = p00 * p[0] + p01 * p[1], p01 * p[0] + p11 * p[1]
    u2 = p[2] - (t00 * p[0] + t10 * p[1])
    u3 = p[3] - (t01 * p[0] + t11 * p[1])
    rest = rest - (m[0] * y0 + m[1] * y1)
    x2, x3 = q00 * u2 + q01 * u3, q01 * u2 + q11 * u3
    return (rest - m[2] * x2) - m[3] * x3


def invert(a_ref):
    lane = lax.broadcasted_iota(jnp.int32, (PB, MP), 1)
    row = lax.broadcasted_iota(jnp.int32, (PB, MP), 0)
    row_half = row[:, :128]
    lane_all = lax.broadcasted_iota(jnp.int32, (MP, MP), 1)
    line = lane[:1]
    for b in range(MP // PB):
        r = b * PB
        panel = a_ref[r : r + PB, :]
        for j8 in range(0, PB, 8):
            c = [jnp.broadcast_to(panel[:, r + j8 + i : r + j8 + i + 1], (PB, 128)) for i in range(8)]
            for h in (0, 4):
                j = j8 + h
                k = r + j
                block = pivot_block(c[h : h + 4], row_half, j)
                for m in range(h + 4, 8):
                    rest = jnp.where((row_half >= j) & (row_half < j + 4), 0.0, c[m])
                    c[m] = eliminate(rest, block, [c[m][j + i : j + i + 1] for i in range(4)], lambda v: v)
                inside = (line >= k) & (line < k + 4)
                p = [
                    jnp.where(line == k + i, 1.0, jnp.where(inside, 0.0, panel[j + i : j + i + 1]))
                    for i in range(4)
                ]
                cleared = ((lane >= k) & (lane < k + 4)) | ((row >= j) & (row < j + 4))
                panel = eliminate(jnp.where(cleared, 0.0, panel), block, p, wide)
        ch, cm, cl = split3(a_ref[:, r : r + PB])
        ph, pm, pw = split3(panel)
        update = dot(
            jnp.concatenate([ch, ch, cm, ch, cm, cl], axis=1),
            jnp.concatenate([ph, pm, ph, pw, pm, ph], axis=0),
        )
        a_ref[...] = jnp.where((lane_all // PB) == b, 0.0, a_ref[...]) - update
        a_ref[r : r + PB, :] = panel


def split3(x):
    high = x.astype(BF)
    rest = x - high.astype(F32)
    mid = rest.astype(BF)
    return high, mid, (rest - mid.astype(F32)).astype(BF)


def split(x):
    high = x.astype(BF)
    return high, (x - high.astype(F32)).astype(BF)


def pencil_kernel(
    core_ref, mine_ref, theirs_ref, q_ref, eigs_ref, out_ref, a_ref, y_ref, pack_ref, own_ref, other_ref
):
    for source, target in ((mine_ref, own_ref), (theirs_ref, other_ref)):
        parts = [source[z].astype(F32) for z in range(NZ)]
        while len(parts) > 1:
            parts = [x + y for x, y in zip(parts[::2], parts[1::2])]
        target[...] = parts[0]
    row, col = square_index()
    first = core_ref[0] == 0
    diags = jnp.where(first, other_ref[64:72, 32:64], own_ref[64:72, 32:64])
    for b in range(SB):
        own = own_ref[pl.ds(b, 8, stride=8), :]
        other = other_ref[pl.ds(b, 8, stride=8), :]
        cross = stacked(jnp.where(first, own, other))
        triangle = stacked(jnp.where(first, other, own))
        n11 = jnp.where(row > col, triangle, jnp.where(row == col, 0.5 * triangle, 0.0))
        n22 = jnp.where(row < col, triangle, jnp.where(row == col, 0.5 * diags[b : b + 1, :], 0.0))
        q1 = q_ref[b * BLK : b * BLK + HALF, :]
        q2 = q_ref[b * BLK + HALF : (b + 1) * BLK, :]
        y = dot(jnp.concatenate([n11, cross], axis=0).astype(BF), q1)
        bottom = y[HALF:] + dot(n22.astype(BF), q2)
        y_ref[b * BLK : (b + 1) * BLK, :] = jnp.concatenate([y[:HALF], bottom], axis=0).astype(BF)
    x = dot_tn(q_ref[...], y_ref[...])
    r = lax.broadcasted_iota(jnp.int32, (MP, MP), 0)
    c = lax.broadcasted_iota(jnp.int32, (MP, MP), 1)
    a_ref[...] = (x + x.T) * (1.0 / 16384.0) + jnp.where(r == c, eigs_ref[...], 0.0)
    invert(a_ref)
    high, low = split(a_ref[...] * (1.0 / MP))
    q = q_ref[...]
    y_high, y_low = split(dot(q, high) + dot(q, low))
    for b in range(SB):
        s = b * BLK
        qb = q_ref[s : s + BLK, :]
        h = dot_nt(qb, y_high[s : s + BLK]) + dot_nt(qb, y_low[s : s + BLK])
        h11, h22 = h[:HALF, :HALF], h[HALF:, HALF:]
        cross = side_by_side(2.0 * h[HALF:, :HALF])
        triangle = side_by_side(jnp.where(row > col, 2.0 * h11, jnp.where(row == col, h11, 2.0 * h22)))
        diag = jnp.sum(jnp.where(row == col, h22, 0.0), axis=0, keepdims=True)
        pack_ref[pl.ds(b, 8, stride=8), :] = jnp.where(first, cross, triangle)
        pack_ref[64 + b : 65 + b, :] = jnp.concatenate([diag, jnp.zeros((1, 96), F32)], axis=1)
    pack_ref[72:80, :] = jnp.zeros((8, 128), F32)
    result = pack_ref[...].astype(BF)
    for z in range(NZ):
        out_ref[z] = result


def pencil_blocks(core, own, other, q, eigs):
    return pl.pallas_call(
        pencil_kernel,
        in_specs=[SMEM, VMEM, VMEM, VMEM, VMEM],
        out_specs=VMEM,
        out_shape=jax.ShapeDtypeStruct((NZ, ZROWS, 128), BF),
        scratch_shapes=[
            pltpu.VMEM((MP, MP), F32),
            pltpu.VMEM((SB * BLK, MP), BF),
            pltpu.VMEM((ZROWS, 128), F32),
            pltpu.VMEM((ZROWS, 128), F32),
            pltpu.VMEM((ZROWS, 128), F32),
        ],
        compiler_params=params(16),
        name="pencil_blocks",
    )(core, own, other, q, eigs)


def select_kernel(bins_ref, onehot_ref, out_ref):
    onehot = onehot_ref[:, 0:64]
    bins = [bins_ref[z].astype(F32) for z in range(NZ)]
    for i in range(9):
        values = jnp.concatenate([x[8 * i : 8 * i + 8] for x in bins], axis=0).astype(BF)
        picked = dot(onehot, values).astype(BF)
        out_ref[:, i * SLOTS : (i + 1) * SLOTS, :] = picked.reshape(NG, SLOTS, 128)


def select_bins(bins, onehot):
    return pl.pallas_call(
        select_kernel,
        in_specs=[VMEM, VMEM],
        out_specs=VMEM,
        out_shape=jax.ShapeDtypeStruct((NG, ROWS, 128), BF),
        compiler_params=params(16),
        name="select_bins",
    )(bins, onehot)


def collect_kernel(onehot_ref, recv_ref, out_ref):
    onehot = onehot_ref[...]
    for i in range(9):
        values = recv_ref[:, i * SLOTS : (i + 1) * SLOTS, :].reshape(NG * SLOTS, 128)
        out_ref[i * CHILDREN_DEV : (i + 1) * CHILDREN_DEV, :] = dot(onehot, values).astype(BF)


def collect(onehot, recv):
    return pl.pallas_call(
        collect_kernel,
        in_specs=[VMEM, VMEM],
        out_specs=VMEM,
        out_shape=jax.ShapeDtypeStruct((9 * CHILDREN_DEV, 128), BF),
        compiler_params=params(16),
        name="collect",
    )(onehot, recv)


def strength_kernel(core_ref, mine_ref, theirs_ref, record_ref, out_ref, own_ref, other_ref):
    step = pl.program_id(0)

    @pl.when(step == 0)
    def _():
        own_ref[...] = mine_ref[...].astype(F32)
        other_ref[...] = theirs_ref[...].astype(F32)

    row, col = square_index()
    first = core_ref[0] == 0
    for j in range(CB):
        c = step * CB + j
        own = own_ref[pl.ds(c, 8, stride=CHILDREN_DEV), :]
        other = other_ref[pl.ds(c, 8, stride=CHILDREN_DEV), :]
        r = pl.ds(8 * CHILDREN_DEV + c, 1)
        diag = jnp.where(first, other_ref[r, :], own_ref[r, :])[:, :HALF]
        cross = stacked(jnp.where(first, own, other))
        triangle = stacked(jnp.where(first, other, own))
        m11 = jnp.where(row >= col, triangle, 0.0)
        m22 = jnp.where(row < col, triangle, jnp.where(row == col, diag, 0.0))
        record = record_ref[j]
        left = dot(jnp.concatenate([m11, cross], axis=0).astype(BF), record[:HALF])
        right = dot(m22.astype(BF), record[HALF:])
        wide_record = record.astype(F32)
        terms = left[:HALF] * wide_record[:HALF] + (left[HALF:] + right) * wide_record[HALF:]
        out_ref[j : j + 1, :] = jnp.sum(terms, axis=0, keepdims=True)


def strengths(core, own, other, record):
    whole = (9 * CHILDREN_DEV, 128)
    return pl.pallas_call(
        strength_kernel,
        grid=(STEPS,),
        in_specs=[
            SMEM,
            pl.BlockSpec(whole, lambda i: (0, 0)),
            pl.BlockSpec(whole, lambda i: (0, 0)),
            pl.BlockSpec((CB, BLK, 128), lambda i: (i, 0, 0)),
        ],
        out_specs=pl.BlockSpec((CB, 128), lambda i: (i, 0)),
        out_shape=jax.ShapeDtypeStruct((CHILDREN_DEV, 128), F32),
        scratch_shapes=[pltpu.VMEM(whole, F32), pltpu.VMEM(whole, F32)],
        compiler_params=params(16),
        name="strengths",
    )(core, own, other, record)


def swap(x):
    return lax.ppermute(x, "mode", [(0, 1), (1, 0)])


def exchange(x, axes):
    return lax.all_to_all(x, axes, split_axis=0, concat_axis=0, tiled=True)


def per_device(coupling, pairs, modes, weights, parent_of, row_block, parent_modes, parent_eigs):
    core = lax.axis_index("mode").astype(jnp.int32).reshape(1)
    parent = parent_of.reshape(CHILDREN_DEV)
    record, own, other = moments(core, pairs.T, parent, row_block, coupling, modes, weights)
    sums, place, onehot = stage(own)
    sent = dispatch(place, sums, swap(other))
    binned, chosen = bin_slots(exchange(sent, ("y", "x")))
    bins = exchange(binned, "z")
    blocks = pencil_blocks(core, bins, swap(bins), parent_modes[0], parent_eigs)
    picked = select_bins(exchange(blocks, "z"), chosen)
    mine = collect(onehot, exchange(picked, ("y", "x")))
    return strengths(core, mine, swap(mine), record)


def solution(mesh):
    grid = Mesh(mesh.devices.reshape(NY, NZ, NX, 2), ("y", "z", "x", "mode"))
    sub = ("y", "z", "x")
    in_specs = (
        P(sub, None, None),
        P(sub, None),
        P(sub, None, "mode"),
        P(sub, "mode"),
        P(sub, None),
        P(sub),
        P(sub, None, None),
        P(sub, None),
    )
    return jax.shard_map(
        per_device, mesh=grid, in_specs=in_specs, out_specs=P(sub, "mode"), check_vma=False
    )
```

```python
import jax
import jax.numpy as jnp
from jax import lax
from jax.experimental import pallas as pl
from jax.experimental.pallas import tpu as pltpu
from jax.sharding import Mesh, PartitionSpec as P

MP = 256
BLK = 64
HALF = 32
SB = 8
CHILDREN_DEV = 64
CB = 32
STEPS = CHILDREN_DEV // CB
NY, NZ, NX = 4, 8, 4
NG = NY * NX
SLOTS = 2 * NZ
ROWS = 9 * SLOTS
ZROWS = 80
PB = 32
BF = jnp.bfloat16
F32 = jnp.float32
VMEM = pl.BlockSpec(memory_space=pltpu.VMEM)
SMEM = pl.BlockSpec(memory_space=pltpu.SMEM)


def params(mib, **more):
    return pltpu.CompilerParams(vmem_limit_bytes=mib * 1024 * 1024, **more)


def dot(a, b):
    return jnp.dot(a, b, preferred_element_type=F32)


def dot_nt(a, b):
    return lax.dot_general(a, b, (((1,), (1,)), ((), ())), preferred_element_type=F32)


def dot_tn(a, b):
    return lax.dot_general(a, b, (((0,), (0,)), ((), ())), preferred_element_type=F32)


def square_index():
    return (
        lax.broadcasted_iota(jnp.int32, (HALF, HALF), 0),
        lax.broadcasted_iota(jnp.int32, (HALF, HALF), 1),
    )


def stacked(x):
    return jnp.concatenate([x[:, 0:32], x[:, 32:64], x[:, 64:96], x[:, 96:128]], axis=0)


def side_by_side(x):
    return jnp.concatenate([x[0:8], x[8:16], x[16:24], x[24:32]], axis=1)


def moments_kernel(
    core_ref, pairs_hbm, parent_hbm, block_hbm, coupling_hbm, modes_hbm, weights_hbm,
    record_hbm, own_hbm, other_hbm,
    pairs_ref, parent_ref, block_ref, coupling_ref, modes_ref, weights_ref, record_ref, own_ref, other_ref,
    sent_ref, count_ref, small_sem, coupling_sem, modes_sem, record_sem, result_sem,
):
    small = [
        pltpu.make_async_copy(source, target, small_sem.at[i])
        for i, (source, target) in enumerate(
            (
                (pairs_hbm, pairs_ref),
                (parent_hbm, parent_ref),
                (block_hbm, block_ref),
                (weights_hbm, weights_ref),
            )
        )
    ]
    for copy in small:
        copy.start()
    row, col = square_index()
    lower = row >= col
    diagonal = lax.broadcasted_iota(jnp.int32, (HALF, BLK), 1) == (
        lax.broadcasted_iota(jnp.int32, (HALF, BLK), 0) + HALF
    )
    slots = lax.broadcasted_iota(jnp.int32, (1, 128), 1)
    first = core_ref[0] == 0

    def copies(step):
        part = pl.ds(step * CB, CB)
        low, high = pl.ds(step * CB, CB // 2), pl.ds(step * CB + CB // 2, CB // 2)
        return (
            pltpu.make_async_copy(modes_hbm.at[low], modes_ref.at[low], modes_sem.at[2 * step]),
            pltpu.make_async_copy(modes_hbm.at[high], modes_ref.at[high], modes_sem.at[2 * step + 1]),
            pltpu.make_async_copy(coupling_hbm.at[part], coupling_ref.at[part], coupling_sem.at[step]),
        )

    def record_copy(step):
        part = pl.ds(step * CB, CB)
        return pltpu.make_async_copy(record_ref.at[part], record_hbm.at[part], record_sem.at[step])

    for step in range(STEPS):
        for copy in copies(step):
            copy.start()
    for p in range(NG * NZ):
        count_ref[p] = 0
    for copy in small:
        copy.wait()

    @pl.loop(0, STEPS)
    def _(step):
        for copy in copies(step):
            copy.wait()
        weights = weights_ref[pl.ds(pl.multiple_of(step * CB, CB), CB), :].astype(F32)
        for pair in range(CB // 2):
            records = []
            for j in (2 * pair, 2 * pair + 1):
                c = step * CB + j
                top = modes_ref[c, pl.ds(pl.multiple_of(pairs_ref[0, c] * BLK, BLK), BLK), :]
                bottom = modes_ref[c, pl.ds(pl.multiple_of(pairs_ref[1, c] * BLK, BLK), BLK), :]
                record = dot(coupling_ref[c], jnp.concatenate([top, bottom], axis=0))
                record = (record * weights[j : j + 1, :]).astype(BF)
                record_ref[c] = record
                records.append(record)
            both = jnp.concatenate(records, axis=0)
            products = dot_nt(both, both)
            for i in range(2):
                c = step * CB + 2 * pair + i
                s = products[i * BLK : (i + 1) * BLK, i * BLK : (i + 1) * BLK]
                cross = side_by_side(s[HALF:, :HALF])
                triangle = side_by_side(jnp.where(lower, s[:HALF, :HALF], s[HALF:, HALF:]))
                own_ref[pl.ds(c, 8, stride=CHILDREN_DEV), :] = jnp.where(first, cross, triangle)
                other_ref[pl.ds(c, 8, stride=CHILDREN_DEV), :] = jnp.where(first, triangle, cross)
                diag = jnp.sum(jnp.where(diagonal, s[HALF:], 0.0), axis=0, keepdims=True)
                zero = jnp.zeros((1, BLK), F32)
                named = zero + (block_ref[c] + 1).astype(F32)
                own_ref[pl.ds(8 * CHILDREN_DEV + c, 1), :] = jnp.concatenate([diag, named], axis=1)
                other_ref[pl.ds(8 * CHILDREN_DEV + c, 1), :] = jnp.concatenate([diag, zero], axis=1)
                p = parent_ref[c]
                k = count_ref[p]
                count_ref[p] = k + 1
                group = (p // (NZ * NX)) * NX + p % NX
                slot = group * SLOTS + ((p // NX) % NZ) * 2 + k
                for h in range(2):
                    hit = jnp.where(slots == slot - 128 * h, 1.0, 0.0)
                    own_ref[pl.ds((9 + h) * CHILDREN_DEV + c, 1), :] = hit
        record_copy(step).start()

    sent_ref[...] = other_ref[...].astype(BF)
    results = (
        pltpu.make_async_copy(sent_ref, other_hbm, result_sem.at[0]),
        pltpu.make_async_copy(own_ref, own_hbm, result_sem.at[1]),
    )
    for copy in results:
        copy.start()
    for step in range(STEPS):
        record_copy(step).wait()
    for copy in results:
        copy.wait()


def moments(core, pairs, parent, block, coupling, modes, weights):
    hbm = pl.BlockSpec(memory_space=pltpu.HBM)
    return pl.pallas_call(
        moments_kernel,
        in_specs=[SMEM, hbm, hbm, hbm, hbm, hbm, hbm],
        out_specs=[hbm, hbm, hbm],
        out_shape=[
            jax.ShapeDtypeStruct((CHILDREN_DEV, BLK, 128), BF),
            jax.ShapeDtypeStruct((11 * CHILDREN_DEV, 128), F32),
            jax.ShapeDtypeStruct((9 * CHILDREN_DEV, 128), BF),
        ],
        scratch_shapes=[
            pltpu.SMEM((2, CHILDREN_DEV), jnp.int32),
            pltpu.SMEM((CHILDREN_DEV,), jnp.int32),
            pltpu.SMEM((CHILDREN_DEV,), jnp.int32),
            pltpu.VMEM((CHILDREN_DEV, BLK, 128), BF),
            pltpu.VMEM((CHILDREN_DEV, 256, 128), BF),
            pltpu.VMEM((CHILDREN_DEV, 128), BF),
            pltpu.VMEM((CHILDREN_DEV, BLK, 128), BF),
            pltpu.VMEM((11 * CHILDREN_DEV, 128), F32),
            pltpu.VMEM((9 * CHILDREN_DEV, 128), F32),
            pltpu.VMEM((9 * CHILDREN_DEV, 128), BF),
            pltpu.SMEM((NG * NZ,), jnp.int32),
            pltpu.SemaphoreType.DMA((4,)),
            pltpu.SemaphoreType.DMA((STEPS,)),
            pltpu.SemaphoreType.DMA((2 * STEPS,)),
            pltpu.SemaphoreType.DMA((STEPS,)),
            pltpu.SemaphoreType.DMA((2,)),
        ],
        compiler_params=params(60),
        name="child_moments",
    )(core, pairs, parent, block, coupling, modes, weights)


def message_row(i, k):
    return k * 8 + i if i < 8 else 16 + k


def every_device(i, k):
    return pl.ds(message_row(i, k), PARENTS, stride=ROWS)


def stage_kernel(own_ref, sums_ref, place_ref, onehot_ref):
    sums_ref[...] = own_ref[: 9 * CHILDREN_DEV, :]
    onehot = jnp.concatenate(
        [own_ref[9 * CHILDREN_DEV : 10 * CHILDREN_DEV, :], own_ref[10 * CHILDREN_DEV :, :]], axis=1
    )
    place_ref[...] = onehot.T.astype(BF)
    onehot_ref[...] = onehot.astype(BF)


def stage(own):
    return pl.pallas_call(
        stage_kernel,
        in_specs=[VMEM],
        out_specs=[VMEM, VMEM, VMEM],
        out_shape=[
            jax.ShapeDtypeStruct((9 * CHILDREN_DEV, 128), F32),
            jax.ShapeDtypeStruct((NG * SLOTS, CHILDREN_DEV), BF),
            jax.ShapeDtypeStruct((CHILDREN_DEV, NG * SLOTS), BF),
        ],
        compiler_params=params(16),
        name="stage",
    )(own)


def dispatch_kernel(place_ref, own_ref, recv_ref, out_ref):
    place = place_ref[...]
    for i in range(9):
        rows = slice(i * CHILDREN_DEV, (i + 1) * CHILDREN_DEV)
        values = (own_ref[rows, :] + recv_ref[rows, :].astype(F32)).astype(BF)
        out_ref[:, i * SLOTS : (i + 1) * SLOTS, :] = dot(place, values).astype(BF).reshape(NG, SLOTS, 128)


def dispatch(place, own, recv):
    return pl.pallas_call(
        dispatch_kernel,
        in_specs=[VMEM, VMEM, VMEM],
        out_specs=VMEM,
        out_shape=jax.ShapeDtypeStruct((NG, ROWS, 128), BF),
        compiler_params=params(16),
        name="dispatch",
    )(place, own, recv)


def bin_kernel(recv_ref, out_ref, onehot_ref):
    count = NG * SLOTS
    meta = recv_ref[:, 8 * SLOTS : ROWS, :].astype(F32).reshape(count, 128)
    slot = lax.broadcasted_iota(jnp.int32, (count, 128), 0) % SLOTS
    lane = lax.broadcasted_iota(jnp.int32, (count, 128), 1)
    meta = pltpu.roll(meta, 64, 1)
    target = meta + (SB * (slot // 2) - 1).astype(F32)
    hit = (lane < 64) & (meta > 0.5) & (target == lane.astype(F32))
    onehot = jnp.where(hit, 1.0, 0.0).astype(BF)
    onehot_ref[...] = onehot
    values = jnp.concatenate(
        [recv_ref[:, i * SLOTS : (i + 1) * SLOTS, :].reshape(count, 128) for i in range(9)], axis=1
    )
    bins = dot_tn(onehot, values)
    zero = jnp.zeros((8, 128), F32)
    for z in range(NZ):
        rows = [bins[8 * z : 8 * z + 8, 128 * i : 128 * (i + 1)] for i in range(9)] + [zero]
        out_ref[z] = jnp.concatenate(rows, axis=0).astype(BF)


def bin_slots(recv):
    return pl.pallas_call(
        bin_kernel,
        in_specs=[VMEM],
        out_specs=[VMEM, VMEM],
        out_shape=[
            jax.ShapeDtypeStruct((NZ, ZROWS, 128), BF),
            jax.ShapeDtypeStruct((NG * SLOTS, 128), BF),
        ],
        compiler_params=params(16),
        name="bin_slots",
    )(recv)


def wide(x):
    return jnp.concatenate([x, x], axis=1)


def pivot_block(c, row, j):
    a00, a01, a11 = c[0][j : j + 1], c[1][j : j + 1], c[1][j + 1 : j + 2]
    a02, a12, a22 = c[2][j : j + 1], c[2][j + 1 : j + 2], c[2][j + 2 : j + 3]
    a03, a13, a23 = c[3][j : j + 1], c[3][j + 1 : j + 2], c[3][j + 2 : j + 3]
    a33 = c[3][j + 3 : j + 4]
    scale = 1.0 / (a00 * a11 - a01 * a01)
    p00, p01, p11 = a11 * scale, -a01 * scale, a00 * scale
    t00, t10 = p00 * a02 + p01 * a12, p01 * a02 + p11 * a12
    t01, t11 = p00 * a03 + p01 * a13, p01 * a03 + p11 * a13
    s00 = a22 - (a02 * t00 + a12 * t10)
    s01 = a23 - (a02 * t01 + a12 * t11)
    s11 = a33 - (a03 * t01 + a13 * t11)
    scale = 1.0 / (s00 * s11 - s01 * s01)
    inside = (row >= j) & (row < j + 4)
    m = [jnp.where(row == j + i, -1.0, jnp.where(inside, 0.0, c[i])) for i in range(4)]
    m[2] = m[2] - (m[0] * t00 + m[1] * t10)
    m[3] = m[3] - (m[0] * t01 + m[1] * t11)
    return (p00, p01, p11), (t00, t10, t01, t11), (s11 * scale, -s01 * scale, s00 * scale), m


def eliminate(rest, block, p, spread):
    (p00, p01, p11), (t00, t10, t01, t11), (q00, q01, q11), m = (
        [spread(v) for v in part] for part in block
    )
    y0, y1 = p00 * p[0] + p01 * p[1], p01 * p[0] + p11 * p[1]
    u2 = p[2] - (t00 * p[0] + t10 * p[1])
    u3 = p[3] - (t01 * p[0] + t11 * p[1])
    rest = rest - (m[0] * y0 + m[1] * y1)
    x2, x3 = q00 * u2 + q01 * u3, q01 * u2 + q11 * u3
    return (rest - m[2] * x2) - m[3] * x3


def invert(a_ref):
    lane = lax.broadcasted_iota(jnp.int32, (PB, MP), 1)
    row = lax.broadcasted_iota(jnp.int32, (PB, MP), 0)
    row_half = row[:, :128]
    lane_all = lax.broadcasted_iota(jnp.int32, (MP, MP), 1)
    line = lane[:1]
    for b in range(MP // PB):
        r = b * PB
        panel = a_ref[r : r + PB, :]
        for j8 in range(0, PB, 8):
            c = [jnp.broadcast_to(panel[:, r + j8 + i : r + j8 + i + 1], (PB, 128)) for i in range(8)]
            for h in (0, 4):
                j = j8 + h
                k = r + j
                block = pivot_block(c[h : h + 4], row_half, j)
                for m in range(h + 4, 8):
                    rest = jnp.where((row_half >= j) & (row_half < j + 4), 0.0, c[m])
                    c[m] = eliminate(rest, block, [c[m][j + i : j + i + 1] for i in range(4)], lambda v: v)
                inside = (line >= k) & (line < k + 4)
                p = [
                    jnp.where(line == k + i, 1.0, jnp.where(inside, 0.0, panel[j + i : j + i + 1]))
                    for i in range(4)
                ]
                cleared = ((lane >= k) & (lane < k + 4)) | ((row >= j) & (row < j + 4))
                panel = eliminate(jnp.where(cleared, 0.0, panel), block, p, wide)
        ch, cm, cl = split3(a_ref[:, r : r + PB])
        ph, pm, pw = split3(panel)
        update = dot(
            jnp.concatenate([ch, ch, cm, ch, cm, cl], axis=1),
            jnp.concatenate([ph, pm, ph, pw, pm, ph], axis=0),
        )
        a_ref[...] = jnp.where((lane_all // PB) == b, 0.0, a_ref[...]) - update
        a_ref[r : r + PB, :] = panel


def split3(x):
    high = x.astype(BF)
    rest = x - high.astype(F32)
    mid = rest.astype(BF)
    return high, mid, (rest - mid.astype(F32)).astype(BF)


def split(x):
    high = x.astype(BF)
    return high, (x - high.astype(F32)).astype(BF)


def pencil_kernel(
    core_ref, mine_ref, theirs_ref, q_ref, eigs_ref, out_ref, a_ref, y_ref, pack_ref, own_ref, other_ref
):
    for source, target in ((mine_ref, own_ref), (theirs_ref, other_ref)):
        parts = [source[z].astype(F32) for z in range(NZ)]
        while len(parts) > 1:
            parts = [x + y for x, y in zip(parts[::2], parts[1::2])]
        target[...] = parts[0]
    row, col = square_index()
    first = core_ref[0] == 0
    diags = jnp.where(first, other_ref[64:72, 32:64], own_ref[64:72, 32:64])
    for b in range(SB):
        own = own_ref[pl.ds(b, 8, stride=8), :]
        other = other_ref[pl.ds(b, 8, stride=8), :]
        cross = stacked(jnp.where(first, own, other))
        triangle = stacked(jnp.where(first, other, own))
        n11 = jnp.where(row > col, triangle, jnp.where(row == col, 0.5 * triangle, 0.0))
        n22 = jnp.where(row < col, triangle, jnp.where(row == col, 0.5 * diags[b : b + 1, :], 0.0))
        q1 = q_ref[b * BLK : b * BLK + HALF, :]
        q2 = q_ref[b * BLK + HALF : (b + 1) * BLK, :]
        y = dot(jnp.concatenate([n11, cross], axis=0).astype(BF), q1)
        bottom = y[HALF:] + dot(n22.astype(BF), q2)
        y_ref[b * BLK : (b + 1) * BLK, :] = jnp.concatenate([y[:HALF], bottom], axis=0).astype(BF)
    x = dot_tn(q_ref[...], y_ref[...])
    r = lax.broadcasted_iota(jnp.int32, (MP, MP), 0)
    c = lax.broadcasted_iota(jnp.int32, (MP, MP), 1)
    a_ref[...] = (x + x.T) * (1.0 / 16384.0) + jnp.where(r == c, eigs_ref[...], 0.0)
    invert(a_ref)
    high, low = split(a_ref[...] * (1.0 / MP))
    q = q_ref[...]
    y_high, y_low = split(dot(q, high) + dot(q, low))
    for b in range(SB):
        s = b * BLK
        qb = q_ref[s : s + BLK, :]
        h = dot_nt(qb, y_high[s : s + BLK]) + dot_nt(qb, y_low[s : s + BLK])
        h11, h22 = h[:HALF, :HALF], h[HALF:, HALF:]
        cross = side_by_side(2.0 * h[HALF:, :HALF])
        triangle = side_by_side(jnp.where(row > col, 2.0 * h11, jnp.where(row == col, h11, 2.0 * h22)))
        diag = jnp.sum(jnp.where(row == col, h22, 0.0), axis=0, keepdims=True)
        pack_ref[pl.ds(b, 8, stride=8), :] = jnp.where(first, cross, triangle)
        pack_ref[64 + b : 65 + b, :] = jnp.concatenate([diag, jnp.zeros((1, 96), F32)], axis=1)
    pack_ref[72:80, :] = jnp.zeros((8, 128), F32)
    result = pack_ref[...].astype(BF)
    for z in range(NZ):
        out_ref[z] = result


def pencil_blocks(core, own, other, q, eigs):
    return pl.pallas_call(
        pencil_kernel,
        in_specs=[SMEM, VMEM, VMEM, VMEM, VMEM],
        out_specs=VMEM,
        out_shape=jax.ShapeDtypeStruct((NZ, ZROWS, 128), BF),
        scratch_shapes=[
            pltpu.VMEM((MP, MP), F32),
            pltpu.VMEM((SB * BLK, MP), BF),
            pltpu.VMEM((ZROWS, 128), F32),
            pltpu.VMEM((ZROWS, 128), F32),
            pltpu.VMEM((ZROWS, 128), F32),
        ],
        compiler_params=params(16),
        name="pencil_blocks",
    )(core, own, other, q, eigs)


def select_kernel(bins_ref, onehot_ref, out_ref):
    onehot = onehot_ref[:, 0:64]
    bins = [bins_ref[z].astype(F32) for z in range(NZ)]
    for i in range(9):
        values = jnp.concatenate([x[8 * i : 8 * i + 8] for x in bins], axis=0).astype(BF)
        picked = dot(onehot, values).astype(BF)
        out_ref[:, i * SLOTS : (i + 1) * SLOTS, :] = picked.reshape(NG, SLOTS, 128)


def select_bins(bins, onehot):
    return pl.pallas_call(
        select_kernel,
        in_specs=[VMEM, VMEM],
        out_specs=VMEM,
        out_shape=jax.ShapeDtypeStruct((NG, ROWS, 128), BF),
        compiler_params=params(16),
        name="select_bins",
    )(bins, onehot)


def collect_kernel(onehot_ref, recv_ref, out_ref):
    onehot = onehot_ref[...]
    for i in range(9):
        values = recv_ref[:, i * SLOTS : (i + 1) * SLOTS, :].reshape(NG * SLOTS, 128)
        out_ref[i * CHILDREN_DEV : (i + 1) * CHILDREN_DEV, :] = dot(onehot, values).astype(BF)


def collect(onehot, recv):
    return pl.pallas_call(
        collect_kernel,
        in_specs=[VMEM, VMEM],
        out_specs=VMEM,
        out_shape=jax.ShapeDtypeStruct((9 * CHILDREN_DEV, 128), BF),
        compiler_params=params(16),
        name="collect",
    )(onehot, recv)


def strength_kernel(core_ref, mine_ref, theirs_ref, record_ref, out_ref, own_ref, other_ref):
    step = pl.program_id(0)

    @pl.when(step == 0)
    def _():
        own_ref[...] = mine_ref[...].astype(F32)
        other_ref[...] = theirs_ref[...].astype(F32)

    row, col = square_index()
    first = core_ref[0] == 0
    for j in range(CB):
        c = step * CB + j
        own = own_ref[pl.ds(c, 8, stride=CHILDREN_DEV), :]
        other = other_ref[pl.ds(c, 8, stride=CHILDREN_DEV), :]
        r = pl.ds(8 * CHILDREN_DEV + c, 1)
        diag = jnp.where(first, other_ref[r, :], own_ref[r, :])[:, :HALF]
        cross = stacked(jnp.where(first, own, other))
        triangle = stacked(jnp.where(first, other, own))
        m11 = jnp.where(row >= col, triangle, 0.0)
        m22 = jnp.where(row < col, triangle, jnp.where(row == col, diag, 0.0))
        record = record_ref[j]
        left = dot(jnp.concatenate([m11, cross], axis=0).astype(BF), record[:HALF])
        right = dot(m22.astype(BF), record[HALF:])
        wide_record = record.astype(F32)
        terms = left[:HALF] * wide_record[:HALF] + (left[HALF:] + right) * wide_record[HALF:]
        out_ref[j : j + 1, :] = jnp.sum(terms, axis=0, keepdims=True)


def strengths(core, own, other, record):
    whole = (9 * CHILDREN_DEV, 128)
    return pl.pallas_call(
        strength_kernel,
        grid=(STEPS,),
        in_specs=[
            SMEM,
            pl.BlockSpec(whole, lambda i: (0, 0)),
            pl.BlockSpec(whole, lambda i: (0, 0)),
            pl.BlockSpec((CB, BLK, 128), lambda i: (i, 0, 0)),
        ],
        out_specs=pl.BlockSpec((CB, 128), lambda i: (i, 0)),
        out_shape=jax.ShapeDtypeStruct((CHILDREN_DEV, 128), F32),
        scratch_shapes=[pltpu.VMEM(whole, F32), pltpu.VMEM(whole, F32)],
        compiler_params=params(16),
        name="strengths",
    )(core, own, other, record)


def swap(x):
    return lax.ppermute(x, "mode", [(0, 1), (1, 0)])


def exchange(x, axes):
    return lax.all_to_all(x, axes, split_axis=0, concat_axis=0, tiled=True)


def per_device(coupling, pairs, modes, weights, parent_of, row_block, parent_modes, parent_eigs):
    core = lax.axis_index("mode").astype(jnp.int32).reshape(1)
    parent = parent_of.reshape(CHILDREN_DEV)
    record, own, other = moments(core, pairs.T, parent, row_block, coupling, modes, weights)
    sums, place, onehot = stage(own)
    sent = dispatch(place, sums, swap(other))
    binned, chosen = bin_slots(exchange(sent, ("y", "x")))
    bins = exchange(binned, "z")
    blocks = pencil_blocks(core, bins, swap(bins), parent_modes[0], parent_eigs)
    picked = select_bins(exchange(blocks, "z"), chosen)
    mine = collect(onehot, exchange(picked, ("y", "x")))
    return strengths(core, mine, swap(mine), record)


def solution(mesh):
    grid = Mesh(mesh.devices.reshape(NY, NZ, NX, 2), ("y", "z", "x", "mode"))
    sub = ("y", "z", "x")
    in_specs = (
        P(sub, None, None),
        P(sub, None),
        P(sub, None, "mode"),
        P(sub, "mode"),
        P(sub, None),
        P(sub),
        P(sub, None, None),
        P(sub, None),
    )
    return jax.shard_map(
        per_device, mesh=grid, in_specs=in_specs, out_specs=P(sub, "mode"), check_vma=False
    )
```
